256 devices in a mesh: dp: 2 (over core), ctx: 128 (over x, y, z).
Axes of the slice: x: 4, y: 4, z: 8, core: 2. Of those that a mesh axis runs over, the one named last changes fastest.
Arguments:
- queries: bfloat16 [2, 65536, 1024], P('dp', 'ctx'), may hold values from -20 to 20
- key_rows: bfloat16 [2, 65536, 1024], P('dp', 'ctx'), may hold values from -14 to 14
- values: bfloat16 [2, 65536, 1024], P('dp', 'ctx'), may hold values from -90 to 90
- grad_out: bfloat16 [2, 65536, 1024], P('dp', 'ctx'), may hold values from -72 to 72
- level_bias: float32 [5, 16], replicated, may hold values from -1.5 to 0.5
Outputs:
- attended: bfloat16 [2, 65536, 1024], P('dp', 'ctx')
- grad_queries: bfloat16 [2, 65536, 1024], P('dp', 'ctx')
- grad_keys: bfloat16 [2, 65536, 1024], P('dp', 'ctx')
- grad_values: bfloat16 [2, 65536, 1024], P('dp', 'ctx')
- grad_bias: float32 [5, 16], replicated
The draws below stay inside these ranges and needn't reach their ends.
All inputs are finite; a program needn't handle non-finite values.
Results may differ from the reference program's by a relative error of at most 0.04.
Values may be sent and summed in bfloat16 or wider, within the bound.
No kernel may reach another device: no remote copies, remote signals or barrier semaphores. Data moves between devices by JAX's collectives and lax.ppermute only.
A program may use at most 256 MiB of HBM per device.

```python
import math
import jax
import jax.numpy as jnp
import numpy as np
from jax import lax

HEADS = 16
D = 1024
BLOCK = 128
LEVELS = 6
SEQ = 65536
GROUPS = 2


REGION = 16


def regional(key, weight):
    table = jax.random.truncated_normal(key, -4.0, 4.0, (GROUPS, SEQ // REGION, D), jnp.float32) * weight
    return jnp.repeat(table, REGION, axis=1)


def draw_queries(key, part):
    key = jax.random.fold_in(key, 1)
    base = jax.random.truncated_normal(key, -4.0, 4.0, (GROUPS, SEQ, D), jnp.float32)
    return base.astype(jnp.bfloat16)


def draw_key_rows(key, part):
    key = jax.random.fold_in(key, 2)
    base = jax.random.truncated_normal(key, -4.0, 4.0, (GROUPS, SEQ, D), jnp.float32)
    base = base + regional(jax.random.fold_in(key, 5), 0.7)
    return base.astype(jnp.bfloat16)


def draw_values(key, part):
    key = jax.random.fold_in(key, 3)
    base = jax.random.truncated_normal(key, -4.0, 4.0, (GROUPS, SEQ, D), jnp.float32)
    base = base + regional(jax.random.fold_in(key, 5), 2.5)
    return base.astype(jnp.bfloat16)


def draw_grad_out(key, part):
    key = jax.random.fold_in(key, 4)
    rising = 1.0 + 2.0 * jnp.arange(SEQ, dtype=jnp.float32)[None, :, None] / SEQ
    base = jax.random.truncated_normal(key, -4.0, 4.0, (GROUPS, SEQ, D), jnp.float32) * rising
    return base.astype(jnp.bfloat16)


def setup_inputs(seed: int = 0) -> dict:
    streams_of = jax.random.split(jax.random.key(seed), 6)
    return {
        "queries": draw_queries(jax.random.fold_in(streams_of[5], 71), 0),
        "key_rows": draw_key_rows(jax.random.fold_in(streams_of[5], 71), 0),
        "values": draw_values(jax.random.fold_in(streams_of[5], 71), 0),
        "grad_out": draw_grad_out(jax.random.fold_in(streams_of[5], 71), 0),
        "level_bias": jnp.clip(jax.random.uniform(streams_of[4], (LEVELS - 1, HEADS), jnp.float32, -1.5, 0.5), -1.5, 0.5),
    }


PRECISE = lax.Precision.HIGHEST
NEGATIVE = -1e+30

def coarsen(row_data):
    paired = row_data.reshape(row_data.shape[0] // 2, 2, row_data.shape[1]).astype(jnp.float32)
    return ((paired[:, 0] + paired[:, 1]) * 0.5).astype(jnp.bfloat16)

def spread(row_data, factor):
    dims = row_data.shape
    widened = jnp.broadcast_to(row_data[:, None], (dims[0], factor) + dims[1:])
    return widened.reshape((dims[0] * factor,) + dims[1:])

def to_bf16(data):
    return lax.optimization_barrier(data.astype(jnp.bfloat16)).astype(jnp.float32)

def level_mask(is_first, block_ids, query_rows, block_total):
    half_rows = BLOCK // 2
    if is_first:
        key_pos = jnp.arange(3 * BLOCK, dtype=jnp.int32)
        side_of = key_pos // BLOCK
        other_block = block_ids[:, None] + side_of[None, :] - 1
        exists = (other_block >= 0) & (other_block < block_total)
        return jnp.broadcast_to(exists[:, None, :], (block_ids.shape[0], query_rows.shape[0], 3 * BLOCK))
    key_pos = jnp.arange(2 * BLOCK, dtype=jnp.int32)
    side_of = key_pos // BLOCK
    key_half = key_pos % BLOCK // half_rows
    other_block = block_ids[:, None] + 2 * side_of[None, :] - 1
    exists = (other_block >= 0) & (other_block < block_total)
    query_half = query_rows // half_rows
    left_ok = (query_half[:, None] == 1) | (key_half[None, :] == 0)
    right_ok = (query_half[:, None] == 0) | (key_half[None, :] == 1)
    pattern = jnp.where(side_of[None, :] == 0, left_ok, right_ok)
    return exists[:, None, :] & pattern[None, :, :]

def windows_of(extended, per_step, is_first):
    if is_first:
        return jnp.concatenate([extended[:per_step], extended[1:per_step + 1], extended[2:per_step + 2]], axis=1)
    return jnp.concatenate([extended[:per_step], extended[2:per_step + 2]], axis=1)

def fold_window(window_grad, per_step, is_first):
    pieces = window_grad.reshape(per_step, -1, BLOCK, window_grad.shape[-1])
    folded = jnp.pad(pieces[:, 0], ((0, 2), (0, 0), (0, 0)))
    if is_first:
        folded = folded + jnp.pad(pieces[:, 1], ((1, 1), (0, 0), (0, 0)))
        folded = folded + jnp.pad(pieces[:, 2], ((2, 0), (0, 0), (0, 0)))
    else:
        folded = folded + jnp.pad(pieces[:, 1], ((2, 0), (0, 0), (0, 0)))
    return folded

def split_heads(data, head_count):
    return data.reshape(data.shape[0], data.shape[1], head_count, data.shape[2] // head_count)

def scores_of(queries, window, offset):
    head_count = offset.shape[0]
    model_width = queries.shape[2]
    scaling = (model_width // head_count) ** (-0.5)
    query_heads = split_heads(queries.astype(jnp.float32), head_count)
    key_heads = split_heads(window[:, :, :model_width].astype(jnp.float32), head_count)
    value_heads = split_heads(window[:, :, model_width:].astype(jnp.float32), head_count)
    scores = jnp.einsum('nrhe,nshe->nhrs', query_heads, key_heads, precision=PRECISE) * scaling
    scores = scores + offset[None, :, None, None]
    return (scores, query_heads, key_heads, value_heads, scaling)

def attend(queries, window, allowed, offset):
    scores, query_heads, key_heads, value_heads, scaling = scores_of(queries, window, offset)
    is_live = allowed[:, None, :, :]
    row_max = lax.optimization_barrier(jnp.max(jnp.where(is_live, scores, NEGATIVE), axis=-1))
    weights = jnp.exp(jnp.where(is_live, scores - row_max[..., None], NEGATIVE))
    row_sum = lax.optimization_barrier(jnp.sum(weights, axis=-1))
    blended = jnp.einsum('nhrs,nshe->nrhe', to_bf16(weights), value_heads, precision=PRECISE)
    return (jnp.swapaxes(row_max, 1, 2), jnp.swapaxes(row_sum, 1, 2), blended)

def attend_back(queries, window, allowed, offset, row_max, grad_rows, correction):
    scores, query_heads, key_heads, value_heads, scaling = scores_of(queries, window, offset)
    is_live = allowed[:, None, :, :]
    weights = jnp.exp(jnp.where(is_live, scores - jnp.swapaxes(row_max, 1, 2)[..., None], NEGATIVE))
    grad_heads = grad_rows.astype(jnp.float32)
    value_dots = jnp.einsum('nrhe,nshe->nhrs', grad_heads, value_heads, precision=PRECISE)
    grad_scores = weights * (value_dots - jnp.swapaxes(correction, 1, 2)[..., None])
    scaled = to_bf16(grad_scores * scaling)
    blocks_here = queries.shape[0]
    model_width = queries.shape[2]
    query_grad = jnp.einsum('nhrs,nshe->nrhe', scaled, key_heads, precision=PRECISE).reshape(blocks_here, -1, model_width)
    key_grad = jnp.einsum('nhrs,nrhe->nshe', scaled, query_heads, precision=PRECISE).reshape(blocks_here, -1, model_width)
    value_grad = jnp.einsum('nhrs,nrhe->nshe', to_bf16(weights), grad_heads, precision=PRECISE).reshape(blocks_here, -1, model_width)
    return (query_grad, jnp.concatenate([key_grad, value_grad], axis=-1), lax.optimization_barrier(jnp.sum(grad_scores, axis=(0, 2, 3))))

def combine(row_maxes, row_sums, blends):
    peak_all = row_maxes[0]
    for height in range(1, len(row_maxes)):
        peak_all = jnp.maximum(peak_all, spread(row_maxes[height], 2 ** height))
    denominator = jnp.zeros(peak_all.shape, jnp.float32)
    numerator = jnp.zeros(blends[0].shape, jnp.float32)
    for height in range(len(row_maxes)):
        factor = jnp.exp(spread(row_maxes[height], 2 ** height) - peak_all)
        denominator = denominator + factor * spread(row_sums[height], 2 ** height)
        numerator = numerator + factor[..., None] * spread(blends[height], 2 ** height)
    attended = (numerator / denominator[..., None]).reshape(peak_all.shape[0], -1).astype(jnp.bfloat16)
    return (attended, peak_all + jnp.log(denominator))

def grad_parts(grad_out, attended, row_maxes, log_total, head_count):
    row_count = grad_out.shape[0]
    grad_heads = grad_out.astype(jnp.float32).reshape(row_count, head_count, -1)
    inner_dot = lax.optimization_barrier(jnp.sum(grad_heads * attended.astype(jnp.float32).reshape(row_count, head_count, -1), axis=-1))
    packs = []
    for height in range(len(row_maxes)):
        group_size = 2 ** height
        factor = jnp.exp(spread(row_maxes[height], group_size) - log_total)
        grad_rows = (grad_heads * factor[..., None]).reshape(row_count // group_size, group_size, head_count, -1)
        grad_rows = grad_rows.sum(axis=1).astype(jnp.bfloat16)
        correction = (factor * inner_dot).reshape(row_count // group_size, group_size, head_count).sum(axis=1)
        packs.append((grad_rows, correction))
    return packs

def level_layout(pair_rows):
    blocks = pair_rows.shape[0] // BLOCK
    per_step = min(blocks, 8)
    return (blocks, per_step, blocks // per_step)

def forward_level(height, coarse_queries, pair_rows, offset):
    blocks, per_step, step_count = level_layout(pair_rows)
    extended_all = jnp.pad(pair_rows.reshape(blocks, BLOCK, -1), ((1, 1), (0, 0), (0, 0)))
    query_blocks = coarse_queries.reshape(step_count, per_step, BLOCK, -1)
    rows_in_block = jnp.arange(BLOCK, dtype=jnp.int32)

    def one_step(packed):
        step_no, query_part = packed
        first_block = step_no * per_step
        extended = lax.dynamic_slice_in_dim(extended_all, first_block, per_step + 2, 0)
        block_ids = first_block + jnp.arange(per_step, dtype=jnp.int32)
        allowed = level_mask(height == 0, block_ids, rows_in_block, blocks)
        return attend(query_part, windows_of(extended, per_step, height == 0), allowed, offset)
    row_max, row_sum, blended = lax.map(one_step, (jnp.arange(step_count, dtype=jnp.int32), query_blocks))
    row_count = blocks * BLOCK
    return (row_max.reshape(row_count, -1), row_sum.reshape(row_count, -1), blended.reshape(row_count, blended.shape[-2], blended.shape[-1]))

def backward_level(height, coarse_queries, pair_rows, offset, row_max, grad_rows, correction):
    blocks, per_step, step_count = level_layout(pair_rows)
    feature = pair_rows.shape[1]
    extended_all = jnp.pad(pair_rows.reshape(blocks, BLOCK, -1), ((1, 1), (0, 0), (0, 0)))
    query_blocks = coarse_queries.reshape(step_count, per_step, BLOCK, -1)
    max_blocks = row_max.reshape(step_count, per_step, BLOCK, -1)
    grad_blocks = grad_rows.reshape(step_count, per_step, BLOCK, grad_rows.shape[-2], grad_rows.shape[-1])
    corr_blocks = correction.reshape(step_count, per_step, BLOCK, -1)
    rows_in_block = jnp.arange(BLOCK, dtype=jnp.int32)

    def one_step(packed):
        step_no, query_part, max_part, grad_part, corr_part = packed
        first_block = step_no * per_step
        extended = lax.dynamic_slice_in_dim(extended_all, first_block, per_step + 2, 0)
        block_ids = first_block + jnp.arange(per_step, dtype=jnp.int32)
        allowed = level_mask(height == 0, block_ids, rows_in_block, blocks)
        query_grad, window_grad, bias_part = attend_back(query_part, windows_of(extended, per_step, height == 0), allowed, offset, max_part, grad_part, corr_part)
        return (query_grad, fold_window(window_grad, per_step, height == 0), bias_part)
    query_grad, folded, bias_parts = lax.map(one_step, (jnp.arange(step_count, dtype=jnp.int32), query_blocks, max_blocks, grad_blocks, corr_blocks))
    interior = folded[:, 1:per_step + 1].reshape(blocks, BLOCK, feature)
    starts = np.arange(step_count) * per_step
    if step_count > 1:
        interior = interior.at[jnp.asarray(starts[1:] - 1, dtype=jnp.int32)].add(folded[1:, 0])
        interior = interior.at[jnp.asarray(starts[:-1] + per_step, dtype=jnp.int32)].add(folded[:-1, per_step + 1])
    return (query_grad.reshape(blocks * BLOCK, -1), interior.reshape(blocks * BLOCK, feature), lax.optimization_barrier(jnp.sum(bias_parts, axis=0)))

def one_group(queries, key_rows, values, grad_out, level_bias):
    head_count = level_bias.shape[1]
    model_width = queries.shape[1]
    row_count = queries.shape[0]
    coarse_q = [queries]
    coarse_kv = [jnp.concatenate([key_rows, values], axis=1)]
    for height in range(1, LEVELS):
        coarse_q.append(coarsen(coarse_q[-1]))
        coarse_kv.append(coarsen(coarse_kv[-1]))
    offsets = [jnp.zeros((head_count,), jnp.float32)] + [level_bias[height] + (height + 1) * math.log(2.0) for height in range(LEVELS - 1)]
    outputs = [forward_level(height, coarse_q[height], coarse_kv[height], offsets[height]) for height in range(LEVELS)]
    attended, log_total = combine([item[0] for item in outputs], [item[1] for item in outputs], [item[2] for item in outputs])
    packs = grad_parts(grad_out, attended, [item[0] for item in outputs], log_total, head_count)
    grad_q = jnp.zeros((row_count, model_width), jnp.float32)
    grad_kv = jnp.zeros((row_count, 2 * model_width), jnp.float32)
    bias_terms = []
    for height in range(LEVELS):
        group_size = 2 ** height
        query_grad, pair_grad, bias_part = backward_level(height, coarse_q[height], coarse_kv[height], offsets[height], outputs[height][0], packs[height][0], packs[height][1])
        grad_q = grad_q + spread(query_grad, group_size) / group_size
        grad_kv = grad_kv + spread(pair_grad, group_size) / group_size
        if height > 0:
            bias_terms.append(bias_part)
    return (attended, grad_q.astype(jnp.bfloat16), grad_kv[:, :model_width].astype(jnp.bfloat16), grad_kv[:, model_width:].astype(jnp.bfloat16), jnp.stack(bias_terms))

def reference(queries, key_rows, values, grad_out, level_bias):
    results = [one_group(queries[member], key_rows[member], values[member], grad_out[member], level_bias) for member in range(GROUPS)]
    stacked = [jnp.stack([result[slot] for result in results]) for slot in range(4)]
    bias_total = results[0][4]
    for member in range(1, GROUPS):
        bias_total = bias_total + results[member][4]
    grad_bias = bias_total * (1.0 / math.sqrt(SEQ * GROUPS))
    return (stacked[0], stacked[1], stacked[2], stacked[3], grad_bias)
```

```python
import math

import jax
import jax.numpy as jnp
from jax import lax
from jax.experimental import pallas as pl
from jax.experimental.pallas import tpu as pltpu
from jax.sharding import PartitionSpec as P

BLOCK = 128
HALF = 64
LEVELS = 6
PAIR = 128
NEGATIVE = -1e30
LN2 = math.log(2.0)
F32 = jnp.float32
BF16 = jnp.bfloat16
MIB = 1 << 20
RING = 8
SHARE = 80
SUB = 2


def dot_nn(a, b):
    return lax.dot_general(a, b, (((1,), (0,)), ((), ())), preferred_element_type=F32)


def dot_nt(a, b):
    return lax.dot_general(a, b, (((1,), (1,)), ((), ())), preferred_element_type=F32)


def iota(shape, dim):
    return lax.broadcasted_iota(jnp.int32, shape, dim)


def halving(n):
    return jnp.where(iota((n // 2, n), 1) // 2 == iota((n // 2, n), 0), 0.5, 0.0).astype(BF16)


def doubling(n, factor):
    return (iota((n * factor, n), 0) // factor == iota((n * factor, n), 1)).astype(BF16)


def coarsen(x):
    rows = x.shape[0]
    step = min(rows, BLOCK)
    mean = halving(step)
    parts = [dot_nn(mean, x[i : i + step]).astype(BF16) for i in range(0, rows, step)]
    return parts[0] if len(parts) == 1 else jnp.concatenate(parts, axis=0)


def uncoarsen(x):
    rows = x.shape[0]
    step = min(rows, HALF)
    up = doubling(step, 2)
    half = (x * 0.5).astype(BF16)
    parts = [dot_nn(up, half[i : i + step]) for i in range(0, rows, step)]
    return parts[0] if len(parts) == 1 else jnp.concatenate(parts, axis=0)


def two_heads(x):
    low = iota(x.shape, 1) < HALF
    zero = jnp.zeros_like(x)
    return jnp.concatenate([jnp.where(low, x, zero), jnp.where(low, zero, x)], axis=0)


def own_head(x, span):
    same = (iota(x.shape, 0) < HALF) == (iota(x.shape, 1) // span % 2 == 0)
    return jnp.where(same, x, 0.0)


def spreader(level):
    rows = 512 >> level
    span = min(rows, HALF)
    shape = (2 * rows, 512)
    c = iota(shape, 0)
    row = c // (2 * span) * span + c % span
    return (iota(shape, 1) // 2**level == row).astype(BF16)


def split3(x):
    high = x.astype(BF16).astype(F32)
    rest = x - high
    mid = rest.astype(BF16).astype(F32)
    return high, mid, rest - mid


def stacked(rows, height):
    shape = (height, rows[0].shape[1])
    which = iota(shape, 0)
    out = jnp.zeros(shape, F32)
    for i, row in enumerate(rows):
        out = jnp.where(which == i, row, out)
    return out


def by_head(top, bottom, x):
    return jnp.concatenate([x[:HALF] * top, x[HALF:] * bottom], axis=0)


def spread_stats(rows, span, spread):
    flat = []
    for row in rows:
        first = iota(row.shape, 1) // span % 2 == 0
        for part in split3(row):
            flat.append(jnp.where(first, part, 0.0))
        for part in split3(row):
            flat.append(jnp.where(first, 0.0, part))
    wide = dot_nn(stacked(flat, 16).astype(BF16), spread)
    out = []
    for i in range(2 * len(rows)):
        out.append(wide[3 * i : 3 * i + 1] + wide[3 * i + 1 : 3 * i + 2] + wide[3 * i + 2 : 3 * i + 3])
    return out


def offset_row(low, high, span, shape):
    return jnp.where(iota(shape, 1) // span % 2 == 0, low, high)


def softmax_of(scores):
    top = jnp.max(scores, axis=0, keepdims=True)
    weights = jnp.exp(scores - top)
    return top, weights, jnp.sum(weights, axis=0, keepdims=True)


def with_bias(scores, biases):
    parts = []
    at = 0
    for lo, hi, bias in biases:
        if lo > at:
            parts.append(scores[at:lo])
        parts.append(scores[lo:hi] + bias)
        at = hi
    if at < scores.shape[0]:
        parts.append(scores[at:])
    return jnp.concatenate(parts, axis=0)


def halo_coarse(left, right):
    left1, right1 = coarsen(left[:128]), coarsen(right[:128])
    left2 = coarsen(jnp.concatenate([left[128:192], left1], axis=0))
    right2 = coarsen(jnp.concatenate([right1, right[128:192]], axis=0))
    return jnp.concatenate([left1, right1, left2, right2], axis=0)


def near_keys(own, coarse, left, right, halo):
    def joined(*parts):
        return jnp.concatenate(parts, axis=0)

    return (
        joined(left[:128], own, right[:128]),
        joined(left[128:192], halo[:64], coarse[:256], halo[64:128], right[128:192]),
        joined(left[192:256], halo[128:192], coarse[256:384], halo[192:256], right[192:256]),
    )


def window_parts(j):
    if j % 2 == 0:
        return (j, j + 4, j + 5)
    return (j - 1, j, j + 4)


def window_spans(j):
    a, b, c = window_parts(j)
    if b == a + 1:
        return [(a * HALF, (b + 1) * HALF), (c * HALF, (c + 1) * HALF)]
    return [(a * HALF, (a + 1) * HALF), (b * HALF, (c + 1) * HALF)]


def window_biases(j, halves, left_bias, right_bias):
    out = []
    for i, part in enumerate(window_parts(j)):
        if part < 2:
            out.append((i * HALF, (i + 1) * HALF, left_bias))
        elif part >= halves + 2:
            out.append((i * HALF, (i + 1) * HALF, right_bias))
    return out


def third_biases(edge_ref):
    return [(i * HALF, (i + 1) * HALF, edge_ref[2 + i]) for i in range(3)]


def rows_of(ref, spans):
    if len(spans) == 1:
        return ref[spans[0][0] : spans[0][1], :]
    return jnp.concatenate([ref[lo:hi, :] for lo, hi in spans], axis=0)


def block_biases(b, left_bias, right_bias):
    if b == 0:
        return [(0, 128, left_bias)]
    if b == 3:
        return [(256, 384, right_bias)]
    return []


def prep_kernel(k_ref, v_ref, right_ref, left_ref, l3_ref, l4_ref, coarse_ref):
    for i, ref in enumerate((k_ref, v_ref)):
        zero = ref[0]
        one = coarsen(zero)
        two = coarsen(one)
        three = coarsen(two)
        right_ref[i, 0:128, :] = zero[384:512]
        right_ref[i, 128:192, :] = one[128:192]
        right_ref[i, 192:256, :] = two[0:64]
        left_ref[i, 0:128, :] = zero[0:128]
        left_ref[i, 128:192, :] = one[64:128]
        left_ref[i, 192:256, :] = two[64:128]
        l3_ref[i] = three
        l4_ref[i] = coarsen(three)
        coarse_ref[i, 0:256, :] = one
        coarse_ref[i, 256:384, :] = two


def query_kernel(q_ref, out_ref):
    rows = q_ref[0] * jnp.asarray(0.125, BF16)
    at = 0
    for level in range(1, LEVELS):
        rows = coarsen(rows)
        out_ref[at : at + (512 >> level), :] = rows
        at += 512 >> level


def share_kernel(flag_ref, own_ref, next_ref, prev_ref, out_ref):
    first = flag_ref[0] > 0
    for i in range(2):
        after, before = next_ref[i], prev_ref[i]
        out_ref[i, 0:32, :] = own_ref[i]
        out_ref[i, 32:64, :] = jnp.where(first, after, before)
        out_ref[i, 64:80, :] = coarsen(jnp.where(first, before, after))


def unshare_kernel(flag_ref, sum_ref, next_ref, prev_ref):
    first = flag_ref[0] > 0
    for i in range(2):
        four = sum_ref[i, 32:64, :]
        five = uncoarsen(sum_ref[i, 64:80, :].astype(F32)).astype(BF16)
        next_ref[i] = jnp.where(first, four, five)
        prev_ref[i] = jnp.where(first, five, four)


def near_forward_kernel(
    off_ref, edge_ref, q_ref, qc_ref, k_ref, v_ref, kvc_ref, nl_ref, nr_ref, f1_ref, f2_ref, f3_ref,
    st_ref, nt_ref, halo_ref, e1, e2, e3, *scratch,
):
    step = pl.program_id(0)

    @pl.when(step == 0)
    def _():
        e1[...] = spreader(1)
        e2[...] = spreader(2)
        e3[...] = spreader(3)

    interleaved(
        near_forward_pair(
            step * SUB + s, off_ref, edge_ref, *[lane_view(r, s) for r in (q_ref, qc_ref, k_ref, v_ref, kvc_ref, nl_ref, nr_ref)],
            [lane_view(r, s) for r in (f1_ref, f2_ref, f3_ref)],
            st_ref.at[s : s + 1], nt_ref.at[s : s + 1], lane_view(halo_ref, s), e1, e2, e3, *[r.at[s] for r in scratch],
        )
        for s in range(SUB)
    )


def near_forward_pair(
    pair, off_ref, edge_ref, q_ref, qc_ref, k_ref, v_ref, kvc_ref, nl_ref, nr_ref, pieces, st_ref, nt_ref, halo_ref,
    e1, e2, e3, k0s, k1s, k2s, vt0, vt1, vt2,
):
    left_bias, right_bias = edge_ref[0], edge_ref[1]
    q0 = q_ref[0] * jnp.asarray(0.125, BF16)
    q1, q2, q3 = qc_ref[0:256], qc_ref[256:384], qc_ref[384:448]
    halos = [halo_coarse(nl_ref[i], nr_ref[i]) for i in range(2)]
    for i in range(2):
        halo_ref[i] = halos[i]
    for dst, x in zip((k0s, k1s, k2s), near_keys(k_ref[0], kvc_ref[0], nl_ref[0], nr_ref[0], halos[0])):
        dst[...] = x
    for dst, x in zip((vt0, vt1, vt2), near_keys(v_ref[0], kvc_ref[1], nl_ref[1], nr_ref[1], halos[1])):
        dst[...] = x.T
    yield

    tops, totals, mixes = [], [], []
    for b in range(4):
        keys = k0s[b * 128 : b * 128 + 384, :]
        scores = dot_nt(keys, two_heads(q0[b * 128 : b * 128 + 128]))
        scores = with_bias(scores, block_biases(b, left_bias, right_bias))
        top, weights, total = softmax_of(scores)
        mixed = dot_nn(vt0[:, b * 128 : b * 128 + 384], weights.astype(BF16))
        tops.append(top)
        totals.append(total)
        mixes.append(jnp.concatenate([mixed[:HALF, :128], mixed[HALF:, 128:]], axis=0))
        yield
    top_a = jnp.concatenate([t[:, :128] for t in tops], axis=1)
    top_b = jnp.concatenate([t[:, 128:] for t in tops], axis=1)
    total_a = jnp.concatenate([t[:, :128] for t in totals], axis=1)
    total_b = jnp.concatenate([t[:, 128:] for t in totals], axis=1)
    st_ref[0, 0:1, :] = top_a
    st_ref[0, 1:2, :] = top_b
    mixed0 = jnp.concatenate(mixes, axis=1)

    coarse = []
    third = [jnp.concatenate([r[i] for r in pieces], axis=0) for i in range(2)]
    for level, keys_ref, vt_ref, queries, spread in (
        (3, third[0], third[1].T, q3, e3), (1, k1s, vt1, q1, e1), (2, k2s, vt2, q2, e2),
    ):
        halves = 8 >> level
        tops, totals, mixes = [], [], []
        for j in range(halves):
            spans = window_spans(j) if level < 3 else [(0, 192)]
            scores = dot_nt(rows_of(keys_ref, spans), two_heads(queries[j * HALF : (j + 1) * HALF]))
            scores = with_bias(
                scores, window_biases(j, halves, left_bias, right_bias) if level < 3 else third_biases(edge_ref)
            )
            top, weights, total = softmax_of(scores)
            vt = vt_ref if level == 3 else jnp.concatenate([vt_ref[:, lo:hi] for lo, hi in spans], axis=1)
            mixes.append(own_head(dot_nn(vt, weights.astype(BF16)), HALF).astype(BF16))
            tops.append(top)
            totals.append(total)
            yield
        top = jnp.concatenate(tops, axis=1)
        total = jnp.concatenate(totals, axis=1)
        st_ref[0, 1 + level : 2 + level, 0 : top.shape[1]] = top
        low = off_ref[level - 1, 2 * pair] + level * LN2
        high = off_ref[level - 1, 2 * pair + 1] + level * LN2
        top = top + offset_row(low, high, HALF, top.shape)
        wide = spread_stats([top, total], HALF, spread[...])
        mixed = dot_nn(jnp.concatenate(mixes, axis=1), spread[...])
        st_ref[0, 7 + 2 * level : 8 + 2 * level, :] = wide[0]
        st_ref[0, 8 + 2 * level : 9 + 2 * level, :] = wide[1]
        coarse.append((wide, mixed))
        yield

    peaks, denoms, factors = [], [], []
    for h, (top0, total0) in enumerate(((top_a, total_a), (top_b, total_b))):
        peak = top0
        for wide, _ in coarse:
            peak = jnp.maximum(peak, wide[h])
        f = [jnp.exp(top0 - peak)] + [jnp.exp(wide[h] - peak) for wide, _ in coarse]
        denom = f[0] * total0
        for i, (wide, _) in enumerate(coarse):
            denom = denom + f[i + 1] * wide[2 + h]
        peaks.append(peak)
        denoms.append(denom)
        factors.append(f)
    numer = by_head(factors[0][0], factors[1][0], mixed0)
    for i, (_, mixed) in enumerate(coarse):
        numer = numer + by_head(factors[0][i + 1], factors[1][i + 1], mixed)
    st_ref[0, 5:6, :] = peaks[0]
    st_ref[0, 6:7, :] = peaks[1]
    st_ref[0, 7:8, :] = denoms[0]
    st_ref[0, 8:9, :] = denoms[1]
    nt_ref[0] = numer


def far_kernel(
    off_ref, far_ref, flag_ref, qc_ref, g_ref, st_ref, nt_ref, ring_ref,
    att_ref, st2_ref, dq_ref, dring_ref, bias_ref, e4, e5,
):
    step = pl.program_id(0)

    @pl.when(step == 0)
    def _():
        e4[...] = spreader(4)
        e5[...] = spreader(5)

    interleaved(
        far_pair(
            step * SUB + s, off_ref, far_ref, flag_ref[0] > 0, lane_view(qc_ref, s), lane_view(g_ref, s),
            *[r.at[s : s + 1] for r in (st_ref, nt_ref)], lane_view(ring_ref, s),
            lane_view(att_ref, s), *[r.at[s : s + 1] for r in (st2_ref, dq_ref)],
            lane_view(dring_ref, s), bias_ref.at[s : s + 1], e4, e5,
        )
        for s in range(SUB)
    )


def ring_rows(rows, lo, hi, devices):
    return jnp.concatenate([rows[SHARE * z + lo : SHARE * z + hi] for z in devices], axis=0)


def far_pair(
    pair, off_ref, far_ref, first, qc_ref, g_ref, st_ref, nt_ref, ring_ref,
    att_ref, st2_ref, dq_ref, dring_ref, bias_ref, e4, e5,
):
    lower, upper = range(RING // 2), range(RING // 2, RING)
    q45 = {4: qc_ref[448:480], 5: qc_ref[480:496]}
    gt = g_ref[0].T.astype(F32)
    windows = {4: [], 5: []}
    for i in range(2):
        rows = ring_ref[i]
        own = jnp.where(first, ring_rows(rows, 0, 32, upper), ring_rows(rows, 0, 32, lower))
        foreign = [ring_rows(rows, 32, 64, lower), ring_rows(rows, 32, 64, upper)]
        near, far = jnp.where(first, foreign[1], foreign[0]), jnp.where(first, foreign[0], foreign[1])
        windows[4].append(jnp.concatenate([own, near], axis=0))
        windows[5].append(jnp.concatenate([ring_rows(rows, 64, 80, range(RING)), coarsen(far)], axis=0))
    levels = []
    for level, spread in ((4, e4), (5, e5)):
        span = 512 >> level
        queries = two_heads(q45[level])
        keys, values = windows[level]
        scores = dot_nt(keys, queries)
        parts = keys.shape[0] // HALF
        biases = [(i * HALF, (i + 1) * HALF, far_ref[level - 4, i]) for i in range(parts)]
        top, weights, total = softmax_of(with_bias(scores, biases))
        mixed = own_head(dot_nn(values.T, weights.astype(BF16)), span).astype(BF16)
        low = off_ref[level - 1, 2 * pair] + level * LN2
        high = off_ref[level - 1, 2 * pair + 1] + level * LN2
        top = top + offset_row(low, high, span, top.shape)
        wide = spread_stats([top, total], span, spread[...])
        levels.append((level, span, queries, weights, wide, dot_nn(mixed, spread[...]), spread))
        yield

    logs, inners, numers = [], [], []
    for h in range(2):
        peak0, denom0 = st_ref[0, 5 + h : 6 + h, :], st_ref[0, 7 + h : 8 + h, :]
        peak = peak0
        for item in levels:
            peak = jnp.maximum(peak, item[4][h])
        keep = jnp.exp(peak0 - peak)
        denom = keep * denom0
        numer = keep * nt_ref[0, h * HALF : (h + 1) * HALF, :]
        for item in levels:
            f = jnp.exp(item[4][h] - peak)
            denom = denom + f * item[4][2 + h]
            numer = numer + f * item[5][h * HALF : (h + 1) * HALF]
        out = (numer / denom).astype(BF16)
        numers.append(out)
        logs.append(peak + jnp.log(denom))
        inners.append(
            jnp.sum(gt[h * HALF : (h + 1) * HALF] * out.astype(F32), axis=0, keepdims=True)
        )
    att_ref[0] = jnp.concatenate(numers, axis=0).T
    st2_ref[0] = stacked([logs[0], logs[1], inners[0], inners[1]], 8)
    yield

    dqt = jnp.zeros((PAIR, 512), F32)
    sums = jnp.zeros((8, 128), F32)
    grads = {}
    for level, span, queries, weights, wide, _, spread in levels:
        dq, bias, dk, dv = level_back(
            weights, *windows[level], queries, gt, wide[:2], logs, inners, span, spread
        )
        grads[level] = (dk.astype(BF16), dv.astype(BF16))
        grads5 = (dk[128:192], dv[128:192])
        dqt = dqt + dq * (0.125 / 2**level)
        sums = place(sums, level, bias, span)
        yield
    for i in range(2):
        four, five = grads[4][i], grads[5][i]
        blank = jnp.zeros((128, PAIR), BF16)
        far = uncoarsen(grads5[i]).astype(BF16)
        for part, on_low in ((lower, True), (upper, False)):
            here = jnp.logical_not(first) if on_low else first
            own = jnp.where(here, four[0:128], blank)
            foreign = jnp.where(here, four[128:256], far)
            for n, z in enumerate(part):
                at = SHARE * z
                dring_ref[i, at : at + 32, :] = own[32 * n : 32 * n + 32]
                dring_ref[i, at + 32 : at + 64, :] = foreign[32 * n : 32 * n + 32]
                dring_ref[i, at + 64 : at + 80, :] = five[16 * z : 16 * z + 16]
    dq_ref[0] = dqt
    bias_ref[0] = sums


def place(sums, level, bias, span):
    first = iota(bias.shape, 1) // span % 2 == 0
    low = jnp.sum(jnp.where(first, bias, 0.0), axis=1, keepdims=True)
    high = jnp.sum(jnp.where(first, 0.0, bias), axis=1, keepdims=True)
    here = iota(sums.shape, 0) == level - 1
    lane = iota(sums.shape, 1)
    sums = jnp.where(here & (lane == 0), low, sums)
    return jnp.where(here & (lane == 1), high, sums)


def grad_rows(gt, tops, logs, inners, span, spread):
    f = [jnp.exp(tops[h] - logs[h]) for h in range(2)]
    g = dot_nt(spread[...], by_head(f[0], f[1], gt).astype(BF16))
    mine = (iota(g.shape, 1) < HALF) == (iota(g.shape, 0) // span % 2 == 0)
    g = jnp.where(mine, g, 0.0).astype(BF16)
    flat = [part for h in range(2) for part in split3(f[h] * inners[h])]
    wide = dot_nt(stacked(flat, 16).astype(BF16), spread[...])
    low = wide[0:1] + wide[1:2] + wide[2:3]
    high = wide[3:4] + wide[4:5] + wide[5:6]
    corr = jnp.where(iota(low.shape, 1) // span % 2 == 0, low, high)
    return g, corr


def window_back(weights, values, queries, g, corr):
    dots = dot_nt(values, g)
    grad = weights * (dots - corr)
    short = grad.astype(BF16)
    return short, dot_nn(short, queries), dot_nn(weights.astype(BF16), g), grad


def level_back(weights, keys, values, queries, gt, tops, logs, inners, span, spread):
    g, corr = grad_rows(gt, tops, logs, inners, span, spread)
    short, dk, dv, grad = window_back(weights, values, queries, g, corr)
    dq = own_head(dot_nn(keys.T, short), span).astype(BF16)
    return dot_nn(dq, spread[...]), jnp.sum(grad, axis=0, keepdims=True), dk, dv


def near_backward_kernel(
    edge_ref, q_ref, qc_ref, k_ref, v_ref, kvc_ref, g_ref, nl_ref, nr_ref, halo_ref, f1_ref, f2_ref, f3_ref,
    st_ref, st2_ref, dqf_ref,
    dq_ref, own_ref, gl_ref, gr_ref, d1_ref, d2_ref, d3_ref, bias_ref,
    e1, e2, e3, *scratch,
):
    step = pl.program_id(0)

    @pl.when(step == 0)
    def _():
        e1[...] = spreader(1)
        e2[...] = spreader(2)
        e3[...] = spreader(3)

    def one(s):
        wide = [lane_view(r, s) for r in (q_ref, qc_ref, k_ref, v_ref, kvc_ref, g_ref, nl_ref, nr_ref, halo_ref)]
        pieces = [lane_view(r, s) for r in (f1_ref, f2_ref, f3_ref)]
        per = [r.at[s : s + 1] for r in (st_ref, st2_ref, dqf_ref, dq_ref)]
        out = [lane_view(r, s) for r in (own_ref, gl_ref, gr_ref, d1_ref, d2_ref, d3_ref)]
        return near_backward_pair(
            edge_ref, *wide, pieces, *per, *out, bias_ref.at[s : s + 1], e1, e2, e3, *[r.at[s] for r in scratch]
        )

    interleaved(one(s) for s in range(SUB))


def near_backward_pair(
    edge_ref, q_ref, qc_ref, k_ref, v_ref, kvc_ref, g_ref, nl_ref, nr_ref, halo_ref, pieces, st_ref, st2_ref, dqf_ref,
    dq_ref, own_ref, gl_ref, gr_ref, d1_ref, d2_ref, d3_ref, bias_ref,
    e1, e2, e3, k0s, k1s, k2s, v0s, v1s, v2s, kt0, kt1, kt2,
    dk0, dk1, dk2, dv0, dv1, dv2,
):
    left_bias, right_bias = edge_ref[0], edge_ref[1]
    q0 = q_ref[0] * jnp.asarray(0.125, BF16)
    q1, q2, q3 = qc_ref[0:256], qc_ref[256:384], qc_ref[384:448]
    keys = near_keys(k_ref[0], kvc_ref[0], nl_ref[0], nr_ref[0], halo_ref[0])
    for dst, tdst, x in zip((k0s, k1s, k2s), (kt0, kt1, kt2), keys):
        dst[...] = x
        tdst[...] = x.T
    for dst, x in zip((v0s, v1s, v2s), near_keys(v_ref[0], kvc_ref[1], nl_ref[1], nr_ref[1], halo_ref[1])):
        dst[...] = x
    for ref in (dk0, dk1, dk2, dv0, dv1, dv2):
        ref[...] = jnp.zeros(ref.shape, F32)

    yield
    gt = g_ref[0].T.astype(F32)
    logs = [st2_ref[0, 0:1, :], st2_ref[0, 1:2, :]]
    inners = [st2_ref[0, 2:3, :], st2_ref[0, 3:4, :]]
    dqt = dqf_ref[0]
    sums = jnp.zeros((8, 128), F32)

    third = [jnp.concatenate([r[i] for r in pieces], axis=0) for i in range(2)]
    queries = two_heads(q3)
    scores = with_bias(dot_nt(third[0], queries), third_biases(edge_ref))
    weights = jnp.exp(scores - st_ref[0, 4:5, 0:128])
    tops = [st_ref[0, 13 + h : 14 + h, :] for h in range(2)]
    dq, bias, dk, dv = level_back(weights, *third, queries, gt, tops, logs, inners, HALF, e3)
    dqt = dqt + dq * (0.125 / 8)
    sums = place(sums, 3, bias, HALF)
    for n, ref in enumerate((d1_ref, d2_ref, d3_ref)):
        ref[0] = dk[n * HALF : (n + 1) * HALF].astype(BF16)
        ref[1] = dv[n * HALF : (n + 1) * HALF].astype(BF16)
    yield

    for level, ks, vs, kt, dk, dv, queries, spread in (
        (1, k1s, v1s, kt1, dk1, dv1, q1, e1),
        (2, k2s, v2s, kt2, dk2, dv2, q2, e2),
    ):
        halves = 8 >> level
        tops = [st_ref[0, 7 + 2 * level + h : 8 + 2 * level + h, :] for h in range(2)]
        g, corr = grad_rows(gt, tops, logs, inners, HALF, spread)
        dqs = []
        bias = jnp.zeros((1, 128), F32)
        for j in range(halves):
            spans = window_spans(j)
            at = slice(j * 128, (j + 1) * 128)
            queries_j = two_heads(queries[j * HALF : (j + 1) * HALF])
            scores = dot_nt(rows_of(ks, spans), queries_j)
            scores = with_bias(scores, window_biases(j, halves, left_bias, right_bias))
            weights = jnp.exp(scores - st_ref[0, 1 + level : 2 + level, at])
            short, dk_j, dv_j, grad = window_back(weights, rows_of(vs, spans), queries_j, g[at], corr[:, at])
            bias = bias + jnp.sum(grad, axis=0, keepdims=True)
            base = 0
            for lo, hi in spans:
                dk[lo:hi, :] += dk_j[base : base + hi - lo]
                dv[lo:hi, :] += dv_j[base : base + hi - lo]
                base += hi - lo
            kt_j = jnp.concatenate([kt[:, lo:hi] for lo, hi in spans], axis=1)
            dqs.append(own_head(dot_nn(kt_j, short), HALF).astype(BF16))
            yield
        dqt = dqt + dot_nn(jnp.concatenate(dqs, axis=1), spread[...]) * (0.125 / 2**level)
        sums = place(sums, level, bias, HALF)
    bias_ref[0] = sums

    g0, corr0 = zero_rows(gt, st_ref, logs, inners)
    dq0 = {}
    for b in (0, 3):
        span = slice(b * 128, b * 128 + 384)
        dq0[b], dk_b, dv_b = block_back(
            b, k0s[span, :], v0s[span, :], kt0[:, span], q0, g0, corr0, st_ref, left_bias, right_bias
        )
        dk0[span, :] += dk_b
        dv0[span, :] += dv_b
        yield
    blank = jnp.zeros((PAIR, 256), F32)
    dq_ref[0] = dqt + jnp.concatenate([dq0[0], blank, dq0[3]], axis=1)

    for i, (zero, one, two) in enumerate(((dk0, dk1, dk2), (dv0, dv1, dv2))):
        left1 = one[0:128, :] + uncoarsen(two[64:128, :])
        left0 = zero[0:128, :] + uncoarsen(left1[64:128])
        gl_ref[i, 0:128, :] = left0.astype(BF16)
        gl_ref[i, 128:192, :] = left1[0:64].astype(BF16)
        gl_ref[i, 192:256, :] = two[0:64, :].astype(BF16)
        right1 = one[384:512, :] + uncoarsen(two[256:320, :])
        right0 = zero[640:768, :] + uncoarsen(right1[0:64])
        gr_ref[i, 0:128, :] = right0.astype(BF16)
        gr_ref[i, 128:192, :] = right1[64:128].astype(BF16)
        gr_ref[i, 192:256, :] = two[320:384, :].astype(BF16)
        mine1 = one[128:384, :] + uncoarsen(two[128:256, :])
        own_ref[i] = zero[128:640, :] + uncoarsen(mine1)


def zero_rows(gt, st_ref, logs, inners):
    f0 = [jnp.exp(st_ref[0, h : h + 1, :] - logs[h]) for h in range(2)]
    g0 = by_head(f0[0], f0[1], gt).astype(BF16).T
    return g0, [f0[h] * inners[h] for h in range(2)]


def block_back(b, keys, values, keys_t, q0, g0, corr0, st_ref, left_bias, right_bias):
    at = slice(b * 128, (b + 1) * 128)
    queries = two_heads(q0[at])
    scores = with_bias(dot_nt(keys, queries), block_biases(b, left_bias, right_bias))
    top = jnp.concatenate([st_ref[0, 0:1, at], st_ref[0, 1:2, at]], axis=1)
    corr = jnp.concatenate([corr0[0][:, at], corr0[1][:, at]], axis=1)
    weights = jnp.exp(scores - top)
    short, dk, dv, _ = window_back(weights, values, queries, two_heads(g0[at]), corr)
    dq = dot_nn(keys_t, short)
    return jnp.concatenate([dq[:HALF, :128], dq[HALF:, 128:]], axis=0) * 0.125, dk, dv


def own_backward_kernel(
    q_ref, k_ref, v_ref, g_ref, st_ref, st2_ref, dqt_ref, own_in_ref, b1_ref, b2_ref, dq_ref, own_ref, bias_ref
):
    bias_ref[...] = b1_ref[...] + b2_ref[...]

    def one(s):
        wide = [lane_view(r, s) for r in (q_ref, k_ref, v_ref, g_ref)]
        per = [r.at[s : s + 1] for r in (st_ref, st2_ref, dqt_ref)]
        return own_backward_pair(*wide, *per, *[lane_view(r, s) for r in (own_in_ref, dq_ref, own_ref)])

    interleaved(one(s) for s in range(SUB))


def own_backward_pair(q_ref, k_ref, v_ref, g_ref, st_ref, st2_ref, dqt_ref, own_in_ref, dq_ref, own_ref):
    q0 = q_ref[0] * jnp.asarray(0.125, BF16)
    keys, values = k_ref[0], v_ref[0]
    keys_t = keys.T
    gt = g_ref[0].T.astype(F32)
    logs = [st2_ref[0, 0:1, :], st2_ref[0, 1:2, :]]
    inners = [st2_ref[0, 2:3, :], st2_ref[0, 3:4, :]]
    g0, corr0 = zero_rows(gt, st_ref, logs, inners)
    yield
    out = {}
    for b in (1, 2):
        span = slice((b - 1) * 128, (b + 2) * 128)
        out[b] = block_back(b, keys[span], values[span], keys_t[:, span], q0, g0, corr0, st_ref, None, None)
        yield
    dqt = dqt_ref[0]
    dqt = jnp.concatenate([dqt[:, :128], dqt[:, 128:256] + out[1][0], dqt[:, 256:384] + out[2][0], dqt[:, 384:]], axis=1)
    dq_ref[0] = dqt.astype(BF16).T
    for i in range(2):
        one, two = out[1][1 + i], out[2][1 + i]
        own_ref[i, 0:128, :] = own_in_ref[i, 0:128, :] + one[0:128]
        own_ref[i, 128:384, :] = own_in_ref[i, 128:384, :] + one[128:384] + two[0:256]
        own_ref[i, 384:512, :] = own_in_ref[i, 384:512, :] + two[256:384]


def finish_kernel(own_ref, left_ref, right_ref, a_ref, b_ref, c_ref, sum_ref, next_ref, prev_ref, dk_ref, dv_ref):
    up2, up4, up8 = doubling(HALF, 2), doubling(HALF, 4), doubling(HALF, 8)
    for i, out in enumerate((dk_ref, dv_ref)):
        four = sum_ref[i, 0:32, :].astype(F32) + next_ref[i].astype(F32) + prev_ref[i].astype(F32)
        three = uncoarsen(four)
        for ref in (a_ref, b_ref, c_ref):
            three = three + ref[i].astype(F32)
        far = dot_nn(up8, three.astype(BF16)) * 0.125
        left1 = dot_nn(up2, left_ref[i, 128:192, :]) * 0.5
        left2 = dot_nn(up4, left_ref[i, 192:256, :]) * 0.25
        right1 = dot_nn(up2, right_ref[i, 128:192, :]) * 0.5
        right2 = dot_nn(up4, right_ref[i, 192:256, :]) * 0.25
        parts = [
            left_ref[i, 0:128, :].astype(F32) + right2[0:128],
            left1 + right2[128:256],
            left2[0:128] + right1,
            left2[128:256] + right_ref[i, 0:128, :].astype(F32),
        ]
        out[0] = (own_ref[i] + far + jnp.concatenate(parts, axis=0)).astype(BF16)


def lanes(rows, *lead, pairs=SUB):
    shape = tuple(lead) + (rows, PAIR * pairs)
    zeros = (0,) * (len(shape) - 1)
    return pl.BlockSpec(shape, lambda p: zeros + (p,))


def per_pair(*shape):
    zeros = (0,) * len(shape)
    return pl.BlockSpec((SUB,) + shape, lambda p: (p,) + zeros)


def interleaved(parts):
    live = list(parts)
    while live:
        for part in list(live):
            try:
                next(part)
            except StopIteration:
                live.remove(part)


def lane_view(ref, s):
    return ref.at[..., s * PAIR : (s + 1) * PAIR]


def scalars():
    return pl.BlockSpec(memory_space=pltpu.SMEM)


def shape_of(*shape, dtype=BF16):
    return jax.ShapeDtypeStruct(shape, dtype)


def call(kernel, steps, in_specs, out_specs, out_shape, scratch, cost, name):
    return pl.pallas_call(
        kernel,
        grid=(steps,),
        in_specs=in_specs,
        out_specs=out_specs,
        out_shape=out_shape,
        scratch_shapes=scratch,
        compiler_params=pltpu.CompilerParams(
            vmem_limit_bytes=48 * MIB, dimension_semantics=("arbitrary",)
        ),
        cost_estimate=pl.CostEstimate(flops=cost, bytes_accessed=cost // 300, transcendentals=0),
        name=name,
    )


def permute(block, route):
    return lax.ppermute(block, "ctx", route)


def shifted(block, distance):
    n = lax.axis_size("ctx")
    return permute(block, [(i, i + distance) for i in range(n) if 0 <= i + distance < n])


def crossed(block, span):
    n = lax.axis_size("ctx")
    route = []
    for i in range(n):
        to = i + 3 * span if i // span % 2 == 0 else i - 3 * span
        if 0 <= to < n:
            route.append((i, to))
    return permute(block, route)


def ring_groups():
    n = lax.axis_size("ctx")
    return [list(range(i, i + RING)) for i in range(0, n, RING)]


def total_over_devices(x):
    count = lax.axis_size("dp") * lax.axis_size("ctx")

    def from_device(x, mask):
        return lax.ppermute(x, ("dp", "ctx"), [(i, i ^ mask) for i in range(count)])

    bits = [1 << i for i in range(count.bit_length() - 1)]
    while bits:
        a, b = bits.pop(0), bits.pop() if len(bits) % 2 else bits.pop(0)
        x = (x + from_device(x, a)) + (from_device(x, b) + from_device(x, a | b))
    return x


def body(queries, key_rows, values, grad_out, level_bias):
    width = queries.shape[2]
    pairs = width // PAIR
    n = lax.axis_size("ctx")
    me = lax.axis_index("ctx")

    def bias_of(flags):
        return jnp.where(jnp.stack(flags), 0.0, NEGATIVE).astype(F32)

    half = me % RING // 2
    is_first = half < 2
    has_prev, has_next = me >= RING, me < n - RING
    near_ring, far_ring = jnp.where(is_first, has_prev, has_next), jnp.where(is_first, has_next, has_prev)
    edge_bias = bias_of([
        me > 0, me < n - 1, me >= 2, me + 2 < n, jnp.where(me % 2 == 0, me + 3 < n, me >= 3)
    ])
    far_bias = jnp.stack([
        bias_of([half != 1, half != 2, near_ring & (half != 3), near_ring & (half != 0)]),
        bias_of([has_prev, has_next, far_ring, far_ring]),
    ])
    flag = is_first.astype(jnp.int32)[None]

    send_right, send_left, l3, l4, kv_coarse = call(
        prep_kernel, pairs // 4,
        [lanes(512, 1, pairs=4)] * 2,
        [lanes(r, 2, pairs=4) for r in (256, 256, 64, 32, 384)],
        [shape_of(2, r, width) for r in (256, 256, 64, 32, 384)],
        [], 400_000_000, "prep",
    )(key_rows, values)

    from_prev = shifted(l4, RING)
    from_next = shifted(l4, -RING)
    near_left = shifted(send_right, 1)
    near_right = shifted(send_left, -1)
    third = [shifted(l3, 2), shifted(l3, -2), crossed(l3, 1)]

    share = call(
        share_kernel, pairs // 4,
        [scalars()] + [lanes(32, 2, pairs=4)] * 3,
        [lanes(SHARE, 2, pairs=4)],
        [shape_of(2, SHARE, width)],
        [], 400_000_000, "share",
    )(flag, l4, from_next, from_prev)[0]
    ring = lax.all_gather(share, "ctx", axis=1, tiled=True, axis_index_groups=ring_groups())

    q_coarse = call(
        query_kernel, pairs // 4,
        [lanes(512, 1, pairs=4)], [lanes(496, pairs=4)], [shape_of(496, width)],
        [], 400_000_000, "queries",
    )(queries)[0]

    spreads = [pltpu.VMEM((r, 512), BF16) for r in (512, 256, 128)]
    key_sets = [pltpu.VMEM((SUB, r, PAIR), BF16) for r in (768, 512, 384)]
    turned = [pltpu.VMEM((SUB, PAIR, r), BF16) for r in (768, 512, 384)]
    sums = [pltpu.VMEM((SUB, r, PAIR), F32) for r in (768, 512, 384)]

    stats, numer, halo = call(
        near_forward_kernel, pairs // SUB,
        [scalars(), scalars(), lanes(512, 1), lanes(496), lanes(512, 1), lanes(512, 1), lanes(384, 2)]
        + [lanes(256, 2)] * 2 + [lanes(64, 2)] * 3,
        [per_pair(16, 512), per_pair(PAIR, 512), lanes(256, 2)],
        [
            shape_of(pairs, 16, 512, dtype=F32), shape_of(pairs, PAIR, 512, dtype=F32), shape_of(2, 256, width)
        ],
        spreads + key_sets + turned, 30_000_000_000, "near_forward",
    )(level_bias, edge_bias, queries, q_coarse, key_rows, values, kv_coarse, near_left, near_right, *third)

    attended, stats2, dq_far, d_ring, bias_far = call(
        far_kernel, pairs // SUB,
        [scalars()] * 3 + [lanes(496), lanes(512, 1), per_pair(16, 512), per_pair(PAIR, 512), lanes(RING * SHARE, 2)],
        [lanes(512, 1), per_pair(8, 512), per_pair(PAIR, 512), lanes(RING * SHARE, 2), per_pair(8, 128)],
        [
            shape_of(1, 512, width),
            shape_of(pairs, 8, 512, dtype=F32),
            shape_of(pairs, PAIR, 512, dtype=F32),
            shape_of(2, RING * SHARE, width),
            shape_of(pairs, 8, 128, dtype=F32),
        ],
        [pltpu.VMEM((r, 512), BF16) for r in (64, 32)], 20_000_000_000, "far",
    )(level_bias, far_bias, flag, q_coarse, grad_out, stats, numer, ring)

    d_share = lax.psum_scatter(d_ring, "ctx", scatter_dimension=1, tiled=True, axis_index_groups=ring_groups())

    grad_qt, own_part, to_left, to_right, d1, d2, d3, bias_near = call(
        near_backward_kernel, pairs // SUB,
        [scalars(), lanes(512, 1), lanes(496), lanes(512, 1), lanes(512, 1), lanes(384, 2), lanes(512, 1)]
        + [lanes(256, 2)] * 3 + [lanes(64, 2)] * 3
        + [per_pair(16, 512), per_pair(8, 512), per_pair(PAIR, 512)],
        [per_pair(PAIR, 512), lanes(512, 2)] + [lanes(256, 2)] * 2 + [lanes(64, 2)] * 3 + [per_pair(8, 128)],
        [shape_of(pairs, PAIR, 512, dtype=F32), shape_of(2, 512, width, dtype=F32)]
        + [shape_of(2, 256, width)] * 2 + [shape_of(2, 64, width)] * 3 + [shape_of(pairs, 8, 128, dtype=F32)],
        spreads + key_sets + key_sets + turned + sums + sums, 30_000_000_000, "near_backward",
    )(
        edge_bias, queries, q_coarse, key_rows, values, kv_coarse, grad_out,
        near_left, near_right, halo, *third, stats, stats2, dq_far,
    )

    back_right, back_left = shifted(to_right, 1), shifted(to_left, -1)
    back = [shifted(d1, -2), shifted(d2, 2), crossed(d3, 1)]

    grad_q, own, bias = call(
        own_backward_kernel, pairs // SUB,
        [lanes(512, 1)] * 4 + [per_pair(16, 512), per_pair(8, 512), per_pair(PAIR, 512), lanes(512, 2)]
        + [per_pair(8, 128)] * 2,
        [lanes(512, 1), lanes(512, 2), per_pair(8, 128)],
        [shape_of(1, 512, width), shape_of(2, 512, width, dtype=F32), shape_of(pairs, 8, 128, dtype=F32)],
        [], 15_000_000_000, "own_backward",
    )(queries, key_rows, values, grad_out, stats, stats2, grad_qt, own_part, bias_far, bias_near)

    share_next, share_prev = call(
        unshare_kernel, pairs // 4,
        [scalars(), lanes(SHARE, 2, pairs=4)],
        [lanes(32, 2, pairs=4)] * 2,
        [shape_of(2, 32, width)] * 2,
        [], 400_000_000, "unshare",
    )(flag, d_share)
    back_next, back_prev = shifted(share_prev, -RING), shifted(share_next, RING)

    bias = jnp.transpose(bias[:, : LEVELS - 1, :2], (1, 0, 2)).reshape(LEVELS - 1, 2 * pairs)
    grad_bias = total_over_devices(bias) * (
        1.0 / math.sqrt(512 * n * lax.axis_size("dp"))
    )

    grad_k, grad_v = call(
        finish_kernel, pairs // 4,
        [lanes(r, 2, pairs=4) for r in (512, 256, 256, 64, 64, 64, SHARE, 32, 32)],
        [lanes(512, 1, pairs=4)] * 2,
        [shape_of(1, 512, width)] * 2,
        [], 400_000_000, "finish",
    )(own, back_right, back_left, *back, d_share, back_next, back_prev)
    return attended, grad_q, grad_k, grad_v, grad_bias


def solution(mesh):
    rows = P("dp", "ctx", None)
    return jax.shard_map(
        body,
        mesh=mesh,
        in_specs=(rows, rows, rows, rows, P()),
        out_specs=(rows, rows, rows, rows, P()),
        check_vma=False,
    )
```

```python
import math

import jax
import jax.numpy as jnp
from jax import lax
from jax.experimental import pallas as pl
from jax.experimental.pallas import tpu as pltpu
from jax.sharding import PartitionSpec as P

BLOCK = 128
HALF = 64
LEVELS = 6
PAIR = 128
NEGATIVE = -1e30
LN2 = math.log(2.0)
F32 = jnp.float32
BF16 = jnp.bfloat16
MIB = 1 << 20
RING = 8
SHARE = 80
SUB = 2


def dot_nn(a, b):
    return lax.dot_general(a, b, (((1,), (0,)), ((), ())), preferred_element_type=F32)


def dot_nt(a, b):
    return lax.dot_general(a, b, (((1,), (1,)), ((), ())), preferred_element_type=F32)


def iota(shape, dim):
    return lax.broadcasted_iota(jnp.int32, shape, dim)


def halving(n):
    return jnp.where(iota((n // 2, n), 1) // 2 == iota((n // 2, n), 0), 0.5, 0.0).astype(BF16)


def doubling(n, factor):
    return (iota((n * factor, n), 0) // factor == iota((n * factor, n), 1)).astype(BF16)


def coarsen(x):
    rows = x.shape[0]
    step = min(rows, BLOCK)
    mean = halving(step)
    parts = [dot_nn(mean, x[i : i + step]).astype(BF16) for i in range(0, rows, step)]
    return parts[0] if len(parts) == 1 else jnp.concatenate(parts, axis=0)


def uncoarsen(x):
    rows = x.shape[0]
    step = min(rows, HALF)
    up = doubling(step, 2)
    half = (x * 0.5).astype(BF16)
    parts = [dot_nn(up, half[i : i + step]) for i in range(0, rows, step)]
    return parts[0] if len(parts) == 1 else jnp.concatenate(parts, axis=0)


def two_heads(x):
    low = iota(x.shape, 1) < HALF
    zero = jnp.zeros_like(x)
    return jnp.concatenate([jnp.where(low, x, zero), jnp.where(low, zero, x)], axis=0)


def own_head(x, span):
    same = (iota(x.shape, 0) < HALF) == (iota(x.shape, 1) // span % 2 == 0)
    return jnp.where(same, x, 0.0)


def spreader(level):
    rows = 512 >> level
    span = min(rows, HALF)
    shape = (2 * rows, 512)
    c = iota(shape, 0)
    row = c // (2 * span) * span + c % span
    return (iota(shape, 1) // 2**level == row).astype(BF16)


def split3(x):
    high = x.astype(BF16).astype(F32)
    rest = x - high
    mid = rest.astype(BF16).astype(F32)
    return high, mid, rest - mid


def stacked(rows, height):
    shape = (height, rows[0].shape[1])
    which = iota(shape, 0)
    out = jnp.zeros(shape, F32)
    for i, row in enumerate(rows):
        out = jnp.where(which == i, row, out)
    return out


def by_head(top, bottom, x):
    return jnp.concatenate([x[:HALF] * top, x[HALF:] * bottom], axis=0)


def spread_stats(rows, span, spread):
    flat = []
    for row in rows:
        first = iota(row.shape, 1) // span % 2 == 0
        for part in split3(row):
            flat.append(jnp.where(first, part, 0.0))
        for part in split3(row):
            flat.append(jnp.where(first, 0.0, part))
    wide = dot_nn(stacked(flat, 16).astype(BF16), spread)
    out = []
    for i in range(2 * len(rows)):
        out.append(wide[3 * i : 3 * i + 1] + wide[3 * i + 1 : 3 * i + 2] + wide[3 * i + 2 : 3 * i + 3])
    return out


def offset_row(low, high, span, shape):
    return jnp.where(iota(shape, 1) // span % 2 == 0, low, high)


def softmax_of(scores):
    top = jnp.max(scores, axis=0, keepdims=True)
    weights = jnp.exp(scores - top)
    return top, weights, jnp.sum(weights, axis=0, keepdims=True)


def with_bias(scores, biases):
    parts = []
    at = 0
    for lo, hi, bias in biases:
        if lo > at:
            parts.append(scores[at:lo])
        parts.append(scores[lo:hi] + bias)
        at = hi
    if at < scores.shape[0]:
        parts.append(scores[at:])
    return jnp.concatenate(parts, axis=0)


def halo_coarse(left, right):
    left1, right1 = coarsen(left[:128]), coarsen(right[:128])
    left2 = coarsen(jnp.concatenate([left[128:192], left1], axis=0))
    right2 = coarsen(jnp.concatenate([right1, right[128:192]], axis=0))
    return jnp.concatenate([left1, right1, left2, right2], axis=0)


def near_keys(own, coarse, left, right, halo):
    def joined(*parts):
        return jnp.concatenate(parts, axis=0)

    return (
        joined(left[:128], own, right[:128]),
        joined(left[128:192], halo[:64], coarse[:256], halo[64:128], right[128:192]),
        joined(left[192:256], halo[128:192], coarse[256:384], halo[192:256], right[192:256]),
    )


def window_parts(j):
    if j % 2 == 0:
        return (j, j + 4, j + 5)
    return (j - 1, j, j + 4)


def window_spans(j):
    a, b, c = window_parts(j)
    if b == a + 1:
        return [(a * HALF, (b + 1) * HALF), (c * HALF, (c + 1) * HALF)]
    return [(a * HALF, (a + 1) * HALF), (b * HALF, (c + 1) * HALF)]


def window_biases(j, halves, left_bias, right_bias):
    out = []
    for i, part in enumerate(window_parts(j)):
        if part < 2:
            out.append((i * HALF, (i + 1) * HALF, left_bias))
        elif part >= halves + 2:
            out.append((i * HALF, (i + 1) * HALF, right_bias))
    return out


def rows_of(ref, spans):
    if len(spans) == 1:
        return ref[spans[0][0] : spans[0][1], :]
    return jnp.concatenate([ref[lo:hi, :] for lo, hi in spans], axis=0)


def block_biases(b, left_bias, right_bias):
    if b == 0:
        return [(0, 128, left_bias)]
    if b == 3:
        return [(256, 384, right_bias)]
    return []


def prep_kernel(k_ref, v_ref, right_ref, left_ref, l3_ref, l4_ref, coarse_ref):
    for i, ref in enumerate((k_ref, v_ref)):
        zero = ref[0]
        one = coarsen(zero)
        two = coarsen(one)
        three = coarsen(two)
        right_ref[i, 0:128, :] = zero[384:512]
        right_ref[i, 128:192, :] = one[128:192]
        right_ref[i, 192:256, :] = two[0:64]
        left_ref[i, 0:128, :] = zero[0:128]
        left_ref[i, 128:192, :] = one[64:128]
        left_ref[i, 192:256, :] = two[64:128]
        l3_ref[i] = three
        l4_ref[i] = coarsen(three)
        coarse_ref[i, 0:256, :] = one
        coarse_ref[i, 256:384, :] = two


def query_kernel(q_ref, out_ref):
    rows = q_ref[0] * jnp.asarray(0.125, BF16)
    at = 0
    for level in range(1, LEVELS):
        rows = coarsen(rows)
        out_ref[at : at + (512 >> level), :] = rows
        at += 512 >> level


def pack_kernel(flag_ref, ring_ref, next_ref, prev_ref, opposite_ref):
    first = flag_ref[0] > 0
    for i in range(2):
        four = ring_ref[i]
        five = coarsen(four)
        next_ref[i, 0:128, :] = jnp.where(first, four[128:256], five)
        next_ref[i, 128:192, :] = five[0:64]
        prev_ref[i, 0:128, :] = jnp.where(first, five, four[0:128])
        prev_ref[i, 128:192, :] = five[64:128]
        opposite_ref[i] = jnp.where(first, four[128:256], four[0:128])


def unshare_kernel(flag_ref, sum_ref, next_ref, prev_ref):
    first = flag_ref[0] > 0
    for i in range(2):
        four = sum_ref[i, 32:64, :]
        five = uncoarsen(sum_ref[i, 64:80, :].astype(F32)).astype(BF16)
        next_ref[i] = jnp.where(first, four, five)
        prev_ref[i] = jnp.where(first, five, four)


def near_forward_kernel(
    off_ref, edge_ref, q_ref, qc_ref, k_ref, v_ref, kvc_ref, nl_ref, nr_ref,
    st_ref, nt_ref, halo_ref, e1, e2, *scratch,
):
    step = pl.program_id(0)

    @pl.when(step == 0)
    def _():
        e1[...] = spreader(1)
        e2[...] = spreader(2)

    interleaved(
        near_forward_pair(
            step * SUB + s, off_ref, edge_ref, *[lane_view(r, s) for r in (q_ref, qc_ref, k_ref, v_ref, kvc_ref, nl_ref, nr_ref)],
            st_ref.at[s : s + 1], nt_ref.at[s : s + 1], lane_view(halo_ref, s), e1, e2, *[r.at[s] for r in scratch],
        )
        for s in range(SUB)
    )


def near_forward_pair(
    pair, off_ref, edge_ref, q_ref, qc_ref, k_ref, v_ref, kvc_ref, nl_ref, nr_ref, st_ref, nt_ref, halo_ref,
    e1, e2, k0s, k1s, k2s, vt0, vt1, vt2,
):
    left_bias, right_bias = edge_ref[0], edge_ref[1]
    q0 = q_ref[0] * jnp.asarray(0.125, BF16)
    q1, q2 = qc_ref[0:256], qc_ref[256:384]
    halos = [halo_coarse(nl_ref[i], nr_ref[i]) for i in range(2)]
    for i in range(2):
        halo_ref[i] = halos[i]
    for dst, x in zip((k0s, k1s, k2s), near_keys(k_ref[0], kvc_ref[0], nl_ref[0], nr_ref[0], halos[0])):
        dst[...] = x
    for dst, x in zip((vt0, vt1, vt2), near_keys(v_ref[0], kvc_ref[1], nl_ref[1], nr_ref[1], halos[1])):
        dst[...] = x.T
    yield

    tops, totals, mixes = [], [], []
    for b in range(4):
        keys = k0s[b * 128 : b * 128 + 384, :]
        scores = dot_nt(keys, two_heads(q0[b * 128 : b * 128 + 128]))
        scores = with_bias(scores, block_biases(b, left_bias, right_bias))
        top, weights, total = softmax_of(scores)
        mixed = dot_nn(vt0[:, b * 128 : b * 128 + 384], weights.astype(BF16))
        tops.append(top)
        totals.append(total)
        mixes.append(jnp.concatenate([mixed[:HALF, :128], mixed[HALF:, 128:]], axis=0))
        yield
    top_a = jnp.concatenate([t[:, :128] for t in tops], axis=1)
    top_b = jnp.concatenate([t[:, 128:] for t in tops], axis=1)
    total_a = jnp.concatenate([t[:, :128] for t in totals], axis=1)
    total_b = jnp.concatenate([t[:, 128:] for t in totals], axis=1)
    st_ref[0, 0:1, :] = top_a
    st_ref[0, 1:2, :] = top_b
    mixed0 = jnp.concatenate(mixes, axis=1)

    coarse = []
    for level, keys_ref, vt_ref, queries, spread in (
        (1, k1s, vt1, q1, e1), (2, k2s, vt2, q2, e2),
    ):
        halves = 8 >> level
        tops, totals, mixes = [], [], []
        for j in range(halves):
            spans = window_spans(j)
            scores = dot_nt(rows_of(keys_ref, spans), two_heads(queries[j * HALF : (j + 1) * HALF]))
            scores = with_bias(scores, window_biases(j, halves, left_bias, right_bias))
            top, weights, total = softmax_of(scores)
            vt = jnp.concatenate([vt_ref[:, lo:hi] for lo, hi in spans], axis=1)
            mixes.append(own_head(dot_nn(vt, weights.astype(BF16)), HALF).astype(BF16))
            tops.append(top)
            totals.append(total)
            yield
        top = jnp.concatenate(tops, axis=1)
        total = jnp.concatenate(totals, axis=1)
        st_ref[0, 1 + level : 2 + level, 0 : top.shape[1]] = top
        low = off_ref[level - 1, 2 * pair] + level * LN2
        high = off_ref[level - 1, 2 * pair + 1] + level * LN2
        top = top + offset_row(low, high, HALF, top.shape)
        wide = spread_stats([top, total], HALF, spread[...])
        mixed = dot_nn(jnp.concatenate(mixes, axis=1), spread[...])
        st_ref[0, 7 + 2 * level : 8 + 2 * level, :] = wide[0]
        st_ref[0, 8 + 2 * level : 9 + 2 * level, :] = wide[1]
        coarse.append((wide, mixed))
        yield

    peaks, denoms, factors = [], [], []
    for h, (top0, total0) in enumerate(((top_a, total_a), (top_b, total_b))):
        peak = top0
        for wide, _ in coarse:
            peak = jnp.maximum(peak, wide[h])
        f = [jnp.exp(top0 - peak)] + [jnp.exp(wide[h] - peak) for wide, _ in coarse]
        denom = f[0] * total0
        for i, (wide, _) in enumerate(coarse):
            denom = denom + f[i + 1] * wide[2 + h]
        peaks.append(peak)
        denoms.append(denom)
        factors.append(f)
    numer = by_head(factors[0][0], factors[1][0], mixed0)
    for i, (_, mixed) in enumerate(coarse):
        numer = numer + by_head(factors[0][i + 1], factors[1][i + 1], mixed)
    st_ref[0, 5:6, :] = peaks[0]
    st_ref[0, 6:7, :] = peaks[1]
    st_ref[0, 7:8, :] = denoms[0]
    st_ref[0, 8:9, :] = denoms[1]
    nt_ref[0] = numer


def far_kernel(
    off_ref, edge_ref, far_ref, flag_ref, qc_ref, g_ref, st_ref, nt_ref,
    f1_ref, f2_ref, f3_ref, opposite_ref, next_ref, prev_ref,
    att_ref, st2_ref, dq_ref, dring_ref, d1_ref, d2_ref, d3_ref, bias_ref, e3, e4, e5,
):
    step = pl.program_id(0)

    @pl.when(step == 0)
    def _():
        e3[...] = spreader(3)
        e4[...] = spreader(4)
        e5[...] = spreader(5)

    def one(s):
        windows = [lane_view(r, s) for r in (f1_ref, f2_ref, f3_ref, opposite_ref, next_ref, prev_ref)]
        grads = [lane_view(r, s) for r in (dring_ref, d1_ref, d2_ref, d3_ref)]
        return far_pair(
            step * SUB + s, off_ref, edge_ref, far_ref, flag_ref[0] > 0, lane_view(qc_ref, s), lane_view(g_ref, s),
            *[r.at[s : s + 1] for r in (st_ref, nt_ref)], *windows,
            lane_view(att_ref, s), *[r.at[s : s + 1] for r in (st2_ref, dq_ref)],
            *grads, bias_ref.at[s : s + 1], (e3, e4, e5),
        )

    interleaved(one(s) for s in range(SUB))


def far_pair(
    pair, off_ref, edge_ref, far_ref, first, qc_ref, g_ref, st_ref, nt_ref,
    f1_ref, f2_ref, f3_ref, opposite_ref, next_ref, prev_ref,
    att_ref, st2_ref, dq_ref, dring_ref, d1_ref, d2_ref, d3_ref, bias_ref, spreads,
):
    lower, upper = range(RING // 2), range(RING // 2, RING)
    coarse_q = {3: qc_ref[384:448], 4: qc_ref[448:480], 5: qc_ref[480:496]}
    gt = g_ref[0].T.astype(F32)
    windows = {3: [], 4: [], 5: []}
    for i in range(2):
        after, before = next_ref[i], prev_ref[i]
        windows[3].append(jnp.concatenate([f1_ref[i], f2_ref[i], f3_ref[i]], axis=0))
        near = jnp.where(first, before[0:128], after[0:128])
        windows[4].append(jnp.concatenate([opposite_ref[i], near], axis=0))
        windows[5].append(jnp.concatenate([
            jnp.where(first, before[128:192], before[0:64]),
            jnp.where(first, after[64:128], after[128:192]),
            jnp.where(first, after[0:64], before[64:128]),
        ], axis=0))
    levels = []
    for level, spread in zip((3, 4, 5), spreads):
        span = 512 >> level
        queries = two_heads(coarse_q[level])
        keys, values = windows[level]
        scores = dot_nt(keys, queries)
        parts = keys.shape[0] // HALF
        biases = [
            (i * HALF, (i + 1) * HALF, edge_ref[2 + i] if level == 3 else far_ref[level - 4, i]) for i in range(parts)
        ]
        top, weights, total = softmax_of(with_bias(scores, biases))
        mixed = own_head(dot_nn(values.T, weights.astype(BF16)), span).astype(BF16)
        low = off_ref[level - 1, 2 * pair] + level * LN2
        high = off_ref[level - 1, 2 * pair + 1] + level * LN2
        top = top + offset_row(low, high, span, top.shape)
        wide = spread_stats([top, total], span, spread[...])
        levels.append((level, span, queries, weights, wide, dot_nn(mixed, spread[...]), spread))
        yield

    logs, inners, numers = [], [], []
    for h in range(2):
        peak0, denom0 = st_ref[0, 5 + h : 6 + h, :], st_ref[0, 7 + h : 8 + h, :]
        peak = peak0
        for item in levels:
            peak = jnp.maximum(peak, item[4][h])
        keep = jnp.exp(peak0 - peak)
        denom = keep * denom0
        numer = keep * nt_ref[0, h * HALF : (h + 1) * HALF, :]
        for item in levels:
            f = jnp.exp(item[4][h] - peak)
            denom = denom + f * item[4][2 + h]
            numer = numer + f * item[5][h * HALF : (h + 1) * HALF]
        out = (numer / denom).astype(BF16)
        numers.append(out)
        logs.append(peak + jnp.log(denom))
        inners.append(
            jnp.sum(gt[h * HALF : (h + 1) * HALF] * out.astype(F32), axis=0, keepdims=True)
        )
    att_ref[0] = jnp.concatenate(numers, axis=0).T
    st2_ref[0] = stacked([logs[0], logs[1], inners[0], inners[1]], 8)
    yield

    dqt = jnp.zeros((PAIR, 512), F32)
    sums = jnp.zeros((8, 128), F32)
    grads = {}
    for level, span, queries, weights, wide, _, spread in levels:
        dq, bias, dk, dv = level_back(
            weights, *windows[level], queries, gt, wide[:2], logs, inners, span, spread
        )
        grads[level] = (dk.astype(BF16), dv.astype(BF16))
        last = (dk[128:192], dv[128:192])
        dqt = dqt + dq * (0.125 / 2**level)
        sums = place(sums, level, bias, span)
        yield
    for i in range(2):
        for n, ref in enumerate((d1_ref, d2_ref, d3_ref)):
            ref[i] = grads[3][i][n * HALF : (n + 1) * HALF]
        four, five = grads[4][i], grads[5][i]
        blank = jnp.zeros((128, PAIR), BF16)
        far = uncoarsen(last[i]).astype(BF16)
        for part, on_low in ((lower, True), (upper, False)):
            here = jnp.logical_not(first) if on_low else first
            own = jnp.where(here, four[0:128], blank)
            foreign = jnp.where(here, four[128:256], far)
            for n, z in enumerate(part):
                at = SHARE * z
                dring_ref[i, at : at + 32, :] = own[32 * n : 32 * n + 32]
                dring_ref[i, at + 32 : at + 64, :] = foreign[32 * n : 32 * n + 32]
                dring_ref[i, at + 64 : at + 80, :] = five[16 * z : 16 * z + 16]
    dq_ref[0] = dqt
    bias_ref[0] = sums


def place(sums, level, bias, span):
    first = iota(bias.shape, 1) // span % 2 == 0
    low = jnp.sum(jnp.where(first, bias, 0.0), axis=1, keepdims=True)
    high = jnp.sum(jnp.where(first, 0.0, bias), axis=1, keepdims=True)
    here = iota(sums.shape, 0) == level - 1
    lane = iota(sums.shape, 1)
    sums = jnp.where(here & (lane == 0), low, sums)
    return jnp.where(here & (lane == 1), high, sums)


def grad_rows(gt, tops, logs, inners, span, spread):
    f = [jnp.exp(tops[h] - logs[h]) for h in range(2)]
    g = dot_nt(spread[...], by_head(f[0], f[1], gt).astype(BF16))
    mine = (iota(g.shape, 1) < HALF) == (iota(g.shape, 0) // span % 2 == 0)
    g = jnp.where(mine, g, 0.0).astype(BF16)
    flat = [part for h in range(2) for part in split3(f[h] * inners[h])]
    wide = dot_nt(stacked(flat, 16).astype(BF16), spread[...])
    low = wide[0:1] + wide[1:2] + wide[2:3]
    high = wide[3:4] + wide[4:5] + wide[5:6]
    corr = jnp.where(iota(low.shape, 1) // span % 2 == 0, low, high)
    return g, corr


def window_back(weights, values, queries, g, corr):
    dots = dot_nt(values, g)
    grad = weights * (dots - corr)
    short = grad.astype(BF16)
    return short, dot_nn(short, queries), dot_nn(weights.astype(BF16), g), grad


def level_back(weights, keys, values, queries, gt, tops, logs, inners, span, spread):
    g, corr = grad_rows(gt, tops, logs, inners, span, spread)
    short, dk, dv, grad = window_back(weights, values, queries, g, corr)
    dq = own_head(dot_nn(keys.T, short), span).astype(BF16)
    return dot_nn(dq, spread[...]), jnp.sum(grad, axis=0, keepdims=True), dk, dv


def near_backward_kernel(
    edge_ref, q_ref, qc_ref, k_ref, v_ref, kvc_ref, g_ref, nl_ref, nr_ref, halo_ref,
    st_ref, st2_ref, dqf_ref,
    dq_ref, own_ref, gl_ref, gr_ref, bias_ref,
    e1, e2, *scratch,
):
    step = pl.program_id(0)

    @pl.when(step == 0)
    def _():
        e1[...] = spreader(1)
        e2[...] = spreader(2)

    def one(s):
        wide = [lane_view(r, s) for r in (q_ref, qc_ref, k_ref, v_ref, kvc_ref, g_ref, nl_ref, nr_ref, halo_ref)]
        per = [r.at[s : s + 1] for r in (st_ref, st2_ref, dqf_ref, dq_ref)]
        out = [lane_view(r, s) for r in (own_ref, gl_ref, gr_ref)]
        return near_backward_pair(
            edge_ref, *wide, *per, *out, bias_ref.at[s : s + 1], e1, e2, *[r.at[s] for r in scratch]
        )

    interleaved(one(s) for s in range(SUB))


def near_backward_pair(
    edge_ref, q_ref, qc_ref, k_ref, v_ref, kvc_ref, g_ref, nl_ref, nr_ref, halo_ref, st_ref, st2_ref, dqf_ref,
    dq_ref, own_ref, gl_ref, gr_ref, bias_ref,
    e1, e2, k0s, k1s, k2s, v0s, v1s, v2s, kt0, kt1, kt2,
    dk0, dk1, dk2, dv0, dv1, dv2,
):
    left_bias, right_bias = edge_ref[0], edge_ref[1]
    q0 = q_ref[0] * jnp.asarray(0.125, BF16)
    q1, q2 = qc_ref[0:256], qc_ref[256:384]
    keys = near_keys(k_ref[0], kvc_ref[0], nl_ref[0], nr_ref[0], halo_ref[0])
    for dst, tdst, x in zip((k0s, k1s, k2s), (kt0, kt1, kt2), keys):
        dst[...] = x
        tdst[...] = x.T
    for dst, x in zip((v0s, v1s, v2s), near_keys(v_ref[0], kvc_ref[1], nl_ref[1], nr_ref[1], halo_ref[1])):
        dst[...] = x
    for ref in (dk0, dk1, dk2, dv0, dv1, dv2):
        ref[...] = jnp.zeros(ref.shape, F32)

    yield
    gt = g_ref[0].T.astype(F32)
    logs = [st2_ref[0, 0:1, :], st2_ref[0, 1:2, :]]
    inners = [st2_ref[0, 2:3, :], st2_ref[0, 3:4, :]]
    dqt = dqf_ref[0]
    sums = jnp.zeros((8, 128), F32)

    for level, ks, vs, kt, dk, dv, queries, spread in (
        (1, k1s, v1s, kt1, dk1, dv1, q1, e1),
        (2, k2s, v2s, kt2, dk2, dv2, q2, e2),
    ):
        halves = 8 >> level
        tops = [st_ref[0, 7 + 2 * level + h : 8 + 2 * level + h, :] for h in range(2)]
        g, corr = grad_rows(gt, tops, logs, inners, HALF, spread)
        dqs = []
        bias = jnp.zeros((1, 128), F32)
        for j in range(halves):
            spans = window_spans(j)
            at = slice(j * 128, (j + 1) * 128)
            queries_j = two_heads(queries[j * HALF : (j + 1) * HALF])
            scores = dot_nt(rows_of(ks, spans), queries_j)
            scores = with_bias(scores, window_biases(j, halves, left_bias, right_bias))
            weights = jnp.exp(scores - st_ref[0, 1 + level : 2 + level, at])
            short, dk_j, dv_j, grad = window_back(weights, rows_of(vs, spans), queries_j, g[at], corr[:, at])
            bias = bias + jnp.sum(grad, axis=0, keepdims=True)
            base = 0
            for lo, hi in spans:
                dk[lo:hi, :] += dk_j[base : base + hi - lo]
                dv[lo:hi, :] += dv_j[base : base + hi - lo]
                base += hi - lo
            kt_j = jnp.concatenate([kt[:, lo:hi] for lo, hi in spans], axis=1)
            dqs.append(own_head(dot_nn(kt_j, short), HALF).astype(BF16))
            yield
        dqt = dqt + dot_nn(jnp.concatenate(dqs, axis=1), spread[...]) * (0.125 / 2**level)
        sums = place(sums, level, bias, HALF)
    bias_ref[0] = sums

    g0, corr0 = zero_rows(gt, st_ref, logs, inners)
    dq0 = {}
    for b in (0, 3):
        span = slice(b * 128, b * 128 + 384)
        dq0[b], dk_b, dv_b = block_back(
            b, k0s[span, :], v0s[span, :], kt0[:, span], q0, g0, corr0, st_ref, left_bias, right_bias
        )
        dk0[span, :] += dk_b
        dv0[span, :] += dv_b
        yield
    blank = jnp.zeros((PAIR, 256), F32)
    dq_ref[0] = dqt + jnp.concatenate([dq0[0], blank, dq0[3]], axis=1)

    for i, (zero, one, two) in enumerate(((dk0, dk1, dk2), (dv0, dv1, dv2))):
        left1 = one[0:128, :] + uncoarsen(two[64:128, :])
        left0 = zero[0:128, :] + uncoarsen(left1[64:128])
        gl_ref[i, 0:128, :] = left0.astype(BF16)
        gl_ref[i, 128:192, :] = left1[0:64].astype(BF16)
        gl_ref[i, 192:256, :] = two[0:64, :].astype(BF16)
        right1 = one[384:512, :] + uncoarsen(two[256:320, :])
        right0 = zero[640:768, :] + uncoarsen(right1[0:64])
        gr_ref[i, 0:128, :] = right0.astype(BF16)
        gr_ref[i, 128:192, :] = right1[64:128].astype(BF16)
        gr_ref[i, 192:256, :] = two[320:384, :].astype(BF16)
        mine1 = one[128:384, :] + uncoarsen(two[128:256, :])
        own_ref[i] = zero[128:640, :] + uncoarsen(mine1)


def zero_rows(gt, st_ref, logs, inners):
    f0 = [jnp.exp(st_ref[0, h : h + 1, :] - logs[h]) for h in range(2)]
    g0 = by_head(f0[0], f0[1], gt).astype(BF16).T
    return g0, [f0[h] * inners[h] for h in range(2)]


def block_back(b, keys, values, keys_t, q0, g0, corr0, st_ref, left_bias, right_bias):
    at = slice(b * 128, (b + 1) * 128)
    queries = two_heads(q0[at])
    scores = with_bias(dot_nt(keys, queries), block_biases(b, left_bias, right_bias))
    top = jnp.concatenate([st_ref[0, 0:1, at], st_ref[0, 1:2, at]], axis=1)
    corr = jnp.concatenate([corr0[0][:, at], corr0[1][:, at]], axis=1)
    weights = jnp.exp(scores - top)
    short, dk, dv, _ = window_back(weights, values, queries, two_heads(g0[at]), corr)
    dq = dot_nn(keys_t, short)
    return jnp.concatenate([dq[:HALF, :128], dq[HALF:, 128:]], axis=0) * 0.125, dk, dv


def own_backward_kernel(
    q_ref, k_ref, v_ref, g_ref, st_ref, st2_ref, dqt_ref, own_in_ref, f1_ref, f2_ref, f3_ref, b1_ref, b2_ref,
    dq_ref, own_ref, bias_ref
):
    bias_ref[...] = b1_ref[...] + b2_ref[...]

    def one(s):
        wide = [lane_view(r, s) for r in (q_ref, k_ref, v_ref, g_ref)]
        per = [r.at[s : s + 1] for r in (st_ref, st2_ref, dqt_ref)]
        pieces = [lane_view(r, s) for r in (f1_ref, f2_ref, f3_ref)]
        return own_backward_pair(*wide, *per, pieces, *[lane_view(r, s) for r in (own_in_ref, dq_ref, own_ref)])

    interleaved(one(s) for s in range(SUB))


def own_backward_pair(
    q_ref, k_ref, v_ref, g_ref, st_ref, st2_ref, dqt_ref, pieces, own_in_ref, dq_ref, own_ref
):
    q0 = q_ref[0] * jnp.asarray(0.125, BF16)
    keys, values = k_ref[0], v_ref[0]
    keys_t = keys.T
    gt = g_ref[0].T.astype(F32)
    logs = [st2_ref[0, 0:1, :], st2_ref[0, 1:2, :]]
    inners = [st2_ref[0, 2:3, :], st2_ref[0, 3:4, :]]
    g0, corr0 = zero_rows(gt, st_ref, logs, inners)
    yield
    out = {}
    for b in (1, 2):
        span = slice((b - 1) * 128, (b + 2) * 128)
        out[b] = block_back(b, keys[span], values[span], keys_t[:, span], q0, g0, corr0, st_ref, None, None)
        yield
    dqt = dqt_ref[0]
    dqt = jnp.concatenate([dqt[:, :128], dqt[:, 128:256] + out[1][0], dqt[:, 256:384] + out[2][0], dqt[:, 384:]], axis=1)
    dq_ref[0] = dqt.astype(BF16).T
    for i in range(2):
        one, two = out[1][1 + i], out[2][1 + i]
        three = sum(ref[i].astype(F32) for ref in pieces) * 0.125
        far = dot_nn(doubling(HALF, 8), three.astype(BF16))
        own_ref[i, 0:128, :] = own_in_ref[i, 0:128, :] + far[0:128] + one[0:128]
        own_ref[i, 128:384, :] = own_in_ref[i, 128:384, :] + far[128:384] + one[128:384] + two[0:256]
        own_ref[i, 384:512, :] = own_in_ref[i, 384:512, :] + far[384:512] + two[256:384]


def finish_kernel(own_ref, left_ref, right_ref, sum_ref, next_ref, prev_ref, dk_ref, dv_ref):
    up2, up4, up16 = doubling(HALF, 2), doubling(HALF, 4), doubling(HALF // 2, 16)
    for i, out in enumerate((dk_ref, dv_ref)):
        four = sum_ref[i, 0:32, :].astype(F32) + next_ref[i].astype(F32) + prev_ref[i].astype(F32)
        far = dot_nn(up16, (four * 0.0625).astype(BF16))
        left1 = dot_nn(up2, left_ref[i, 128:192, :]) * 0.5
        left2 = dot_nn(up4, left_ref[i, 192:256, :]) * 0.25
        right1 = dot_nn(up2, right_ref[i, 128:192, :]) * 0.5
        right2 = dot_nn(up4, right_ref[i, 192:256, :]) * 0.25
        parts = [
            left_ref[i, 0:128, :].astype(F32) + right2[0:128],
            left1 + right2[128:256],
            left2[0:128] + right1,
            left2[128:256] + right_ref[i, 0:128, :].astype(F32),
        ]
        out[0] = (own_ref[i] + far + jnp.concatenate(parts, axis=0)).astype(BF16)


def lanes(rows, *lead, pairs=SUB):
    shape = tuple(lead) + (rows, PAIR * pairs)
    zeros = (0,) * (len(shape) - 1)
    return pl.BlockSpec(shape, lambda p: zeros + (p,))


def per_pair(*shape):
    zeros = (0,) * len(shape)
    return pl.BlockSpec((SUB,) + shape, lambda p: (p,) + zeros)


def interleaved(parts):
    live = list(parts)
    while live:
        for part in list(live):
            try:
                next(part)
            except StopIteration:
                live.remove(part)


def lane_view(ref, s):
    return ref.at[..., s * PAIR : (s + 1) * PAIR]


def scalars():
    return pl.BlockSpec(memory_space=pltpu.SMEM)


def shape_of(*shape, dtype=BF16):
    return jax.ShapeDtypeStruct(shape, dtype)


def call(kernel, steps, in_specs, out_specs, out_shape, scratch, cost, name):
    return pl.pallas_call(
        kernel,
        grid=(steps,),
        in_specs=in_specs,
        out_specs=out_specs,
        out_shape=out_shape,
        scratch_shapes=scratch,
        compiler_params=pltpu.CompilerParams(
            vmem_limit_bytes=48 * MIB, dimension_semantics=("arbitrary",)
        ),
        cost_estimate=pl.CostEstimate(flops=cost, bytes_accessed=cost // 300, transcendentals=0),
        name=name,
    )


def permute(block, route):
    return lax.ppermute(block, "ctx", route)


def shifted(block, distance):
    n = lax.axis_size("ctx")
    return permute(block, [(i, i + distance) for i in range(n) if 0 <= i + distance < n])


def crossed(block, span):
    n = lax.axis_size("ctx")
    route = []
    for i in range(n):
        to = i + 3 * span if i // span % 2 == 0 else i - 3 * span
        if 0 <= to < n:
            route.append((i, to))
    return permute(block, route)


def ring_groups():
    n = lax.axis_size("ctx")
    return [list(range(i, i + RING)) for i in range(0, n, RING)]


def total_over_devices(x):
    count = lax.axis_size("dp") * lax.axis_size("ctx")

    def from_device(x, mask):
        return lax.ppermute(x, ("dp", "ctx"), [(i, i ^ mask) for i in range(count)])

    bits = [1 << i for i in range(count.bit_length() - 1)]
    bits = bits[3:] + bits[:3]
    for a, b in zip(bits[::2], bits[1::2]):
        x = (x + from_device(x, a)) + (from_device(x, b) + from_device(x, a | b))
    return x


def body(queries, key_rows, values, grad_out, level_bias):
    width = queries.shape[2]
    pairs = width // PAIR
    n = lax.axis_size("ctx")
    me = lax.axis_index("ctx")

    def bias_of(flags):
        return jnp.where(jnp.stack(flags), 0.0, NEGATIVE).astype(F32)

    half = me % RING // 2
    is_first = half < 2
    has_prev, has_next = me >= RING, me < n - RING
    near_ring, far_ring = jnp.where(is_first, has_prev, has_next), jnp.where(is_first, has_next, has_prev)
    edge_bias = bias_of([
        me > 0, me < n - 1, me >= 2, me + 2 < n, jnp.where(me % 2 == 0, me + 3 < n, me >= 3)
    ])
    far_bias = jnp.stack([
        bias_of([half != 1, half != 2, near_ring & (half != 3), near_ring & (half != 0)]),
        bias_of([has_prev, has_next, far_ring, far_ring]),
    ])
    flag = is_first.astype(jnp.int32)[None]

    send_right, send_left, l3, l4, kv_coarse = call(
        prep_kernel, pairs // 4,
        [lanes(512, 1, pairs=4)] * 2,
        [lanes(r, 2, pairs=4) for r in (256, 256, 64, 32, 384)],
        [shape_of(2, r, width) for r in (256, 256, 64, 32, 384)],
        [], 400_000_000, "prep",
    )(key_rows, values)

    ring = lax.all_gather(l4, "ctx", axis=1, tiled=True, axis_index_groups=ring_groups())
    near_left = shifted(send_right, 1)
    near_right = shifted(send_left, -1)
    third = [shifted(l3, 2), shifted(l3, -2), crossed(l3, 1)]

    to_next, to_prev, opposite = call(
        pack_kernel, pairs // 4,
        [scalars(), lanes(256, 2, pairs=4)],
        [lanes(r, 2, pairs=4) for r in (192, 192, 128)],
        [shape_of(2, r, width) for r in (192, 192, 128)],
        [], 400_000_000, "pack",
    )(flag, ring)
    from_prev = shifted(to_next, RING)
    from_next = shifted(to_prev, -RING)

    q_coarse = call(
        query_kernel, pairs // 4,
        [lanes(512, 1, pairs=4)], [lanes(496, pairs=4)], [shape_of(496, width)],
        [], 400_000_000, "queries",
    )(queries)[0]

    spreads = [pltpu.VMEM((r, 512), BF16) for r in (512, 256)]
    key_sets = [pltpu.VMEM((SUB, r, PAIR), BF16) for r in (768, 512, 384)]
    turned = [pltpu.VMEM((SUB, PAIR, r), BF16) for r in (768, 512, 384)]
    sums = [pltpu.VMEM((SUB, r, PAIR), F32) for r in (768, 512, 384)]

    stats, numer, halo = call(
        near_forward_kernel, pairs // SUB,
        [scalars(), scalars(), lanes(512, 1), lanes(496), lanes(512, 1), lanes(512, 1), lanes(384, 2)]
        + [lanes(256, 2)] * 2,
        [per_pair(16, 512), per_pair(PAIR, 512), lanes(256, 2)],
        [
            shape_of(pairs, 16, 512, dtype=F32), shape_of(pairs, PAIR, 512, dtype=F32), shape_of(2, 256, width)
        ],
        spreads + key_sets + turned, 30_000_000_000, "near_forward",
    )(level_bias, edge_bias, queries, q_coarse, key_rows, values, kv_coarse, near_left, near_right)

    attended, stats2, dq_far, d_ring, d1, d2, d3, bias_far = call(
        far_kernel, pairs // SUB,
        [scalars()] * 4 + [lanes(496), lanes(512, 1), per_pair(16, 512), per_pair(PAIR, 512)]
        + [lanes(r, 2) for r in (64, 64, 64, 128, 192, 192)],
        [lanes(512, 1), per_pair(8, 512), per_pair(PAIR, 512), lanes(RING * SHARE, 2)]
        + [lanes(64, 2)] * 3 + [per_pair(8, 128)],
        [
            shape_of(1, 512, width),
            shape_of(pairs, 8, 512, dtype=F32),
            shape_of(pairs, PAIR, 512, dtype=F32),
            shape_of(2, RING * SHARE, width),
        ] + [shape_of(2, 64, width)] * 3 + [shape_of(pairs, 8, 128, dtype=F32)],
        [pltpu.VMEM((r, 512), BF16) for r in (128, 64, 32)], 20_000_000_000, "far",
    )(
        level_bias, edge_bias, far_bias, flag, q_coarse, grad_out, stats, numer,
        *third, opposite, from_next, from_prev,
    )
    back = [shifted(d1, -2), shifted(d2, 2), crossed(d3, 1)]

    d_share = lax.psum_scatter(d_ring, "ctx", scatter_dimension=1, tiled=True, axis_index_groups=ring_groups())

    grad_qt, own_part, to_left, to_right, bias_near = call(
        near_backward_kernel, pairs // SUB,
        [scalars(), lanes(512, 1), lanes(496), lanes(512, 1), lanes(512, 1), lanes(384, 2), lanes(512, 1)]
        + [lanes(256, 2)] * 3
        + [per_pair(16, 512), per_pair(8, 512), per_pair(PAIR, 512)],
        [per_pair(PAIR, 512), lanes(512, 2)] + [lanes(256, 2)] * 2 + [per_pair(8, 128)],
        [shape_of(pairs, PAIR, 512, dtype=F32), shape_of(2, 512, width, dtype=F32)]
        + [shape_of(2, 256, width)] * 2 + [shape_of(pairs, 8, 128, dtype=F32)],
        spreads + key_sets + key_sets + turned + sums + sums, 30_000_000_000, "near_backward",
    )(
        edge_bias, queries, q_coarse, key_rows, values, kv_coarse, grad_out,
        near_left, near_right, halo, stats, stats2, dq_far,
    )

    back_right, back_left = shifted(to_right, 1), shifted(to_left, -1)

    grad_q, own, bias = call(
        own_backward_kernel, pairs // SUB,
        [lanes(512, 1)] * 4 + [per_pair(16, 512), per_pair(8, 512), per_pair(PAIR, 512), lanes(512, 2)]
        + [lanes(64, 2)] * 3 + [per_pair(8, 128)] * 2,
        [lanes(512, 1), lanes(512, 2), per_pair(8, 128)],
        [shape_of(1, 512, width), shape_of(2, 512, width, dtype=F32), shape_of(pairs, 8, 128, dtype=F32)],
        [], 15_000_000_000, "own_backward",
    )(queries, key_rows, values, grad_out, stats, stats2, grad_qt, own_part, *back, bias_far, bias_near)

    share_next, share_prev = call(
        unshare_kernel, pairs // 4,
        [scalars(), lanes(SHARE, 2, pairs=4)],
        [lanes(32, 2, pairs=4)] * 2,
        [shape_of(2, 32, width)] * 2,
        [], 400_000_000, "unshare",
    )(flag, d_share)
    back_next, back_prev = shifted(share_prev, -RING), shifted(share_next, RING)

    bias = jnp.transpose(bias[:, : LEVELS - 1, :2], (1, 0, 2)).reshape(LEVELS - 1, 2 * pairs)
    grad_bias = total_over_devices(bias) * (
        1.0 / math.sqrt(512 * n * lax.axis_size("dp"))
    )

    grad_k, grad_v = call(
        finish_kernel, pairs // 4,
        [lanes(r, 2, pairs=4) for r in (512, 256, 256, SHARE, 32, 32)],
        [lanes(512, 1, pairs=4)] * 2,
        [shape_of(1, 512, width)] * 2,
        [], 400_000_000, "finish",
    )(own, back_right, back_left, d_share, back_next, back_prev)
    return attended, grad_q, grad_k, grad_v, grad_bias


def solution(mesh):
    rows = P("dp", "ctx", None)
    return jax.shard_map(
        body,
        mesh=mesh,
        in_specs=(rows, rows, rows, rows, P()),
        out_specs=(rows, rows, rows, rows, P()),
        check_vma=False,
    )
```

```python
import math

import jax
import jax.numpy as jnp
from jax import lax
from jax.experimental import pallas as pl
from jax.experimental.pallas import tpu as pltpu
from jax.sharding import PartitionSpec as P

BLOCK = 128
HALF = 64
LEVELS = 6
PAIR = 128
NEGATIVE = -1e30
LN2 = math.log(2.0)
F32 = jnp.float32
BF16 = jnp.bfloat16
MIB = 1 << 20
RING = 8
SHARE = 80
SUB = 2


def dot_nn(a, b):
    return lax.dot_general(a, b, (((1,), (0,)), ((), ())), preferred_element_type=F32)


def dot_nt(a, b):
    return lax.dot_general(a, b, (((1,), (1,)), ((), ())), preferred_element_type=F32)


def iota(shape, dim):
    return lax.broadcasted_iota(jnp.int32, shape, dim)


def halving(n):
    return jnp.where(iota((n // 2, n), 1) // 2 == iota((n // 2, n), 0), 0.5, 0.0).astype(BF16)


def doubling(n, factor):
    return (iota((n * factor, n), 0) // factor == iota((n * factor, n), 1)).astype(BF16)


def coarsen(x):
    rows = x.shape[0]
    step = min(rows, BLOCK)
    mean = halving(step)
    parts = [dot_nn(mean, x[i : i + step]).astype(BF16) for i in range(0, rows, step)]
    return parts[0] if len(parts) == 1 else jnp.concatenate(parts, axis=0)


def uncoarsen(x):
    rows = x.shape[0]
    step = min(rows, HALF)
    up = doubling(step, 2)
    half = (x * 0.5).astype(BF16)
    parts = [dot_nn(up, half[i : i + step]) for i in range(0, rows, step)]
    return parts[0] if len(parts) == 1 else jnp.concatenate(parts, axis=0)


def two_heads(x):
    low = iota(x.shape, 1) < HALF
    zero = jnp.zeros_like(x)
    return jnp.concatenate([jnp.where(low, x, zero), jnp.where(low, zero, x)], axis=0)


def own_head(x, span):
    same = (iota(x.shape, 0) < HALF) == (iota(x.shape, 1) // span % 2 == 0)
    return jnp.where(same, x, 0.0)


def spreader(level):
    rows = 512 >> level
    span = min(rows, HALF)
    shape = (2 * rows, 512)
    c = iota(shape, 0)
    row = c // (2 * span) * span + c % span
    return (iota(shape, 1) // 2**level == row).astype(BF16)


def split3(x):
    high = x.astype(BF16).astype(F32)
    rest = x - high
    mid = rest.astype(BF16).astype(F32)
    return high, mid, rest - mid


def stacked(rows, height):
    shape = (height, rows[0].shape[1])
    which = iota(shape, 0)
    out = jnp.zeros(shape, F32)
    for i, row in enumerate(rows):
        out = jnp.where(which == i, row, out)
    return out


def by_head(top, bottom, x):
    return jnp.concatenate([x[:HALF] * top, x[HALF:] * bottom], axis=0)


def spread_stats(rows, span, spread):
    flat = []
    for row in rows:
        first = iota(row.shape, 1) // span % 2 == 0
        for part in split3(row):
            flat.append(jnp.where(first, part, 0.0))
        for part in split3(row):
            flat.append(jnp.where(first, 0.0, part))
    wide = dot_nn(stacked(flat, 16).astype(BF16), spread)
    out = []
    for i in range(2 * len(rows)):
        out.append(wide[3 * i : 3 * i + 1] + wide[3 * i + 1 : 3 * i + 2] + wide[3 * i + 2 : 3 * i + 3])
    return out


def offset_row(low, high, span, shape):
    return jnp.where(iota(shape, 1) // span % 2 == 0, low, high)


def softmax_of(scores):
    top = jnp.max(scores, axis=0, keepdims=True)
    weights = jnp.exp(scores - top)
    return top, weights, jnp.sum(weights, axis=0, keepdims=True)


def with_bias(scores, biases):
    parts = []
    at = 0
    for lo, hi, bias in biases:
        if lo > at:
            parts.append(scores[at:lo])
        parts.append(scores[lo:hi] + bias)
        at = hi
    if at < scores.shape[0]:
        parts.append(scores[at:])
    return jnp.concatenate(parts, axis=0)


def halo_coarse(left, right):
    left1, right1 = coarsen(left[:128]), coarsen(right[:128])
    left2 = coarsen(jnp.concatenate([left[128:192], left1], axis=0))
    right2 = coarsen(jnp.concatenate([right1, right[128:192]], axis=0))
    return jnp.concatenate([left1, right1, left2, right2], axis=0)


def near_keys(own, coarse, left, right, halo):
    def joined(*parts):
        return jnp.concatenate(parts, axis=0)

    return (
        joined(left[:128], own, right[:128]),
        joined(left[128:192], halo[:64], coarse[:256], halo[64:128], right[128:192]),
        joined(left[192:256], halo[128:192], coarse[256:384], halo[192:256], right[192:256]),
    )


def window_parts(j):
    if j % 2 == 0:
        return (j, j + 4, j + 5)
    return (j - 1, j, j + 4)


def window_spans(j):
    a, b, c = window_parts(j)
    if b == a + 1:
        return [(a * HALF, (b + 1) * HALF), (c * HALF, (c + 1) * HALF)]
    return [(a * HALF, (a + 1) * HALF), (b * HALF, (c + 1) * HALF)]


def window_biases(j, halves, left_bias, right_bias):
    out = []
    for i, part in enumerate(window_parts(j)):
        if part < 2:
            out.append((i * HALF, (i + 1) * HALF, left_bias))
        elif part >= halves + 2:
            out.append((i * HALF, (i + 1) * HALF, right_bias))
    return out


def rows_of(ref, spans):
    if len(spans) == 1:
        return ref[spans[0][0] : spans[0][1], :]
    return jnp.concatenate([ref[lo:hi, :] for lo, hi in spans], axis=0)


def block_biases(b, left_bias, right_bias):
    if b == 0:
        return [(0, 128, left_bias)]
    if b == 3:
        return [(256, 384, right_bias)]
    return []


def prep_kernel(k_ref, v_ref, right_ref, left_ref, l3_ref, l4_ref, coarse_ref):
    for i, ref in enumerate((k_ref, v_ref)):
        zero = ref[0]
        one = coarsen(zero)
        two = coarsen(one)
        three = coarsen(two)
        right_ref[i, 0:128, :] = zero[384:512]
        right_ref[i, 128:192, :] = one[128:192]
        right_ref[i, 192:256, :] = two[0:64]
        left_ref[i, 0:128, :] = zero[0:128]
        left_ref[i, 128:192, :] = one[64:128]
        left_ref[i, 192:256, :] = two[64:128]
        l3_ref[i] = three
        l4_ref[i] = coarsen(three)
        coarse_ref[i, 0:256, :] = one
        coarse_ref[i, 256:384, :] = two


def query_kernel(q_ref, out_ref):
    rows = q_ref[0] * jnp.asarray(0.125, BF16)
    at = 0
    for level in range(1, LEVELS):
        rows = coarsen(rows)
        out_ref[at : at + (512 >> level), :] = rows
        at += 512 >> level


def pack_kernel(flag_ref, ring_ref, _, __, ___, next_ref, prev_ref, opposite_ref):
    first = flag_ref[0] > 0
    for i in range(2):
        four = ring_ref[i]
        five = coarsen(four)
        next_ref[i, 0:128, :] = jnp.where(first, four[128:256], five)
        next_ref[i, 128:192, :] = five[0:64]
        prev_ref[i, 0:128, :] = jnp.where(first, five, four[0:128])
        prev_ref[i, 128:192, :] = five[64:128]
        opposite_ref[i] = jnp.where(first, four[128:256], four[0:128])


def unshare_kernel(flag_ref, sum_ref, next_ref, prev_ref):
    first = flag_ref[0] > 0
    for i in range(2):
        four = sum_ref[i, 32:64, :]
        five = uncoarsen(sum_ref[i, 64:80, :].astype(F32)).astype(BF16)
        next_ref[i] = jnp.where(first, four, five)
        prev_ref[i] = jnp.where(first, five, four)


def block_forward(b, keys, values_t, q0, left_bias, right_bias):
    scores = dot_nt(keys, two_heads(q0[b * 128 : b * 128 + 128]))
    scores = with_bias(scores, block_biases(b, left_bias, right_bias))
    top, weights, total = softmax_of(scores)
    mixed = dot_nn(values_t, weights.astype(BF16))
    return top, total, jnp.concatenate([mixed[:HALF, :128], mixed[HALF:, 128:]], axis=0)


def inner_forward_kernel(q_ref, k_ref, v_ref, l3_ref, st_ref, mix_ref, third_ref):
    third_ref[...] = l3_ref[...]

    def one(s):
        q0 = lane_view(q_ref, s)[0] * jnp.asarray(0.125, BF16)
        keys, values_t = lane_view(k_ref, s)[0], lane_view(v_ref, s)[0].T
        yield
        for i in range(2):
            span = slice(i * 128, i * 128 + 384)
            top, total, mixed = block_forward(1 + i, keys[span], values_t[:, span], q0, None, None)
            st_ref[s, 0:1, i * 256 : i * 256 + 256] = top
            st_ref[s, 1:2, i * 256 : i * 256 + 256] = total
            mix_ref[s, :, i * 128 : i * 128 + 128] = mixed
            yield

    interleaved(one(s) for s in range(SUB))


def near_forward_kernel(
    off_ref, edge_ref, q_ref, qc_ref, k_ref, v_ref, kvc_ref, nl_ref, nr_ref, ist_ref, imix_ref,
    st_ref, nt_ref, halo_ref, e1, e2, *scratch,
):
    step = pl.program_id(0)

    @pl.when(step == 0)
    def _():
        e1[...] = spreader(1)
        e2[...] = spreader(2)

    interleaved(
        near_forward_pair(
            step * SUB + s, off_ref, edge_ref, *[lane_view(r, s) for r in (q_ref, qc_ref, k_ref, v_ref, kvc_ref, nl_ref, nr_ref)],
            *[r.at[s : s + 1] for r in (ist_ref, imix_ref, st_ref, nt_ref)], lane_view(halo_ref, s), e1, e2, *[r.at[s] for r in scratch],
        )
        for s in range(SUB)
    )


def near_forward_pair(
    pair, off_ref, edge_ref, q_ref, qc_ref, k_ref, v_ref, kvc_ref, nl_ref, nr_ref, ist_ref, imix_ref,
    st_ref, nt_ref, halo_ref,
    e1, e2, k0s, k1s, k2s, vt0, vt1, vt2,
):
    left_bias, right_bias = edge_ref[0], edge_ref[1]
    q0 = q_ref[0] * jnp.asarray(0.125, BF16)
    q1, q2 = qc_ref[0:256], qc_ref[256:384]
    halos = [halo_coarse(nl_ref[i], nr_ref[i]) for i in range(2)]
    for i in range(2):
        halo_ref[i] = halos[i]
    for dst, x in zip((k0s, k1s, k2s), near_keys(k_ref[0], kvc_ref[0], nl_ref[0], nr_ref[0], halos[0])):
        dst[...] = x
    for dst, x in zip((vt0, vt1, vt2), near_keys(v_ref[0], kvc_ref[1], nl_ref[1], nr_ref[1], halos[1])):
        dst[...] = x.T
    yield

    blocks = {}
    for b in (0, 3):
        span = slice(b * 128, b * 128 + 384)
        blocks[b] = block_forward(b, k0s[span, :], vt0[:, span], q0, left_bias, right_bias)
        yield
    for i in range(2):
        at = slice(i * 256, i * 256 + 256)
        blocks[1 + i] = ist_ref[0, 0:1, at], ist_ref[0, 1:2, at], imix_ref[0, :, i * 128 : i * 128 + 128]
    tops, totals, mixes = zip(*[blocks[b] for b in range(4)])
    top_a = jnp.concatenate([t[:, :128] for t in tops], axis=1)
    top_b = jnp.concatenate([t[:, 128:] for t in tops], axis=1)
    total_a = jnp.concatenate([t[:, :128] for t in totals], axis=1)
    total_b = jnp.concatenate([t[:, 128:] for t in totals], axis=1)
    st_ref[0, 0:1, :] = top_a
    st_ref[0, 1:2, :] = top_b
    mixed0 = jnp.concatenate(mixes, axis=1)

    coarse = []
    for level, keys_ref, vt_ref, queries, spread in (
        (1, k1s, vt1, q1, e1), (2, k2s, vt2, q2, e2),
    ):
        halves = 8 >> level
        tops, totals, mixes = [], [], []
        for j in range(halves):
            spans = window_spans(j)
            scores = dot_nt(rows_of(keys_ref, spans), two_heads(queries[j * HALF : (j + 1) * HALF]))
            scores = with_bias(scores, window_biases(j, halves, left_bias, right_bias))
            top, weights, total = softmax_of(scores)
            vt = jnp.concatenate([vt_ref[:, lo:hi] for lo, hi in spans], axis=1)
            mixes.append(own_head(dot_nn(vt, weights.astype(BF16)), HALF).astype(BF16))
            tops.append(top)
            totals.append(total)
            yield
        top = jnp.concatenate(tops, axis=1)
        total = jnp.concatenate(totals, axis=1)
        st_ref[0, 1 + level : 2 + level, 0 : top.shape[1]] = top
        low = off_ref[level - 1, 2 * pair] + level * LN2
        high = off_ref[level - 1, 2 * pair + 1] + level * LN2
        top = top + offset_row(low, high, HALF, top.shape)
        wide = spread_stats([top, total], HALF, spread[...])
        mixed = dot_nn(jnp.concatenate(mixes, axis=1), spread[...])
        st_ref[0, 7 + 2 * level : 8 + 2 * level, :] = wide[0]
        st_ref[0, 8 + 2 * level : 9 + 2 * level, :] = wide[1]
        coarse.append((wide, mixed))
        yield

    peaks, denoms, factors = [], [], []
    for h, (top0, total0) in enumerate(((top_a, total_a), (top_b, total_b))):
        peak = top0
        for wide, _ in coarse:
            peak = jnp.maximum(peak, wide[h])
        f = [jnp.exp(top0 - peak)] + [jnp.exp(wide[h] - peak) for wide, _ in coarse]
        denom = f[0] * total0
        for i, (wide, _) in enumerate(coarse):
            denom = denom + f[i + 1] * wide[2 + h]
        peaks.append(peak)
        denoms.append(denom)
        factors.append(f)
    numer = by_head(factors[0][0], factors[1][0], mixed0)
    for i, (_, mixed) in enumerate(coarse):
        numer = numer + by_head(factors[0][i + 1], factors[1][i + 1], mixed)
    st_ref[0, 5:6, :] = peaks[0]
    st_ref[0, 6:7, :] = peaks[1]
    st_ref[0, 7:8, :] = denoms[0]
    st_ref[0, 8:9, :] = denoms[1]
    nt_ref[0] = numer


def far_kernel(
    off_ref, edge_ref, far_ref, flag_ref, qc_ref, g_ref, st_ref, nt_ref,
    opposite_ref, next_ref, prev_ref, f1_ref, f2_ref, f3_ref,
    att_ref, st2_ref, dq_ref, dring_ref, d1_ref, d2_ref, d3_ref, bias_ref, e3, e4, e5,
):
    step = pl.program_id(0)

    @pl.when(step == 0)
    def _():
        e3[...] = spreader(3)
        e4[...] = spreader(4)
        e5[...] = spreader(5)

    def one(s):
        windows = [lane_view(r, s) for r in (f1_ref, f2_ref, f3_ref, opposite_ref, next_ref, prev_ref)]
        grads = [lane_view(r, s) for r in (dring_ref, d1_ref, d2_ref, d3_ref)]
        return far_pair(
            step * SUB + s, off_ref, edge_ref, far_ref, flag_ref[0] > 0, lane_view(qc_ref, s), lane_view(g_ref, s),
            *[r.at[s : s + 1] for r in (st_ref, nt_ref)], *windows,
            lane_view(att_ref, s), *[r.at[s : s + 1] for r in (st2_ref, dq_ref)],
            *grads, bias_ref.at[s : s + 1], (e3, e4, e5),
        )

    interleaved(one(s) for s in range(SUB))


def far_pair(
    pair, off_ref, edge_ref, far_ref, first, qc_ref, g_ref, st_ref, nt_ref,
    f1_ref, f2_ref, f3_ref, opposite_ref, next_ref, prev_ref,
    att_ref, st2_ref, dq_ref, dring_ref, d1_ref, d2_ref, d3_ref, bias_ref, spreads,
):
    lower, upper = range(RING // 2), range(RING // 2, RING)
    coarse_q = {3: qc_ref[384:448], 4: qc_ref[448:480], 5: qc_ref[480:496]}
    gt = g_ref[0].T.astype(F32)
    windows = {3: [], 4: [], 5: []}
    for i in range(2):
        after, before = next_ref[i], prev_ref[i]
        windows[3].append(jnp.concatenate([f1_ref[i], f2_ref[i], f3_ref[i]], axis=0))
        near = jnp.where(first, before[0:128], after[0:128])
        windows[4].append(jnp.concatenate([opposite_ref[i], near], axis=0))
        windows[5].append(jnp.concatenate([
            jnp.where(first, before[128:192], before[0:64]),
            jnp.where(first, after[64:128], after[128:192]),
            jnp.where(first, after[0:64], before[64:128]),
        ], axis=0))
    levels = []
    for level, spread in zip((3, 4, 5), spreads):
        span = 512 >> level
        queries = two_heads(coarse_q[level])
        keys, values = windows[level]
        scores = dot_nt(keys, queries)
        parts = keys.shape[0] // HALF
        biases = [
            (i * HALF, (i + 1) * HALF, edge_ref[2 + i] if level == 3 else far_ref[level - 4, i]) for i in range(parts)
        ]
        top, weights, total = softmax_of(with_bias(scores, biases))
        mixed = own_head(dot_nn(values.T, weights.astype(BF16)), span).astype(BF16)
        low = off_ref[level - 1, 2 * pair] + level * LN2
        high = off_ref[level - 1, 2 * pair + 1] + level * LN2
        top = top + offset_row(low, high, span, top.shape)
        wide = spread_stats([top, total], span, spread[...])
        levels.append((level, span, queries, weights, wide, dot_nn(mixed, spread[...]), spread))
        yield

    logs, inners, numers = [], [], []
    for h in range(2):
        peak0, denom0 = st_ref[0, 5 + h : 6 + h, :], st_ref[0, 7 + h : 8 + h, :]
        peak = peak0
        for item in levels:
            peak = jnp.maximum(peak, item[4][h])
        keep = jnp.exp(peak0 - peak)
        denom = keep * denom0
        numer = keep * nt_ref[0, h * HALF : (h + 1) * HALF, :]
        for item in levels:
            f = jnp.exp(item[4][h] - peak)
            denom = denom + f * item[4][2 + h]
            numer = numer + f * item[5][h * HALF : (h + 1) * HALF]
        out = (numer / denom).astype(BF16)
        numers.append(out)
        logs.append(peak + jnp.log(denom))
        inners.append(
            jnp.sum(gt[h * HALF : (h + 1) * HALF] * out.astype(F32), axis=0, keepdims=True)
        )
    att_ref[0] = jnp.concatenate(numers, axis=0).T
    st2_ref[0] = stacked([logs[0], logs[1], inners[0], inners[1]], 8)
    yield

    dqt = jnp.zeros((PAIR, 512), F32)
    sums = jnp.zeros((8, 128), F32)
    grads = {}
    for level, span, queries, weights, wide, _, spread in levels:
        dq, bias, dk, dv = level_back(
            weights, *windows[level], queries, gt, wide[:2], logs, inners, span, spread
        )
        grads[level] = (dk.astype(BF16), dv.astype(BF16))
        last = (dk[128:192], dv[128:192])
        dqt = dqt + dq * (0.125 / 2**level)
        sums = place(sums, level, bias, span)
        yield
    for i in range(2):
        for n, ref in enumerate((d1_ref, d2_ref, d3_ref)):
            ref[i] = grads[3][i][n * HALF : (n + 1) * HALF]
        four, five = grads[4][i], grads[5][i]
        blank = jnp.zeros((128, PAIR), BF16)
        far = uncoarsen(last[i]).astype(BF16)
        for part, on_low in ((lower, True), (upper, False)):
            here = jnp.logical_not(first) if on_low else first
            own = jnp.where(here, four[0:128], blank)
            foreign = jnp.where(here, four[128:256], far)
            for n, z in enumerate(part):
                at = SHARE * z
                dring_ref[i, at : at + 32, :] = own[32 * n : 32 * n + 32]
                dring_ref[i, at + 32 : at + 64, :] = foreign[32 * n : 32 * n + 32]
                dring_ref[i, at + 64 : at + 80, :] = five[16 * z : 16 * z + 16]
    dq_ref[0] = dqt
    bias_ref[0] = sums


def place(sums, level, bias, span):
    first = iota(bias.shape, 1) // span % 2 == 0
    low = jnp.sum(jnp.where(first, bias, 0.0), axis=1, keepdims=True)
    high = jnp.sum(jnp.where(first, 0.0, bias), axis=1, keepdims=True)
    here = iota(sums.shape, 0) == level - 1
    lane = iota(sums.shape, 1)
    sums = jnp.where(here & (lane == 0), low, sums)
    return jnp.where(here & (lane == 1), high, sums)


def grad_rows(gt, tops, logs, inners, span, spread):
    f = [jnp.exp(tops[h] - logs[h]) for h in range(2)]
    g = dot_nt(spread[...], by_head(f[0], f[1], gt).astype(BF16))
    mine = (iota(g.shape, 1) < HALF) == (iota(g.shape, 0) // span % 2 == 0)
    g = jnp.where(mine, g, 0.0).astype(BF16)
    flat = [part for h in range(2) for part in split3(f[h] * inners[h])]
    wide = dot_nt(stacked(flat, 16).astype(BF16), spread[...])
    low = wide[0:1] + wide[1:2] + wide[2:3]
    high = wide[3:4] + wide[4:5] + wide[5:6]
    corr = jnp.where(iota(low.shape, 1) // span % 2 == 0, low, high)
    return g, corr


def window_back(weights, values, queries, g, corr):
    dots = dot_nt(values, g)
    grad = weights * (dots - corr)
    short = grad.astype(BF16)
    return short, dot_nn(short, queries), dot_nn(weights.astype(BF16), g), grad


def level_back(weights, keys, values, queries, gt, tops, logs, inners, span, spread):
    g, corr = grad_rows(gt, tops, logs, inners, span, spread)
    short, dk, dv, grad = window_back(weights, values, queries, g, corr)
    dq = own_head(dot_nn(keys.T, short), span).astype(BF16)
    return dot_nn(dq, spread[...]), jnp.sum(grad, axis=0, keepdims=True), dk, dv


def near_backward_kernel(
    edge_ref, q_ref, qc_ref, k_ref, v_ref, kvc_ref, g_ref, nl_ref, nr_ref, halo_ref,
    st_ref, st2_ref, dqf_ref,
    dq_ref, own_ref, gl_ref, gr_ref, bias_ref,
    e1, e2, *scratch,
):
    step = pl.program_id(0)

    @pl.when(step == 0)
    def _():
        e1[...] = spreader(1)
        e2[...] = spreader(2)

    def one(s):
        wide = [lane_view(r, s) for r in (q_ref, qc_ref, k_ref, v_ref, kvc_ref, g_ref, nl_ref, nr_ref, halo_ref)]
        per = [r.at[s : s + 1] for r in (st_ref, st2_ref, dqf_ref, dq_ref)]
        out = [lane_view(r, s) for r in (own_ref, gl_ref, gr_ref)]
        return near_backward_pair(
            edge_ref, *wide, *per, *out, bias_ref.at[s : s + 1], e1, e2, *[r.at[s] for r in scratch]
        )

    interleaved(one(s) for s in range(SUB))


def near_backward_pair(
    edge_ref, q_ref, qc_ref, k_ref, v_ref, kvc_ref, g_ref, nl_ref, nr_ref, halo_ref, st_ref, st2_ref, dqf_ref,
    dq_ref, own_ref, gl_ref, gr_ref, bias_ref,
    e1, e2, k0s, k1s, k2s, v0s, v1s, v2s, kt0, kt1, kt2,
    dk0, dk1, dk2, dv0, dv1, dv2,
):
    left_bias, right_bias = edge_ref[0], edge_ref[1]
    q0 = q_ref[0] * jnp.asarray(0.125, BF16)
    q1, q2 = qc_ref[0:256], qc_ref[256:384]
    keys = near_keys(k_ref[0], kvc_ref[0], nl_ref[0], nr_ref[0], halo_ref[0])
    for dst, tdst, x in zip((k0s, k1s, k2s), (kt0, kt1, kt2), keys):
        dst[...] = x
        tdst[...] = x.T
    for dst, x in zip((v0s, v1s, v2s), near_keys(v_ref[0], kvc_ref[1], nl_ref[1], nr_ref[1], halo_ref[1])):
        dst[...] = x
    for ref in (dk0, dk1, dk2, dv0, dv1, dv2):
        ref[...] = jnp.zeros(ref.shape, F32)

    yield
    gt = g_ref[0].T.astype(F32)
    logs = [st2_ref[0, 0:1, :], st2_ref[0, 1:2, :]]
    inners = [st2_ref[0, 2:3, :], st2_ref[0, 3:4, :]]
    dqt = dqf_ref[0]
    sums = jnp.zeros((8, 128), F32)

    for level, ks, vs, kt, dk, dv, queries, spread in (
        (1, k1s, v1s, kt1, dk1, dv1, q1, e1),
        (2, k2s, v2s, kt2, dk2, dv2, q2, e2),
    ):
        halves = 8 >> level
        tops = [st_ref[0, 7 + 2 * level + h : 8 + 2 * level + h, :] for h in range(2)]
        g, corr = grad_rows(gt, tops, logs, inners, HALF, spread)
        dqs = []
        bias = jnp.zeros((1, 128), F32)
        for j in range(halves):
            spans = window_spans(j)
            at = slice(j * 128, (j + 1) * 128)
            queries_j = two_heads(queries[j * HALF : (j + 1) * HALF])
            scores = dot_nt(rows_of(ks, spans), queries_j)
            scores = with_bias(scores, window_biases(j, halves, left_bias, right_bias))
            weights = jnp.exp(scores - st_ref[0, 1 + level : 2 + level, at])
            short, dk_j, dv_j, grad = window_back(weights, rows_of(vs, spans), queries_j, g[at], corr[:, at])
            bias = bias + jnp.sum(grad, axis=0, keepdims=True)
            base = 0
            for lo, hi in spans:
                dk[lo:hi, :] += dk_j[base : base + hi - lo]
                dv[lo:hi, :] += dv_j[base : base + hi - lo]
                base += hi - lo
            kt_j = jnp.concatenate([kt[:, lo:hi] for lo, hi in spans], axis=1)
            dqs.append(own_head(dot_nn(kt_j, short), HALF).astype(BF16))
            yield
        dqt = dqt + dot_nn(jnp.concatenate(dqs, axis=1), spread[...]) * (0.125 / 2**level)
        sums = place(sums, level, bias, HALF)
    bias_ref[0] = sums

    g0, corr0 = zero_rows(gt, st_ref, logs, inners)
    dq0 = {}
    for b in (0, 3):
        span = slice(b * 128, b * 128 + 384)
        dq0[b], dk_b, dv_b = block_back(
            b, k0s[span, :], v0s[span, :], kt0[:, span], q0, g0, corr0, st_ref, left_bias, right_bias
        )
        dk0[span, :] += dk_b
        dv0[span, :] += dv_b
        yield
    blank = jnp.zeros((PAIR, 256), F32)
    dq_ref[0] = dqt + jnp.concatenate([dq0[0], blank, dq0[3]], axis=1)

    for i, (zero, one, two) in enumerate(((dk0, dk1, dk2), (dv0, dv1, dv2))):
        left1 = one[0:128, :] + uncoarsen(two[64:128, :])
        left0 = zero[0:128, :] + uncoarsen(left1[64:128])
        gl_ref[i, 0:128, :] = left0.astype(BF16)
        gl_ref[i, 128:192, :] = left1[0:64].astype(BF16)
        gl_ref[i, 192:256, :] = two[0:64, :].astype(BF16)
        right1 = one[384:512, :] + uncoarsen(two[256:320, :])
        right0 = zero[640:768, :] + uncoarsen(right1[0:64])
        gr_ref[i, 0:128, :] = right0.astype(BF16)
        gr_ref[i, 128:192, :] = right1[64:128].astype(BF16)
        gr_ref[i, 192:256, :] = two[320:384, :].astype(BF16)
        mine1 = one[128:384, :] + uncoarsen(two[128:256, :])
        own_ref[i] = zero[128:640, :] + uncoarsen(mine1)


def zero_rows(gt, st_ref, logs, inners):
    f0 = [jnp.exp(st_ref[0, h : h + 1, :] - logs[h]) for h in range(2)]
    g0 = by_head(f0[0], f0[1], gt).astype(BF16).T
    return g0, [f0[h] * inners[h] for h in range(2)]


def block_back(b, keys, values, keys_t, q0, g0, corr0, st_ref, left_bias, right_bias):
    at = slice(b * 128, (b + 1) * 128)
    queries = two_heads(q0[at])
    scores = with_bias(dot_nt(keys, queries), block_biases(b, left_bias, right_bias))
    top = jnp.concatenate([st_ref[0, 0:1, at], st_ref[0, 1:2, at]], axis=1)
    corr = jnp.concatenate([corr0[0][:, at], corr0[1][:, at]], axis=1)
    weights = jnp.exp(scores - top)
    short, dk, dv, _ = window_back(weights, values, queries, two_heads(g0[at]), corr)
    dq = dot_nn(keys_t, short)
    return jnp.concatenate([dq[:HALF, :128], dq[HALF:, 128:]], axis=0) * 0.125, dk, dv


def own_backward_kernel(
    q_ref, k_ref, v_ref, g_ref, st_ref, st2_ref, dqt_ref, own_in_ref, f1_ref, f2_ref, f3_ref, b1_ref, b2_ref,
    dq_ref, own_ref, bias_ref
):
    bias_ref[...] = b1_ref[...] + b2_ref[...]

    def one(s):
        wide = [lane_view(r, s) for r in (q_ref, k_ref, v_ref, g_ref)]
        per = [r.at[s : s + 1] for r in (st_ref, st2_ref, dqt_ref)]
        pieces = [lane_view(r, s) for r in (f1_ref, f2_ref, f3_ref)]
        return own_backward_pair(*wide, *per, pieces, *[lane_view(r, s) for r in (own_in_ref, dq_ref, own_ref)])

    interleaved(one(s) for s in range(SUB))


def own_backward_pair(
    q_ref, k_ref, v_ref, g_ref, st_ref, st2_ref, dqt_ref, pieces, own_in_ref, dq_ref, own_ref
):
    q0 = q_ref[0] * jnp.asarray(0.125, BF16)
    keys, values = k_ref[0], v_ref[0]
    keys_t = keys.T
    gt = g_ref[0].T.astype(F32)
    logs = [st2_ref[0, 0:1, :], st2_ref[0, 1:2, :]]
    inners = [st2_ref[0, 2:3, :], st2_ref[0, 3:4, :]]
    g0, corr0 = zero_rows(gt, st_ref, logs, inners)
    yield
    out = {}
    for b in (1, 2):
        span = slice((b - 1) * 128, (b + 2) * 128)
        out[b] = block_back(b, keys[span], values[span], keys_t[:, span], q0, g0, corr0, st_ref, None, None)
        yield
    dqt = dqt_ref[0]
    dqt = jnp.concatenate([dqt[:, :128], dqt[:, 128:256] + out[1][0], dqt[:, 256:384] + out[2][0], dqt[:, 384:]], axis=1)
    dq_ref[0] = dqt.astype(BF16).T
    for i in range(2):
        one, two = out[1][1 + i], out[2][1 + i]
        three = sum(ref[i].astype(F32) for ref in pieces) * 0.125
        far = dot_nn(doubling(HALF, 8), three.astype(BF16))
        own_ref[i, 0:128, :] = own_in_ref[i, 0:128, :] + far[0:128] + one[0:128]
        own_ref[i, 128:384, :] = own_in_ref[i, 128:384, :] + far[128:384] + one[128:384] + two[0:256]
        own_ref[i, 384:512, :] = own_in_ref[i, 384:512, :] + far[384:512] + two[256:384]


def finish_kernel(own_ref, left_ref, right_ref, sum_ref, next_ref, prev_ref, dk_ref, dv_ref):
    up2, up4, up16 = doubling(HALF, 2), doubling(HALF, 4), doubling(HALF // 2, 16)
    for i, out in enumerate((dk_ref, dv_ref)):
        four = sum_ref[i, 0:32, :].astype(F32) + next_ref[i].astype(F32) + prev_ref[i].astype(F32)
        far = dot_nn(up16, (four * 0.0625).astype(BF16))
        left1 = dot_nn(up2, left_ref[i, 128:192, :]) * 0.5
        left2 = dot_nn(up4, left_ref[i, 192:256, :]) * 0.25
        right1 = dot_nn(up2, right_ref[i, 128:192, :]) * 0.5
        right2 = dot_nn(up4, right_ref[i, 192:256, :]) * 0.25
        parts = [
            left_ref[i, 0:128, :].astype(F32) + right2[0:128],
            left1 + right2[128:256],
            left2[0:128] + right1,
            left2[128:256] + right_ref[i, 0:128, :].astype(F32),
        ]
        out[0] = (own_ref[i] + far + jnp.concatenate(parts, axis=0)).astype(BF16)


def lanes(rows, *lead, pairs=SUB):
    shape = tuple(lead) + (rows, PAIR * pairs)
    zeros = (0,) * (len(shape) - 1)
    return pl.BlockSpec(shape, lambda p: zeros + (p,))


def per_pair(*shape):
    zeros = (0,) * len(shape)
    return pl.BlockSpec((SUB,) + shape, lambda p: (p,) + zeros)


def interleaved(parts):
    live = list(parts)
    while live:
        for part in list(live):
            try:
                next(part)
            except StopIteration:
                live.remove(part)


def lane_view(ref, s):
    return ref.at[..., s * PAIR : (s + 1) * PAIR]


def scalars():
    return pl.BlockSpec(memory_space=pltpu.SMEM)


def shape_of(*shape, dtype=BF16):
    return jax.ShapeDtypeStruct(shape, dtype)


def call(kernel, steps, in_specs, out_specs, out_shape, scratch, cost, name, mib=48):
    return pl.pallas_call(
        kernel,
        grid=(steps,),
        in_specs=in_specs,
        out_specs=out_specs,
        out_shape=out_shape,
        scratch_shapes=scratch,
        compiler_params=pltpu.CompilerParams(
            vmem_limit_bytes=mib * MIB, dimension_semantics=("arbitrary",)
        ),
        cost_estimate=pl.CostEstimate(flops=cost, bytes_accessed=cost // 300, transcendentals=0),
        name=name,
    )


def permute(block, route):
    return lax.ppermute(block, "ctx", route)


def shifted(block, distance):
    n = lax.axis_size("ctx")
    return permute(block, [(i, i + distance) for i in range(n) if 0 <= i + distance < n])


def crossed(block, span):
    n = lax.axis_size("ctx")
    route = []
    for i in range(n):
        to = i + 3 * span if i // span % 2 == 0 else i - 3 * span
        if 0 <= to < n:
            route.append((i, to))
    return permute(block, route)


def ring_groups():
    n = lax.axis_size("ctx")
    return [list(range(i, i + RING)) for i in range(0, n, RING)]


def total_over(x, bits):
    count = lax.axis_size("dp") * lax.axis_size("ctx")

    def from_device(x, mask):
        return lax.ppermute(x, ("dp", "ctx"), [(i, i ^ mask) for i in range(count)])

    for at in range(0, len(bits), 2):
        a = 1 << bits[at]
        first = x + from_device(x, a)
        if at + 1 < len(bits):
            b = 1 << bits[at + 1]
            first = first + (from_device(x, b) + from_device(x, a | b))
        x = first
    return x


def body(queries, key_rows, values, grad_out, level_bias):
    width = queries.shape[2]
    pairs = width // PAIR
    n = lax.axis_size("ctx")
    me = lax.axis_index("ctx")

    def bias_of(flags):
        return jnp.where(jnp.stack(flags), 0.0, NEGATIVE).astype(F32)

    half = me % RING // 2
    is_first = half < 2
    has_prev, has_next = me >= RING, me < n - RING
    near_ring, far_ring = jnp.where(is_first, has_prev, has_next), jnp.where(is_first, has_next, has_prev)
    edge_bias = bias_of([
        me > 0, me < n - 1, me >= 2, me + 2 < n, jnp.where(me % 2 == 0, me + 3 < n, me >= 3)
    ])
    far_bias = jnp.stack([
        bias_of([half != 1, half != 2, near_ring & (half != 3), near_ring & (half != 0)]),
        bias_of([has_prev, has_next, far_ring, far_ring]),
    ])
    flag = is_first.astype(jnp.int32)[None]

    send_right, send_left, l3, l4, kv_coarse = call(
        prep_kernel, pairs // 4,
        [lanes(512, 1, pairs=4)] * 2,
        [lanes(r, 2, pairs=4) for r in (256, 256, 64, 32, 384)],
        [shape_of(2, r, width) for r in (256, 256, 64, 32, 384)],
        [], 400_000_000, "prep", 60,
    )(key_rows, values)

    ring = lax.all_gather(l4, "ctx", axis=1, tiled=True, axis_index_groups=ring_groups())
    near_left = shifted(send_right, 1)
    near_right = shifted(send_left, -1)
    inner_stats, inner_mixed, third_out = call(
        inner_forward_kernel, pairs // SUB,
        [lanes(512, 1)] * 3 + [lanes(64, 2)],
        [per_pair(8, 512), per_pair(PAIR, 256), lanes(64, 2)],
        [shape_of(pairs, 8, 512, dtype=F32), shape_of(pairs, PAIR, 256, dtype=F32), shape_of(2, 64, width)],
        [], 10_000_000_000, "inner_forward",
    )(queries, key_rows, values, l3)
    third = [shifted(third_out, 2), shifted(third_out, -2), crossed(third_out, 1)]

    to_next, to_prev, opposite = call(
        pack_kernel, pairs // 4,
        [scalars(), lanes(256, 2, pairs=4)]
        + [pl.BlockSpec(memory_space=pl.ANY)] * 3,
        [lanes(r, 2, pairs=4) for r in (192, 192, 128)],
        [shape_of(2, r, width) for r in (192, 192, 128)],
        [], 400_000_000, "pack",
    )(flag, ring, inner_stats, near_left, near_right)
    from_prev = shifted(to_next, RING)
    from_next = shifted(to_prev, -RING)

    q_coarse = call(
        query_kernel, pairs // 4,
        [lanes(512, 1, pairs=4)], [lanes(496, pairs=4)], [shape_of(496, width)],
        [], 400_000_000, "queries",
    )(queries)[0]

    spreads = [pltpu.VMEM((r, 512), BF16) for r in (512, 256)]
    key_sets = [pltpu.VMEM((SUB, r, PAIR), BF16) for r in (768, 512, 384)]
    turned = [pltpu.VMEM((SUB, PAIR, r), BF16) for r in (768, 512, 384)]
    sums = [pltpu.VMEM((SUB, r, PAIR), F32) for r in (768, 512, 384)]

    stats, numer, halo = call(
        near_forward_kernel, pairs // SUB,
        [scalars(), scalars(), lanes(512, 1), lanes(496), lanes(512, 1), lanes(512, 1), lanes(384, 2)]
        + [lanes(256, 2)] * 2 + [per_pair(8, 512), per_pair(PAIR, 256)],
        [per_pair(16, 512), per_pair(PAIR, 512), lanes(256, 2)],
        [
            shape_of(pairs, 16, 512, dtype=F32), shape_of(pairs, PAIR, 512, dtype=F32), shape_of(2, 256, width)
        ],
        spreads + key_sets + turned, 30_000_000_000, "near_forward",
    )(level_bias, edge_bias, queries, q_coarse, key_rows, values, kv_coarse, near_left, near_right, inner_stats, inner_mixed)

    attended, stats2, dq_far, d_ring, d1, d2, d3, bias_far = call(
        far_kernel, pairs // SUB,
        [scalars()] * 4 + [lanes(496), lanes(512, 1), per_pair(16, 512), per_pair(PAIR, 512)]
        + [lanes(r, 2) for r in (128, 192, 192, 64, 64, 64)],
        [lanes(512, 1), per_pair(8, 512), per_pair(PAIR, 512), lanes(RING * SHARE, 2)]
        + [lanes(64, 2)] * 3 + [per_pair(8, 128)],
        [
            shape_of(1, 512, width),
            shape_of(pairs, 8, 512, dtype=F32),
            shape_of(pairs, PAIR, 512, dtype=F32),
            shape_of(2, RING * SHARE, width),
        ] + [shape_of(2, 64, width)] * 3 + [shape_of(pairs, 8, 128, dtype=F32)],
        [pltpu.VMEM((r, 512), BF16) for r in (128, 64, 32)], 20_000_000_000, "far",
    )(
        level_bias, edge_bias, far_bias, flag, q_coarse, grad_out, stats, numer,
        opposite, from_next, from_prev, *third,
    )
    back = [shifted(d1, -2), shifted(d2, 2), crossed(d3, 1)]

    d_share = lax.psum_scatter(d_ring, "ctx", scatter_dimension=1, tiled=True, axis_index_groups=ring_groups())

    grad_qt, own_part, to_left, to_right, bias_near = call(
        near_backward_kernel, pairs // SUB,
        [scalars(), lanes(512, 1), lanes(496), lanes(512, 1), lanes(512, 1), lanes(384, 2), lanes(512, 1)]
        + [lanes(256, 2)] * 3
        + [per_pair(16, 512), per_pair(8, 512), per_pair(PAIR, 512)],
        [per_pair(PAIR, 512), lanes(512, 2)] + [lanes(256, 2)] * 2 + [per_pair(8, 128)],
        [shape_of(pairs, PAIR, 512, dtype=F32), shape_of(2, 512, width, dtype=F32)]
        + [shape_of(2, 256, width)] * 2 + [shape_of(pairs, 8, 128, dtype=F32)],
        spreads + key_sets + key_sets + turned + sums + sums, 30_000_000_000, "near_backward",
    )(
        edge_bias, queries, q_coarse, key_rows, values, kv_coarse, grad_out,
        near_left, near_right, halo, stats, stats2, dq_far,
    )

    back_right, back_left = shifted(to_right, 1), shifted(to_left, -1)

    grad_q, own, bias = call(
        own_backward_kernel, pairs // SUB,
        [lanes(512, 1)] * 4 + [per_pair(16, 512), per_pair(8, 512), per_pair(PAIR, 512), lanes(512, 2)]
        + [lanes(64, 2)] * 3 + [per_pair(8, 128)] * 2,
        [lanes(512, 1), lanes(512, 2), per_pair(8, 128)],
        [shape_of(1, 512, width), shape_of(2, 512, width, dtype=F32), shape_of(pairs, 8, 128, dtype=F32)],
        [], 15_000_000_000, "own_backward",
    )(queries, key_rows, values, grad_out, stats, stats2, grad_qt, own_part, *back, bias_far, bias_near)

    share_next, share_prev = call(
        unshare_kernel, pairs // 4,
        [scalars(), lanes(SHARE, 2, pairs=4)],
        [lanes(32, 2, pairs=4)] * 2,
        [shape_of(2, 32, width)] * 2,
        [], 400_000_000, "unshare",
    )(flag, d_share)
    bias = jnp.transpose(bias[:, : LEVELS - 1, :2], (1, 0, 2)).reshape(LEVELS - 1, 2 * pairs)
    count = n * lax.axis_size("dp")
    bias = total_over(bias, range(3, count.bit_length() - 1))
    back_next, back_prev = shifted(share_prev, -RING), shifted(share_next, RING)
    bias, back_next, back_prev = lax.optimization_barrier((bias, back_next, back_prev))
    grad_bias = total_over(bias, range(3)) * (
        1.0 / math.sqrt(512 * count)
    )

    grad_k, grad_v = call(
        finish_kernel, pairs // 4,
        [lanes(r, 2, pairs=4) for r in (512, 256, 256, SHARE, 32, 32)],
        [lanes(512, 1, pairs=4)] * 2,
        [shape_of(1, 512, width)] * 2,
        [], 400_000_000, "finish",
    )(own, back_right, back_left, d_share, back_next, back_prev)
    return attended, grad_q, grad_k, grad_v, grad_bias


def solution(mesh):
    rows = P("dp", "ctx", None)
    return jax.shard_map(
        body,
        mesh=mesh,
        in_specs=(rows, rows, rows, rows, P()),
        out_specs=(rows, rows, rows, rows, P()),
        check_vma=False,
    )
```

```python
import math

import jax
import jax.numpy as jnp
from jax import lax
from jax.experimental import pallas as pl
from jax.experimental.pallas import tpu as pltpu
from jax.sharding import PartitionSpec as P

BLOCK = 128
HALF = 64
LEVELS = 6
PAIR = 128
NEGATIVE = -1e30
LN2 = math.log(2.0)
F32 = jnp.float32
BF16 = jnp.bfloat16
MIB = 1 << 20
RING = 8
SUB = 2


def dot_nn(a, b):
    return lax.dot_general(a, b, (((1,), (0,)), ((), ())), preferred_element_type=F32)


def dot_nt(a, b):
    return lax.dot_general(a, b, (((1,), (1,)), ((), ())), preferred_element_type=F32)


def iota(shape, dim):
    return lax.broadcasted_iota(jnp.int32, shape, dim)


def halving(n):
    return jnp.where(iota((n // 2, n), 1) // 2 == iota((n // 2, n), 0), 0.5, 0.0).astype(BF16)


def doubling(n, factor):
    return (iota((n * factor, n), 0) // factor == iota((n * factor, n), 1)).astype(BF16)


def coarsen(x):
    rows = x.shape[0]
    step = min(rows, BLOCK)
    mean = halving(step)
    parts = [dot_nn(mean, x[i : i + step]).astype(BF16) for i in range(0, rows, step)]
    return parts[0] if len(parts) == 1 else jnp.concatenate(parts, axis=0)


def uncoarsen(x):
    rows = x.shape[0]
    step = min(rows, HALF)
    up = doubling(step, 2)
    half = (x * 0.5).astype(BF16)
    parts = [dot_nn(up, half[i : i + step]) for i in range(0, rows, step)]
    return parts[0] if len(parts) == 1 else jnp.concatenate(parts, axis=0)


def two_heads(x):
    low = iota(x.shape, 1) < HALF
    zero = jnp.zeros_like(x)
    return jnp.concatenate([jnp.where(low, x, zero), jnp.where(low, zero, x)], axis=0)


def own_head(x, span):
    same = (iota(x.shape, 0) < HALF) == (iota(x.shape, 1) // span % 2 == 0)
    return jnp.where(same, x, 0.0)


def spreader(level):
    rows = 512 >> level
    span = min(rows, HALF)
    shape = (2 * rows, 512)
    c = iota(shape, 0)
    row = c // (2 * span) * span + c % span
    return (iota(shape, 1) // 2**level == row).astype(BF16)


def split3(x):
    high = x.astype(BF16).astype(F32)
    rest = x - high
    mid = rest.astype(BF16).astype(F32)
    return high, mid, rest - mid


def stacked(rows, height):
    shape = (height, rows[0].shape[1])
    which = iota(shape, 0)
    out = jnp.zeros(shape, F32)
    for i, row in enumerate(rows):
        out = jnp.where(which == i, row, out)
    return out


def by_head(top, bottom, x):
    return jnp.concatenate([x[:HALF] * top, x[HALF:] * bottom], axis=0)


def spread_stats(rows, span, spread):
    flat = []
    for row in rows:
        first = iota(row.shape, 1) // span % 2 == 0
        for part in split3(row):
            flat.append(jnp.where(first, part, 0.0))
        for part in split3(row):
            flat.append(jnp.where(first, 0.0, part))
    wide = dot_nn(stacked(flat, 16).astype(BF16), spread)
    out = []
    for i in range(2 * len(rows)):
        out.append(wide[3 * i : 3 * i + 1] + wide[3 * i + 1 : 3 * i + 2] + wide[3 * i + 2 : 3 * i + 3])
    return out


def offset_row(low, high, span, shape):
    return jnp.where(iota(shape, 1) // span % 2 == 0, low, high)


def softmax_of(scores):
    top = jnp.max(scores, axis=0, keepdims=True)
    weights = jnp.exp(scores - top)
    return top, weights, jnp.sum(weights, axis=0, keepdims=True)


def with_bias(scores, biases):
    parts = []
    at = 0
    for lo, hi, bias in biases:
        if lo > at:
            parts.append(scores[at:lo])
        parts.append(scores[lo:hi] + bias)
        at = hi
    if at < scores.shape[0]:
        parts.append(scores[at:])
    return jnp.concatenate(parts, axis=0)


def halo_coarse(left, right):
    left1, right1 = coarsen(left[:128]), coarsen(right[:128])
    left2 = coarsen(jnp.concatenate([left[128:192], left1], axis=0))
    right2 = coarsen(jnp.concatenate([right1, right[128:192]], axis=0))
    return jnp.concatenate([left1, right1, left2, right2], axis=0)


def near_keys(own, coarse, left, right, halo):
    def joined(*parts):
        return jnp.concatenate(parts, axis=0)

    return (
        joined(left[:128], own, right[:128]),
        joined(left[128:192], halo[:64], coarse[:256], halo[64:128], right[128:192]),
        joined(left[192:256], halo[128:192], coarse[256:384], halo[192:256], right[192:256]),
    )


def window_parts(j):
    if j % 2 == 0:
        return (j, j + 4, j + 5)
    return (j - 1, j, j + 4)


def window_spans(j):
    a, b, c = window_parts(j)
    if b == a + 1:
        return [(a * HALF, (b + 1) * HALF), (c * HALF, (c + 1) * HALF)]
    return [(a * HALF, (a + 1) * HALF), (b * HALF, (c + 1) * HALF)]


def window_biases(j, halves, left_bias, right_bias):
    out = []
    for i, part in enumerate(window_parts(j)):
        if part < 2:
            out.append((i * HALF, (i + 1) * HALF, left_bias))
        elif part >= halves + 2:
            out.append((i * HALF, (i + 1) * HALF, right_bias))
    return out


def rows_of(ref, spans):
    if len(spans) == 1:
        return ref[spans[0][0] : spans[0][1], :]
    return jnp.concatenate([ref[lo:hi, :] for lo, hi in spans], axis=0)


def block_biases(b, left_bias, right_bias):
    if b == 0:
        return [(0, 128, left_bias)]
    if b == 3:
        return [(256, 384, right_bias)]
    return []


def prep_kernel(k_ref, v_ref, right_ref, left_ref, l3_ref, l4_ref, coarse_ref):
    for i, ref in enumerate((k_ref, v_ref)):
        zero = ref[0]
        one = coarsen(zero)
        two = coarsen(one)
        three = coarsen(two)
        right_ref[i, 0:128, :] = zero[384:512]
        right_ref[i, 128:192, :] = one[128:192]
        right_ref[i, 192:256, :] = two[0:64]
        left_ref[i, 0:128, :] = zero[0:128]
        left_ref[i, 128:192, :] = one[64:128]
        left_ref[i, 192:256, :] = two[64:128]
        l3_ref[i] = three
        l4_ref[i] = coarsen(three)
        coarse_ref[i, 0:256, :] = one
        coarse_ref[i, 256:384, :] = two


def query_kernel(q_ref, out_ref):
    rows = q_ref[0] * jnp.asarray(0.125, BF16)
    at = 0
    for level in range(1, LEVELS):
        rows = coarsen(rows)
        out_ref[at : at + (512 >> level), :] = rows
        at += 512 >> level


def pack_kernel(flag_ref, ring_ref, _, __, ___, next_ref, prev_ref, opposite_ref):
    first = flag_ref[0] > 0
    for i in range(2):
        four = ring_ref[i]
        five = coarsen(four)
        next_ref[i, 0:128, :] = jnp.where(first, four[128:256], five)
        next_ref[i, 128:192, :] = five[0:64]
        prev_ref[i, 0:128, :] = jnp.where(first, five, four[0:128])
        prev_ref[i, 128:192, :] = five[64:128]
        opposite_ref[i] = jnp.where(first, four[128:256], four[0:128])


def fold_kernel(flag_ref, opposite_ref, next_ref, prev_ref, _, ring_ref):
    first = flag_ref[0] > 0
    for i in range(2):
        own = opposite_ref[i].astype(F32)
        after, before = next_ref[i].astype(F32), prev_ref[i].astype(F32)
        five = jnp.where(first, before[0:128], after[0:128])
        five = five + jnp.concatenate([after[128:192], before[128:192]], axis=0)
        low = jnp.where(first, 0.0, own + before[0:128])
        high = jnp.where(first, own + after[0:128], 0.0)
        ring_ref[i] = (uncoarsen(five) + jnp.concatenate([low, high], axis=0)).astype(BF16)


def block_forward(b, keys, values_t, q0, left_bias, right_bias):
    scores = dot_nt(keys, two_heads(q0[b * 128 : b * 128 + 128]))
    scores = with_bias(scores, block_biases(b, left_bias, right_bias))
    top, weights, total = softmax_of(scores)
    mixed = dot_nn(values_t, weights.astype(BF16))
    return top, total, jnp.concatenate([mixed[:HALF, :128], mixed[HALF:, 128:]], axis=0)


def inner_forward_kernel(q_ref, k_ref, v_ref, l3_ref, st_ref, mix_ref, third_ref):
    third_ref[...] = l3_ref[...]

    def one(s):
        q0 = lane_view(q_ref, s)[0] * jnp.asarray(0.125, BF16)
        keys, values_t = lane_view(k_ref, s)[0], lane_view(v_ref, s)[0].T
        yield
        for i in range(2):
            span = slice(i * 128, i * 128 + 384)
            top, total, mixed = block_forward(1 + i, keys[span], values_t[:, span], q0, None, None)
            st_ref[s, 0:1, i * 256 : i * 256 + 256] = top
            st_ref[s, 1:2, i * 256 : i * 256 + 256] = total
            mix_ref[s, :, i * 128 : i * 128 + 128] = mixed
            yield

    interleaved(one(s) for s in range(SUB))


def near_forward_kernel(
    off_ref, edge_ref, q_ref, qc_ref, k_ref, v_ref, kvc_ref, nl_ref, nr_ref, ist_ref, imix_ref,
    st_ref, nt_ref, halo_ref, e1, e2, *scratch,
):
    step = pl.program_id(0)

    @pl.when(step == 0)
    def _():
        e1[...] = spreader(1)
        e2[...] = spreader(2)

    interleaved(
        near_forward_pair(
            step * SUB + s, off_ref, edge_ref, *[lane_view(r, s) for r in (q_ref, qc_ref, k_ref, v_ref, kvc_ref, nl_ref, nr_ref)],
            *[r.at[s : s + 1] for r in (ist_ref, imix_ref, st_ref, nt_ref)], lane_view(halo_ref, s), e1, e2, *[r.at[s] for r in scratch],
        )
        for s in range(SUB)
    )


def near_forward_pair(
    pair, off_ref, edge_ref, q_ref, qc_ref, k_ref, v_ref, kvc_ref, nl_ref, nr_ref, ist_ref, imix_ref,
    st_ref, nt_ref, halo_ref,
    e1, e2, k0s, k1s, k2s, vt0, vt1, vt2,
):
    left_bias, right_bias = edge_ref[0], edge_ref[1]
    q0 = q_ref[0] * jnp.asarray(0.125, BF16)
    q1, q2 = qc_ref[0:256], qc_ref[256:384]
    halos = [halo_coarse(nl_ref[i], nr_ref[i]) for i in range(2)]
    for i in range(2):
        halo_ref[i] = halos[i]
    for dst, x in zip((k0s, k1s, k2s), near_keys(k_ref[0], kvc_ref[0], nl_ref[0], nr_ref[0], halos[0])):
        dst[...] = x
    for dst, x in zip((vt0, vt1, vt2), near_keys(v_ref[0], kvc_ref[1], nl_ref[1], nr_ref[1], halos[1])):
        dst[...] = x.T
    yield

    blocks = {}
    for b in (0, 3):
        span = slice(b * 128, b * 128 + 384)
        blocks[b] = block_forward(b, k0s[span, :], vt0[:, span], q0, left_bias, right_bias)
        yield
    for i in range(2):
        at = slice(i * 256, i * 256 + 256)
        blocks[1 + i] = ist_ref[0, 0:1, at], ist_ref[0, 1:2, at], imix_ref[0, :, i * 128 : i * 128 + 128]
    tops, totals, mixes = zip(*[blocks[b] for b in range(4)])
    top_a = jnp.concatenate([t[:, :128] for t in tops], axis=1)
    top_b = jnp.concatenate([t[:, 128:] for t in tops], axis=1)
    total_a = jnp.concatenate([t[:, :128] for t in totals], axis=1)
    total_b = jnp.concatenate([t[:, 128:] for t in totals], axis=1)
    st_ref[0, 0:1, :] = top_a
    st_ref[0, 1:2, :] = top_b
    mixed0 = jnp.concatenate(mixes, axis=1)

    coarse = []
    for level, keys_ref, vt_ref, queries, spread in (
        (1, k1s, vt1, q1, e1), (2, k2s, vt2, q2, e2),
    ):
        halves = 8 >> level
        tops, totals, mixes = [], [], []
        for j in range(halves):
            spans = window_spans(j)
            scores = dot_nt(rows_of(keys_ref, spans), two_heads(queries[j * HALF : (j + 1) * HALF]))
            scores = with_bias(scores, window_biases(j, halves, left_bias, right_bias))
            top, weights, total = softmax_of(scores)
            vt = jnp.concatenate([vt_ref[:, lo:hi] for lo, hi in spans], axis=1)
            mixes.append(own_head(dot_nn(vt, weights.astype(BF16)), HALF).astype(BF16))
            tops.append(top)
            totals.append(total)
            yield
        top = jnp.concatenate(tops, axis=1)
        total = jnp.concatenate(totals, axis=1)
        st_ref[0, 1 + level : 2 + level, 0 : top.shape[1]] = top
        low = off_ref[level - 1, 2 * pair] + level * LN2
        high = off_ref[level - 1, 2 * pair + 1] + level * LN2
        top = top + offset_row(low, high, HALF, top.shape)
        wide = spread_stats([top, total], HALF, spread[...])
        mixed = dot_nn(jnp.concatenate(mixes, axis=1), spread[...])
        st_ref[0, 7 + 2 * level : 8 + 2 * level, :] = wide[0]
        st_ref[0, 8 + 2 * level : 9 + 2 * level, :] = wide[1]
        coarse.append((wide, mixed))
        yield

    peaks, denoms, factors = [], [], []
    for h, (top0, total0) in enumerate(((top_a, total_a), (top_b, total_b))):
        peak = top0
        for wide, _ in coarse:
            peak = jnp.maximum(peak, wide[h])
        f = [jnp.exp(top0 - peak)] + [jnp.exp(wide[h] - peak) for wide, _ in coarse]
        denom = f[0] * total0
        for i, (wide, _) in enumerate(coarse):
            denom = denom + f[i + 1] * wide[2 + h]
        peaks.append(peak)
        denoms.append(denom)
        factors.append(f)
    numer = by_head(factors[0][0], factors[1][0], mixed0)
    for i, (_, mixed) in enumerate(coarse):
        numer = numer + by_head(factors[0][i + 1], factors[1][i + 1], mixed)
    st_ref[0, 5:6, :] = peaks[0]
    st_ref[0, 6:7, :] = peaks[1]
    st_ref[0, 7:8, :] = denoms[0]
    st_ref[0, 8:9, :] = denoms[1]
    nt_ref[0] = numer


def far_kernel(
    off_ref, edge_ref, far_ref, flag_ref, qc_ref, g_ref, st_ref, nt_ref,
    opposite_ref, next_ref, prev_ref, f1_ref, f2_ref, f3_ref,
    att_ref, st2_ref, dq_ref, dopp_ref, dnext_ref, dprev_ref, d1_ref, d2_ref, d3_ref, bias_ref, e3, e4, e5,
):
    step = pl.program_id(0)

    @pl.when(step == 0)
    def _():
        e3[...] = spreader(3)
        e4[...] = spreader(4)
        e5[...] = spreader(5)

    def one(s):
        windows = [lane_view(r, s) for r in (f1_ref, f2_ref, f3_ref, opposite_ref, next_ref, prev_ref)]
        grads = [lane_view(r, s) for r in (dopp_ref, dnext_ref, dprev_ref, d1_ref, d2_ref, d3_ref)]
        return far_pair(
            step * SUB + s, off_ref, edge_ref, far_ref, flag_ref[0] > 0, lane_view(qc_ref, s), lane_view(g_ref, s),
            *[r.at[s : s + 1] for r in (st_ref, nt_ref)], *windows,
            lane_view(att_ref, s), *[r.at[s : s + 1] for r in (st2_ref, dq_ref)],
            *grads, bias_ref.at[s : s + 1], (e3, e4, e5),
        )

    interleaved(one(s) for s in range(SUB))


def far_pair(
    pair, off_ref, edge_ref, far_ref, first, qc_ref, g_ref, st_ref, nt_ref,
    f1_ref, f2_ref, f3_ref, opposite_ref, next_ref, prev_ref,
    att_ref, st2_ref, dq_ref, dopp_ref, dnext_ref, dprev_ref, d1_ref, d2_ref, d3_ref, bias_ref, spreads,
):
    coarse_q = {3: qc_ref[384:448], 4: qc_ref[448:480], 5: qc_ref[480:496]}
    gt = g_ref[0].T.astype(F32)
    windows = {3: [], 4: [], 5: []}
    for i in range(2):
        after, before = next_ref[i], prev_ref[i]
        windows[3].append(jnp.concatenate([f1_ref[i], f2_ref[i], f3_ref[i]], axis=0))
        near = jnp.where(first, before[0:128], after[0:128])
        windows[4].append(jnp.concatenate([opposite_ref[i], near], axis=0))
        windows[5].append(jnp.concatenate([
            jnp.where(first, before[128:192], before[0:64]),
            jnp.where(first, after[64:128], after[128:192]),
            jnp.where(first, after[0:64], before[64:128]),
        ], axis=0))
    levels = []
    for level, spread in zip((3, 4, 5), spreads):
        span = 512 >> level
        queries = two_heads(coarse_q[level])
        keys, values = windows[level]
        scores = dot_nt(keys, queries)
        parts = keys.shape[0] // HALF
        biases = [
            (i * HALF, (i + 1) * HALF, edge_ref[2 + i] if level == 3 else far_ref[level - 4, i]) for i in range(parts)
        ]
        top, weights, total = softmax_of(with_bias(scores, biases))
        mixed = own_head(dot_nn(values.T, weights.astype(BF16)), span).astype(BF16)
        low = off_ref[level - 1, 2 * pair] + level * LN2
        high = off_ref[level - 1, 2 * pair + 1] + level * LN2
        top = top + offset_row(low, high, span, top.shape)
        wide = spread_stats([top, total], span, spread[...])
        levels.append((level, span, queries, weights, wide, dot_nn(mixed, spread[...]), spread))
        yield

    logs, inners, numers = [], [], []
    for h in range(2):
        peak0, denom0 = st_ref[0, 5 + h : 6 + h, :], st_ref[0, 7 + h : 8 + h, :]
        peak = peak0
        for item in levels:
            peak = jnp.maximum(peak, item[4][h])
        keep = jnp.exp(peak0 - peak)
        denom = keep * denom0
        numer = keep * nt_ref[0, h * HALF : (h + 1) * HALF, :]
        for item in levels:
            f = jnp.exp(item[4][h] - peak)
            denom = denom + f * item[4][2 + h]
            numer = numer + f * item[5][h * HALF : (h + 1) * HALF]
        out = (numer / denom).astype(BF16)
        numers.append(out)
        logs.append(peak + jnp.log(denom))
        inners.append(
            jnp.sum(gt[h * HALF : (h + 1) * HALF] * out.astype(F32), axis=0, keepdims=True)
        )
    att_ref[0] = jnp.concatenate(numers, axis=0).T
    st2_ref[0] = stacked([logs[0], logs[1], inners[0], inners[1]], 8)
    yield

    dqt = jnp.zeros((PAIR, 512), F32)
    sums = jnp.zeros((8, 128), F32)
    grads = {}
    for level, span, queries, weights, wide, _, spread in levels:
        dq, bias, dk, dv = level_back(
            weights, *windows[level], queries, gt, wide[:2], logs, inners, span, spread
        )
        grads[level] = (dk.astype(BF16), dv.astype(BF16))
        dqt = dqt + dq * (0.125 / 2**level)
        sums = place(sums, level, bias, span)
        yield
    for i in range(2):
        for n, ref in enumerate((d1_ref, d2_ref, d3_ref)):
            ref[i] = grads[3][i][n * HALF : (n + 1) * HALF]
        four, five = grads[4][i], grads[5][i]
        start, end, third = five[0:64], five[64:128], five[128:192]
        blank = jnp.zeros_like(start)
        dopp_ref[i] = four[0:128]
        near_start = jnp.concatenate([four[128:256], start], axis=0)
        near_end = jnp.concatenate([four[128:256], end], axis=0)
        dprev_ref[i] = jnp.where(first, near_start, jnp.concatenate([start, third, blank], axis=0))
        dnext_ref[i] = jnp.where(first, jnp.concatenate([third, end, blank], axis=0), near_end)
    dq_ref[0] = dqt
    bias_ref[0] = sums


def place(sums, level, bias, span):
    first = iota(bias.shape, 1) // span % 2 == 0
    low = jnp.sum(jnp.where(first, bias, 0.0), axis=1, keepdims=True)
    high = jnp.sum(jnp.where(first, 0.0, bias), axis=1, keepdims=True)
    here = iota(sums.shape, 0) == level - 1
    lane = iota(sums.shape, 1)
    sums = jnp.where(here & (lane == 0), low, sums)
    return jnp.where(here & (lane == 1), high, sums)


def grad_rows(gt, tops, logs, inners, span, spread):
    f = [jnp.exp(tops[h] - logs[h]) for h in range(2)]
    g = dot_nt(spread[...], by_head(f[0], f[1], gt).astype(BF16))
    mine = (iota(g.shape, 1) < HALF) == (iota(g.shape, 0) // span % 2 == 0)
    g = jnp.where(mine, g, 0.0).astype(BF16)
    flat = [part for h in range(2) for part in split3(f[h] * inners[h])]
    wide = dot_nt(stacked(flat, 16).astype(BF16), spread[...])
    low = wide[0:1] + wide[1:2] + wide[2:3]
    high = wide[3:4] + wide[4:5] + wide[5:6]
    corr = jnp.where(iota(low.shape, 1) // span % 2 == 0, low, high)
    return g, corr


def window_back(weights, values, queries, g, corr):
    dots = dot_nt(values, g)
    grad = weights * (dots - corr)
    short = grad.astype(BF16)
    return short, dot_nn(short, queries), dot_nn(weights.astype(BF16), g), grad


def level_back(weights, keys, values, queries, gt, tops, logs, inners, span, spread):
    g, corr = grad_rows(gt, tops, logs, inners, span, spread)
    short, dk, dv, grad = window_back(weights, values, queries, g, corr)
    dq = own_head(dot_nn(keys.T, short), span).astype(BF16)
    return dot_nn(dq, spread[...]), jnp.sum(grad, axis=0, keepdims=True), dk, dv


def near_backward_kernel(
    edge_ref, q_ref, qc_ref, k_ref, v_ref, kvc_ref, g_ref, nl_ref, nr_ref, halo_ref, own_in_ref,
    st_ref, st2_ref, dqt_ref, bias_in_ref, _,
    dq_ref, own_ref, gl_ref, gr_ref, bias_ref,
    e1, e2, *scratch,
):
    step = pl.program_id(0)

    @pl.when(step == 0)
    def _():
        e1[...] = spreader(1)
        e2[...] = spreader(2)

    def one(s):
        wide = [lane_view(r, s) for r in (q_ref, qc_ref, k_ref, v_ref, kvc_ref, g_ref, nl_ref, nr_ref, halo_ref)]
        per = [r.at[s : s + 1] for r in (st_ref, st2_ref, dqt_ref, bias_in_ref)]
        out = [lane_view(r, s) for r in (own_in_ref, dq_ref, own_ref, gl_ref, gr_ref)]
        return near_backward_pair(
            edge_ref, *wide, *per, *out, bias_ref.at[s : s + 1], e1, e2, *[r.at[s] for r in scratch]
        )

    interleaved(one(s) for s in range(SUB))


def near_backward_pair(
    edge_ref, q_ref, qc_ref, k_ref, v_ref, kvc_ref, g_ref, nl_ref, nr_ref, halo_ref,
    st_ref, st2_ref, dqt_ref, bias_in_ref, own_in_ref, dq_ref, own_ref, gl_ref, gr_ref, bias_ref,
    e1, e2, k0s, k1s, k2s, v0s, v1s, v2s, kt0, kt1, kt2,
    dk0, dk1, dk2, dv0, dv1, dv2,
):
    left_bias, right_bias = edge_ref[0], edge_ref[1]
    q0 = q_ref[0] * jnp.asarray(0.125, BF16)
    q1, q2 = qc_ref[0:256], qc_ref[256:384]
    keys = near_keys(k_ref[0], kvc_ref[0], nl_ref[0], nr_ref[0], halo_ref[0])
    for dst, tdst, x in zip((k0s, k1s, k2s), (kt0, kt1, kt2), keys):
        dst[...] = x
        tdst[...] = x.T
    for dst, x in zip((v0s, v1s, v2s), near_keys(v_ref[0], kvc_ref[1], nl_ref[1], nr_ref[1], halo_ref[1])):
        dst[...] = x
    for ref in (dk0, dk1, dk2, dv0, dv1, dv2):
        ref[...] = jnp.zeros(ref.shape, F32)

    yield
    gt = g_ref[0].T.astype(F32)
    logs = [st2_ref[0, 0:1, :], st2_ref[0, 1:2, :]]
    inners = [st2_ref[0, 2:3, :], st2_ref[0, 3:4, :]]
    dqt = dqt_ref[0]
    sums = bias_in_ref[0]

    for level, ks, vs, kt, dk, dv, queries, spread in (
        (1, k1s, v1s, kt1, dk1, dv1, q1, e1),
        (2, k2s, v2s, kt2, dk2, dv2, q2, e2),
    ):
        halves = 8 >> level
        tops = [st_ref[0, 7 + 2 * level + h : 8 + 2 * level + h, :] for h in range(2)]
        g, corr = grad_rows(gt, tops, logs, inners, HALF, spread)
        dqs = []
        bias = jnp.zeros((1, 128), F32)
        for j in range(halves):
            spans = window_spans(j)
            at = slice(j * 128, (j + 1) * 128)
            queries_j = two_heads(queries[j * HALF : (j + 1) * HALF])
            scores = dot_nt(rows_of(ks, spans), queries_j)
            scores = with_bias(scores, window_biases(j, halves, left_bias, right_bias))
            weights = jnp.exp(scores - st_ref[0, 1 + level : 2 + level, at])
            short, dk_j, dv_j, grad = window_back(weights, rows_of(vs, spans), queries_j, g[at], corr[:, at])
            bias = bias + jnp.sum(grad, axis=0, keepdims=True)
            base = 0
            for lo, hi in spans:
                dk[lo:hi, :] += dk_j[base : base + hi - lo]
                dv[lo:hi, :] += dv_j[base : base + hi - lo]
                base += hi - lo
            kt_j = jnp.concatenate([kt[:, lo:hi] for lo, hi in spans], axis=1)
            dqs.append(own_head(dot_nn(kt_j, short), HALF).astype(BF16))
            yield
        dqt = dqt + dot_nn(jnp.concatenate(dqs, axis=1), spread[...]) * (0.125 / 2**level)
        sums = place(sums, level, bias, HALF)
    bias_ref[0] = sums

    g0, corr0 = zero_rows(gt, st_ref, logs, inners)
    dq0 = {}
    for b in (0, 3):
        span = slice(b * 128, b * 128 + 384)
        dq0[b], dk_b, dv_b = block_back(
            b, k0s[span, :], v0s[span, :], kt0[:, span], q0, g0, corr0, st_ref, left_bias, right_bias
        )
        dk0[span, :] += dk_b
        dv0[span, :] += dv_b
        yield
    blank = jnp.zeros((PAIR, 256), F32)
    dqt = dqt + jnp.concatenate([dq0[0], blank, dq0[3]], axis=1)
    dq_ref[0] = dqt.astype(BF16).T

    for i, (zero, one, two) in enumerate(((dk0, dk1, dk2), (dv0, dv1, dv2))):
        left1 = one[0:128, :] + uncoarsen(two[64:128, :])
        left0 = zero[0:128, :] + uncoarsen(left1[64:128])
        gl_ref[i, 0:128, :] = left0.astype(BF16)
        gl_ref[i, 128:192, :] = left1[0:64].astype(BF16)
        gl_ref[i, 192:256, :] = two[0:64, :].astype(BF16)
        right1 = one[384:512, :] + uncoarsen(two[256:320, :])
        right0 = zero[640:768, :] + uncoarsen(right1[0:64])
        gr_ref[i, 0:128, :] = right0.astype(BF16)
        gr_ref[i, 128:192, :] = right1[64:128].astype(BF16)
        gr_ref[i, 192:256, :] = two[320:384, :].astype(BF16)
        mine1 = one[128:384, :] + uncoarsen(two[128:256, :])
        own_ref[i] = own_in_ref[i] + zero[128:640, :] + uncoarsen(mine1)


def zero_rows(gt, st_ref, logs, inners):
    f0 = [jnp.exp(st_ref[0, h : h + 1, :] - logs[h]) for h in range(2)]
    g0 = by_head(f0[0], f0[1], gt).astype(BF16).T
    return g0, [f0[h] * inners[h] for h in range(2)]


def block_back(b, keys, values, keys_t, q0, g0, corr0, st_ref, left_bias, right_bias):
    at = slice(b * 128, (b + 1) * 128)
    queries = two_heads(q0[at])
    scores = with_bias(dot_nt(keys, queries), block_biases(b, left_bias, right_bias))
    top = jnp.concatenate([st_ref[0, 0:1, at], st_ref[0, 1:2, at]], axis=1)
    corr = jnp.concatenate([corr0[0][:, at], corr0[1][:, at]], axis=1)
    weights = jnp.exp(scores - top)
    short, dk, dv, _ = window_back(weights, values, queries, two_heads(g0[at]), corr)
    dq = dot_nn(keys_t, short)
    return jnp.concatenate([dq[:HALF, :128], dq[HALF:, 128:]], axis=0) * 0.125, dk, dv


def own_backward_kernel(
    q_ref, k_ref, v_ref, g_ref, st_ref, st2_ref, dqf_ref, d1_ref, d2_ref, d3_ref,
    dqt_ref, own_ref, o1_ref, o2_ref, o3_ref,
):
    for ref, out_ref in ((d1_ref, o1_ref), (d2_ref, o2_ref), (d3_ref, o3_ref)):
        out_ref[...] = ref[...]

    def one(s):
        wide = [lane_view(r, s) for r in (q_ref, k_ref, v_ref, g_ref)]
        per = [r.at[s : s + 1] for r in (st_ref, st2_ref, dqf_ref, dqt_ref)]
        return own_backward_pair(*wide, *per, lane_view(own_ref, s))

    interleaved(one(s) for s in range(SUB))


def own_backward_pair(q_ref, k_ref, v_ref, g_ref, st_ref, st2_ref, dqf_ref, dqt_ref, own_ref):
    q0 = q_ref[0] * jnp.asarray(0.125, BF16)
    keys, values = k_ref[0], v_ref[0]
    keys_t = keys.T
    gt = g_ref[0].T.astype(F32)
    logs = [st2_ref[0, 0:1, :], st2_ref[0, 1:2, :]]
    inners = [st2_ref[0, 2:3, :], st2_ref[0, 3:4, :]]
    g0, corr0 = zero_rows(gt, st_ref, logs, inners)
    yield
    out = {}
    for b in (1, 2):
        span = slice((b - 1) * 128, (b + 2) * 128)
        out[b] = block_back(b, keys[span], values[span], keys_t[:, span], q0, g0, corr0, st_ref, None, None)
        yield
    blank = jnp.zeros((PAIR, PAIR), F32)
    dqt_ref[0] = dqf_ref[0] + jnp.concatenate([blank, out[1][0], out[2][0], blank], axis=1)
    for i in range(2):
        one, two = out[1][1 + i], out[2][1 + i]
        own_ref[i, 0:128, :] = one[0:128]
        own_ref[i, 128:384, :] = one[128:384] + two[0:256]
        own_ref[i, 384:512, :] = two[256:384]


def finish_kernel(own_ref, left_ref, right_ref, a_ref, b_ref, c_ref, four_ref, dk_ref, dv_ref):
    up2, up4, up8 = [doubling(HALF, factor) for factor in (2, 4, 8)]
    up16 = doubling(HALF // 2, 16)
    for i, out in enumerate((dk_ref, dv_ref)):
        three = sum(ref[i].astype(F32) for ref in (a_ref, b_ref, c_ref)) * 0.125
        far = dot_nn(up16, four_ref[i]) * 0.0625 + dot_nn(up8, three.astype(BF16))
        left1 = dot_nn(up2, left_ref[i, 128:192, :]) * 0.5
        left2 = dot_nn(up4, left_ref[i, 192:256, :]) * 0.25
        right1 = dot_nn(up2, right_ref[i, 128:192, :]) * 0.5
        right2 = dot_nn(up4, right_ref[i, 192:256, :]) * 0.25
        parts = [
            left_ref[i, 0:128, :].astype(F32) + right2[0:128],
            left1 + right2[128:256],
            left2[0:128] + right1,
            left2[128:256] + right_ref[i, 0:128, :].astype(F32),
        ]
        out[0] = (own_ref[i] + far + jnp.concatenate(parts, axis=0)).astype(BF16)


def lanes(rows, *lead, pairs=SUB):
    shape = tuple(lead) + (rows, PAIR * pairs)
    zeros = (0,) * (len(shape) - 1)
    return pl.BlockSpec(shape, lambda p: zeros + (p,))


def per_pair(*shape):
    zeros = (0,) * len(shape)
    return pl.BlockSpec((SUB,) + shape, lambda p: (p,) + zeros)


def interleaved(parts):
    live = list(parts)
    while live:
        for part in list(live):
            try:
                next(part)
            except StopIteration:
                live.remove(part)


def lane_view(ref, s):
    return ref.at[..., s * PAIR : (s + 1) * PAIR]


def scalars():
    return pl.BlockSpec(memory_space=pltpu.SMEM)


def shape_of(*shape, dtype=BF16):
    return jax.ShapeDtypeStruct(shape, dtype)


def call(kernel, steps, in_specs, out_specs, out_shape, scratch, cost, name, mib=48):
    return pl.pallas_call(
        kernel,
        grid=(steps,),
        in_specs=in_specs,
        out_specs=out_specs,
        out_shape=out_shape,
        scratch_shapes=scratch,
        compiler_params=pltpu.CompilerParams(
            vmem_limit_bytes=mib * MIB, dimension_semantics=("arbitrary",)
        ),
        cost_estimate=pl.CostEstimate(flops=cost, bytes_accessed=cost // 300, transcendentals=0),
        name=name,
    )


def permute(block, route):
    return lax.ppermute(block, "ctx", route)


def shifted(block, distance):
    n = lax.axis_size("ctx")
    return permute(block, [(i, i + distance) for i in range(n) if 0 <= i + distance < n])


def crossed(block, span):
    n = lax.axis_size("ctx")
    route = []
    for i in range(n):
        to = i + 3 * span if i // span % 2 == 0 else i - 3 * span
        if 0 <= to < n:
            route.append((i, to))
    return permute(block, route)


def ring_groups():
    n = lax.axis_size("ctx")
    return [list(range(i, i + RING)) for i in range(0, n, RING)]


def total_over(x, bits):
    count = lax.axis_size("dp") * lax.axis_size("ctx")

    def from_device(x, mask):
        return lax.ppermute(x, ("dp", "ctx"), [(i, i ^ mask) for i in range(count)])

    for at in range(0, len(bits), 2):
        a = 1 << bits[at]
        first = x + from_device(x, a)
        if at + 1 < len(bits):
            b = 1 << bits[at + 1]
            first = first + (from_device(x, b) + from_device(x, a | b))
        x = first
    return x


def body(queries, key_rows, values, grad_out, level_bias):
    width = queries.shape[2]
    pairs = width // PAIR
    n = lax.axis_size("ctx")
    me = lax.axis_index("ctx")

    def bias_of(flags):
        return jnp.where(jnp.stack(flags), 0.0, NEGATIVE).astype(F32)

    half = me % RING // 2
    is_first = half < 2
    has_prev, has_next = me >= RING, me < n - RING
    near_ring, far_ring = jnp.where(is_first, has_prev, has_next), jnp.where(is_first, has_next, has_prev)
    edge_bias = bias_of([
        me > 0, me < n - 1, me >= 2, me + 2 < n, jnp.where(me % 2 == 0, me + 3 < n, me >= 3)
    ])
    far_bias = jnp.stack([
        bias_of([half != 1, half != 2, near_ring & (half != 3), near_ring & (half != 0)]),
        bias_of([has_prev, has_next, far_ring, far_ring]),
    ])
    flag = is_first.astype(jnp.int32)[None]

    send_right, send_left, l3, l4, kv_coarse = call(
        prep_kernel, pairs // 4,
        [lanes(512, 1, pairs=4)] * 2,
        [lanes(r, 2, pairs=4) for r in (256, 256, 64, 32, 384)],
        [shape_of(2, r, width) for r in (256, 256, 64, 32, 384)],
        [], 400_000_000, "prep", 60,
    )(key_rows, values)

    ring = lax.all_gather(l4, "ctx", axis=1, tiled=True, axis_index_groups=ring_groups())
    near_left = shifted(send_right, 1)
    near_right = shifted(send_left, -1)
    inner_stats, inner_mixed, third_out = call(
        inner_forward_kernel, pairs // SUB,
        [lanes(512, 1)] * 3 + [lanes(64, 2)],
        [per_pair(8, 512), per_pair(PAIR, 256), lanes(64, 2)],
        [shape_of(pairs, 8, 512, dtype=F32), shape_of(pairs, PAIR, 256, dtype=F32), shape_of(2, 64, width)],
        [], 10_000_000_000, "inner_forward",
    )(queries, key_rows, values, l3)
    third = [shifted(third_out, 2), shifted(third_out, -2), crossed(third_out, 1)]

    to_next, to_prev, opposite = call(
        pack_kernel, pairs // 4,
        [scalars(), lanes(256, 2, pairs=4)]
        + [pl.BlockSpec(memory_space=pl.ANY)] * 3,
        [lanes(r, 2, pairs=4) for r in (192, 192, 128)],
        [shape_of(2, r, width) for r in (192, 192, 128)],
        [], 400_000_000, "pack",
    )(flag, ring, inner_stats, near_left, near_right)
    from_prev = shifted(to_next, RING)
    from_next = shifted(to_prev, -RING)

    q_coarse = call(
        query_kernel, pairs // 4,
        [lanes(512, 1, pairs=4)], [lanes(496, pairs=4)], [shape_of(496, width)],
        [], 400_000_000, "queries",
    )(queries)[0]

    spreads = [pltpu.VMEM((r, 512), BF16) for r in (512, 256)]
    key_sets = [pltpu.VMEM((SUB, r, PAIR), BF16) for r in (768, 512, 384)]
    turned = [pltpu.VMEM((SUB, PAIR, r), BF16) for r in (768, 512, 384)]
    sums = [pltpu.VMEM((SUB, r, PAIR), F32) for r in (768, 512, 384)]

    stats, numer, halo = call(
        near_forward_kernel, pairs // SUB,
        [scalars(), scalars(), lanes(512, 1), lanes(496), lanes(512, 1), lanes(512, 1), lanes(384, 2)]
        + [lanes(256, 2)] * 2 + [per_pair(8, 512), per_pair(PAIR, 256)],
        [per_pair(16, 512), per_pair(PAIR, 512), lanes(256, 2)],
        [
            shape_of(pairs, 16, 512, dtype=F32), shape_of(pairs, PAIR, 512, dtype=F32), shape_of(2, 256, width)
        ],
        spreads + key_sets + turned, 30_000_000_000, "near_forward",
    )(level_bias, edge_bias, queries, q_coarse, key_rows, values, kv_coarse, near_left, near_right, inner_stats, inner_mixed)

    attended, stats2, dq_far, d_opposite, d_next, d_prev, d1, d2, d3, bias_far = call(
        far_kernel, pairs // SUB,
        [scalars()] * 4 + [lanes(496), lanes(512, 1), per_pair(16, 512), per_pair(PAIR, 512)]
        + [lanes(r, 2) for r in (128, 192, 192, 64, 64, 64)],
        [lanes(512, 1), per_pair(8, 512), per_pair(PAIR, 512)]
        + [lanes(r, 2) for r in (128, 192, 192, 64, 64, 64)] + [per_pair(8, 128)],
        [
            shape_of(1, 512, width),
            shape_of(pairs, 8, 512, dtype=F32),
            shape_of(pairs, PAIR, 512, dtype=F32),
        ] + [shape_of(2, r, width) for r in (128, 192, 192, 64, 64, 64)] + [shape_of(pairs, 8, 128, dtype=F32)],
        [pltpu.VMEM((r, 512), BF16) for r in (128, 64, 32)], 20_000_000_000, "far",
    )(
        level_bias, edge_bias, far_bias, flag, q_coarse, grad_out, stats, numer,
        opposite, from_next, from_prev, *third,
    )
    back_next, back_prev = shifted(d_prev, -RING), shifted(d_next, RING)

    grad_qt, own_part, d1, d2, d3 = call(
        own_backward_kernel, pairs // SUB,
        [lanes(512, 1)] * 4 + [per_pair(16, 512), per_pair(8, 512), per_pair(PAIR, 512)]
        + [lanes(64, 2)] * 3,
        [per_pair(PAIR, 512), lanes(512, 2)] + [lanes(64, 2)] * 3,
        [shape_of(pairs, PAIR, 512, dtype=F32), shape_of(2, 512, width, dtype=F32)] + [shape_of(2, 64, width)] * 3,
        [], 15_000_000_000, "own_backward",
    )(queries, key_rows, values, grad_out, stats, stats2, dq_far, d1, d2, d3)
    back = [shifted(d1, -2), shifted(d2, 2), crossed(d3, 1)]

    d_ring = call(
        fold_kernel, pairs // 4,
        [scalars()] + [lanes(r, 2, pairs=4) for r in (128, 192, 192)] + [pl.BlockSpec(memory_space=pl.ANY)],
        [lanes(256, 2, pairs=4)],
        [shape_of(2, 256, width)],
        [], 400_000_000, "fold",
    )(flag, d_opposite, back_next, back_prev, grad_qt)[0]
    d_four = lax.psum_scatter(d_ring, "ctx", scatter_dimension=1, tiled=True, axis_index_groups=ring_groups())

    grad_q, own, to_left, to_right, bias = call(
        near_backward_kernel, pairs // SUB,
        [scalars(), lanes(512, 1), lanes(496), lanes(512, 1), lanes(512, 1), lanes(384, 2), lanes(512, 1)]
        + [lanes(256, 2)] * 3 + [lanes(512, 2)]
        + [per_pair(16, 512), per_pair(8, 512), per_pair(PAIR, 512), per_pair(8, 128)]
        + [pl.BlockSpec(memory_space=pl.ANY)],
        [lanes(512, 1), lanes(512, 2)] + [lanes(256, 2)] * 2 + [per_pair(8, 128)],
        [shape_of(1, 512, width), shape_of(2, 512, width, dtype=F32)]
        + [shape_of(2, 256, width)] * 2 + [shape_of(pairs, 8, 128, dtype=F32)],
        spreads + key_sets + key_sets + turned + sums + sums, 30_000_000_000, "near_backward",
    )(
        edge_bias, queries, q_coarse, key_rows, values, kv_coarse, grad_out,
        near_left, near_right, halo, own_part, stats, stats2, grad_qt, bias_far, d_ring,
    )
    back_right, back_left = shifted(to_right, 1), shifted(to_left, -1)

    bias = jnp.transpose(bias[:, : LEVELS - 1, :2], (1, 0, 2)).reshape(LEVELS - 1, 2 * pairs)
    count = n * lax.axis_size("dp")
    bias, *back = lax.optimization_barrier((bias, *back))
    bias = total_over(bias, range(3, count.bit_length() - 1))
    grad_bias = total_over(bias, range(3)) * (1.0 / math.sqrt(512 * count))

    grad_k, grad_v = call(
        finish_kernel, pairs // 4,
        [lanes(r, 2, pairs=4) for r in (512, 256, 256, 64, 64, 64, 32)],
        [lanes(512, 1, pairs=4)] * 2,
        [shape_of(1, 512, width)] * 2,
        [], 400_000_000, "finish",
    )(own, back_right, back_left, *back, d_four)
    return attended, grad_q, grad_k, grad_v, grad_bias


def solution(mesh):
    rows = P("dp", "ctx", None)
    return jax.shard_map(
        body,
        mesh=mesh,
        in_specs=(rows, rows, rows, rows, P()),
        out_specs=(rows, rows, rows, rows, P()),
        check_vma=False,
    )
```

```python
import math

import jax
import jax.numpy as jnp
from jax import lax
from jax.experimental import pallas as pl
from jax.experimental.pallas import tpu as pltpu
from jax.sharding import PartitionSpec as P

BLOCK = 128
HALF = 64
LEVELS = 6
PAIR = 128
NEGATIVE = -1e30
LN2 = math.log(2.0)
F32 = jnp.float32
BF16 = jnp.bfloat16
MIB = 1 << 20
RING = 8
SHARE = 96
TOTAL_ROWS = {1: (13, 14), 2: (15, 4)}
SUB = 2


def dot_nn(a, b):
    return lax.dot_general(a, b, (((1,), (0,)), ((), ())), preferred_element_type=F32)


def dot_nt(a, b):
    return lax.dot_general(a, b, (((1,), (1,)), ((), ())), preferred_element_type=F32)


def iota(shape, dim):
    return lax.broadcasted_iota(jnp.int32, shape, dim)


def halving(n):
    return jnp.where(iota((n // 2, n), 1) // 2 == iota((n // 2, n), 0), 0.5, 0.0).astype(BF16)


def doubling(n, factor):
    return (iota((n * factor, n), 0) // factor == iota((n * factor, n), 1)).astype(BF16)


def coarsen(x):
    rows = x.shape[0]
    step = min(rows, BLOCK)
    mean = halving(step)
    parts = [dot_nn(mean, x[i : i + step]).astype(BF16) for i in range(0, rows, step)]
    return parts[0] if len(parts) == 1 else jnp.concatenate(parts, axis=0)


def uncoarsen(x):
    rows = x.shape[0]
    step = min(rows, HALF)
    up = doubling(step, 2)
    half = (x * 0.5).astype(BF16)
    parts = [dot_nn(up, half[i : i + step]) for i in range(0, rows, step)]
    return parts[0] if len(parts) == 1 else jnp.concatenate(parts, axis=0)


def two_heads(x):
    low = iota(x.shape, 1) < HALF
    zero = jnp.zeros_like(x)
    return jnp.concatenate([jnp.where(low, x, zero), jnp.where(low, zero, x)], axis=0)


def own_head(x, span):
    same = (iota(x.shape, 0) < HALF) == (iota(x.shape, 1) // span % 2 == 0)
    return jnp.where(same, x, 0.0)


def spreader(level):
    rows = 512 >> level
    span = min(rows, HALF)
    shape = (2 * rows, 512)
    c = iota(shape, 0)
    row = c // (2 * span) * span + c % span
    return (iota(shape, 1) // 2**level == row).astype(BF16)


def split3(x):
    high = x.astype(BF16).astype(F32)
    rest = x - high
    mid = rest.astype(BF16).astype(F32)
    return high, mid, rest - mid


def stacked(rows, height):
    shape = (height, rows[0].shape[1])
    which = iota(shape, 0)
    out = jnp.zeros(shape, F32)
    for i, row in enumerate(rows):
        out = jnp.where(which == i, row, out)
    return out


def by_head(top, bottom, x):
    return jnp.concatenate([x[:HALF] * top, x[HALF:] * bottom], axis=0)


def spread_stats(rows, span, spread):
    flat = []
    for row in rows:
        first = iota(row.shape, 1) // span % 2 == 0
        for part in split3(row):
            flat.append(jnp.where(first, part, 0.0))
        for part in split3(row):
            flat.append(jnp.where(first, 0.0, part))
    wide = dot_nn(stacked(flat, 16).astype(BF16), spread)
    out = []
    for i in range(2 * len(rows)):
        out.append(wide[3 * i : 3 * i + 1] + wide[3 * i + 1 : 3 * i + 2] + wide[3 * i + 2 : 3 * i + 3])
    return out


def offset_row(low, high, span, shape):
    return jnp.where(iota(shape, 1) // span % 2 == 0, low, high)


def softmax_of(scores):
    top = jnp.max(scores, axis=0, keepdims=True)
    weights = jnp.exp(scores - top)
    return top, weights, jnp.sum(weights, axis=0, keepdims=True)


def with_bias(scores, biases):
    parts = []
    at = 0
    for lo, hi, bias in biases:
        if lo > at:
            parts.append(scores[at:lo])
        parts.append(scores[lo:hi] + bias)
        at = hi
    if at < scores.shape[0]:
        parts.append(scores[at:])
    return jnp.concatenate(parts, axis=0)


def halo_coarse(left, right):
    left1, right1 = coarsen(left[:128]), coarsen(right[:128])
    left2 = coarsen(jnp.concatenate([left[128:192], left1], axis=0))
    right2 = coarsen(jnp.concatenate([right1, right[128:192]], axis=0))
    return jnp.concatenate([left1, right1, left2, right2], axis=0)


def near_keys(own, coarse, left, right, halo):
    def joined(*parts):
        return jnp.concatenate(parts, axis=0)

    return (
        joined(left[:128], own, right[:128]),
        joined(left[128:192], halo[:64], coarse[:256], halo[64:128], right[128:192]),
        joined(left[192:256], halo[128:192], coarse[256:384], halo[192:256], right[192:256]),
    )


def window_parts(j):
    if j % 2 == 0:
        return (j, j + 4, j + 5)
    return (j - 1, j, j + 4)


def window_spans(j):
    a, b, c = window_parts(j)
    if b == a + 1:
        return [(a * HALF, (b + 1) * HALF), (c * HALF, (c + 1) * HALF)]
    return [(a * HALF, (a + 1) * HALF), (b * HALF, (c + 1) * HALF)]


def window_biases(j, halves, left_bias, right_bias):
    out = []
    for i, part in enumerate(window_parts(j)):
        if part < 2:
            out.append((i * HALF, (i + 1) * HALF, left_bias))
        elif part >= halves + 2:
            out.append((i * HALF, (i + 1) * HALF, right_bias))
    return out


def rows_of(ref, spans):
    if len(spans) == 1:
        return ref[spans[0][0] : spans[0][1], :]
    return jnp.concatenate([ref[lo:hi, :] for lo, hi in spans], axis=0)


def block_biases(b, left_bias, right_bias):
    if b == 0:
        return [(0, 128, left_bias)]
    if b == 3:
        return [(256, 384, right_bias)]
    return []


def prep_kernel(k_ref, v_ref, right_ref, left_ref, l3_ref, l4_ref, coarse_ref):
    for i, ref in enumerate((k_ref, v_ref)):
        zero = ref[0]
        one = coarsen(zero)
        two = coarsen(one)
        three = coarsen(two)
        right_ref[i, 0:128, :] = zero[384:512]
        right_ref[i, 128:192, :] = one[128:192]
        right_ref[i, 192:256, :] = two[0:64]
        left_ref[i, 0:128, :] = zero[0:128]
        left_ref[i, 128:192, :] = one[64:128]
        left_ref[i, 192:256, :] = two[64:128]
        l3_ref[i] = three
        l4_ref[i] = coarsen(three)
        coarse_ref[i, 0:256, :] = one
        coarse_ref[i, 256:384, :] = two


def query_kernel(q_ref, out_ref):
    rows = q_ref[0] * jnp.asarray(0.125, BF16)
    at = 0
    for level in range(1, LEVELS):
        rows = coarsen(rows)
        out_ref[at : at + (512 >> level), :] = rows
        at += 512 >> level


def pack_kernel(flag_ref, ring_ref, _, __, ___, next_ref, prev_ref, opposite_ref):
    first = flag_ref[0] > 0
    for i in range(2):
        four = ring_ref[i]
        five = coarsen(four)
        next_ref[i, 0:128, :] = jnp.where(first, four[128:256], five)
        next_ref[i, 128:192, :] = five[0:64]
        prev_ref[i, 0:128, :] = jnp.where(first, five, four[0:128])
        prev_ref[i, 128:192, :] = five[64:128]
        opposite_ref[i] = jnp.where(first, four[128:256], four[0:128])


def unshare_kernel(flag_ref, sum_ref, _, next_ref, prev_ref, cells_ref):
    first = flag_ref[0] > 0
    cells_ref[...] = sum_ref[0, 80:96, :].astype(F32)
    for i in range(2):
        four = sum_ref[i, 32:64, :]
        five = uncoarsen(sum_ref[i, 64:80, :].astype(F32)).astype(BF16)
        next_ref[i] = jnp.where(first, four, five)
        prev_ref[i] = jnp.where(first, five, four)


def block_forward(b, keys, values_t, q0, left_bias, right_bias):
    scores = dot_nt(keys, two_heads(q0[b * 128 : b * 128 + 128]))
    scores = with_bias(scores, block_biases(b, left_bias, right_bias))
    top, weights, total = softmax_of(scores)
    mixed = dot_nn(values_t, weights.astype(BF16))
    return top, total, jnp.concatenate([mixed[:HALF, :128], mixed[HALF:, 128:]], axis=0)


def inner_forward_kernel(q_ref, k_ref, v_ref, l3_ref, st_ref, mix_ref, third_ref):
    third_ref[...] = l3_ref[...]

    def one(s):
        q0 = lane_view(q_ref, s)[0] * jnp.asarray(0.125, BF16)
        keys, values_t = lane_view(k_ref, s)[0], lane_view(v_ref, s)[0].T
        yield
        for i in range(2):
            span = slice(i * 128, i * 128 + 384)
            top, total, mixed = block_forward(1 + i, keys[span], values_t[:, span], q0, None, None)
            st_ref[s, 0:1, i * 256 : i * 256 + 256] = top
            st_ref[s, 1:2, i * 256 : i * 256 + 256] = total
            mix_ref[s, :, i * 128 : i * 128 + 128] = mixed
            yield

    interleaved(one(s) for s in range(SUB))


def near_forward_kernel(
    off_ref, edge_ref, q_ref, qc_ref, k_ref, v_ref, kvc_ref, nl_ref, nr_ref, ist_ref, imix_ref,
    st_ref, nt_ref, mx_ref, halo_ref, e1, e2, *scratch,
):
    step = pl.program_id(0)

    @pl.when(step == 0)
    def _():
        e1[...] = spreader(1)
        e2[...] = spreader(2)

    interleaved(
        near_forward_pair(
            step * SUB + s, off_ref, edge_ref, *[lane_view(r, s) for r in (q_ref, qc_ref, k_ref, v_ref, kvc_ref, nl_ref, nr_ref)],
            *[r.at[s : s + 1] for r in (ist_ref, imix_ref, st_ref, nt_ref, mx_ref)], lane_view(halo_ref, s), e1, e2, *[r.at[s] for r in scratch],
        )
        for s in range(SUB)
    )


def near_forward_pair(
    pair, off_ref, edge_ref, q_ref, qc_ref, k_ref, v_ref, kvc_ref, nl_ref, nr_ref, ist_ref, imix_ref,
    st_ref, nt_ref, mx_ref, halo_ref,
    e1, e2, k0s, k1s, k2s, vt0, vt1, vt2,
):
    left_bias, right_bias = edge_ref[0], edge_ref[1]
    q0 = q_ref[0] * jnp.asarray(0.125, BF16)
    q1, q2 = qc_ref[0:256], qc_ref[256:384]
    halos = [halo_coarse(nl_ref[i], nr_ref[i]) for i in range(2)]
    for i in range(2):
        halo_ref[i] = halos[i]
    for dst, x in zip((k0s, k1s, k2s), near_keys(k_ref[0], kvc_ref[0], nl_ref[0], nr_ref[0], halos[0])):
        dst[...] = x
    for dst, x in zip((vt0, vt1, vt2), near_keys(v_ref[0], kvc_ref[1], nl_ref[1], nr_ref[1], halos[1])):
        dst[...] = x.T
    yield

    blocks = {}
    for b in (0, 3):
        span = slice(b * 128, b * 128 + 384)
        blocks[b] = block_forward(b, k0s[span, :], vt0[:, span], q0, left_bias, right_bias)
        yield
    for i in range(2):
        at = slice(i * 256, i * 256 + 256)
        blocks[1 + i] = ist_ref[0, 0:1, at], ist_ref[0, 1:2, at], imix_ref[0, :, i * 128 : i * 128 + 128]
    tops, totals, mixes = zip(*[blocks[b] for b in range(4)])
    top_a = jnp.concatenate([t[:, :128] for t in tops], axis=1)
    top_b = jnp.concatenate([t[:, 128:] for t in tops], axis=1)
    total_a = jnp.concatenate([t[:, :128] for t in totals], axis=1)
    total_b = jnp.concatenate([t[:, 128:] for t in totals], axis=1)
    st_ref[0, 0:1, :] = top_a
    st_ref[0, 1:2, :] = top_b
    mixed0 = jnp.concatenate(mixes, axis=1)

    coarse = []
    for level, keys_ref, vt_ref, queries, spread in (
        (1, k1s, vt1, q1, e1), (2, k2s, vt2, q2, e2),
    ):
        halves = 8 >> level
        tops, totals, mixes = [], [], []
        for j in range(halves):
            spans = window_spans(j)
            scores = dot_nt(rows_of(keys_ref, spans), two_heads(queries[j * HALF : (j + 1) * HALF]))
            scores = with_bias(scores, window_biases(j, halves, left_bias, right_bias))
            top, weights, total = softmax_of(scores)
            vt = jnp.concatenate([vt_ref[:, lo:hi] for lo, hi in spans], axis=1)
            mixes.append(own_head(dot_nn(vt, weights.astype(BF16)), HALF).astype(BF16))
            tops.append(top)
            totals.append(total)
            yield
        top = jnp.concatenate(tops, axis=1)
        total = jnp.concatenate(totals, axis=1)
        st_ref[0, 1 + level : 2 + level, 0 : top.shape[1]] = top
        low = off_ref[level - 1, 2 * pair] + level * LN2
        high = off_ref[level - 1, 2 * pair + 1] + level * LN2
        top = top + offset_row(low, high, HALF, top.shape)
        wide = spread_stats([top, total], HALF, spread[...])
        mixed = dot_nn(jnp.concatenate(mixes, axis=1), spread[...])
        st_ref[0, 7 + 2 * level : 8 + 2 * level, :] = wide[0]
        st_ref[0, 8 + 2 * level : 9 + 2 * level, :] = wide[1]
        for h in range(2):
            at = TOTAL_ROWS[level][h]
            st_ref[0, at : at + 1, :] = wide[2 + h]
        mx_ref[0, level - 1] = mixed.astype(BF16)
        coarse.append((wide, mixed))
        yield

    peaks, denoms, factors = [], [], []
    for h, (top0, total0) in enumerate(((top_a, total_a), (top_b, total_b))):
        peak = top0
        for wide, _ in coarse:
            peak = jnp.maximum(peak, wide[h])
        f = [jnp.exp(top0 - peak)] + [jnp.exp(wide[h] - peak) for wide, _ in coarse]
        denom = f[0] * total0
        for i, (wide, _) in enumerate(coarse):
            denom = denom + f[i + 1] * wide[2 + h]
        peaks.append(peak)
        denoms.append(denom)
        factors.append(f)
    numer = by_head(factors[0][0], factors[1][0], mixed0)
    for i, (_, mixed) in enumerate(coarse):
        numer = numer + by_head(factors[0][i + 1], factors[1][i + 1], mixed)
    st_ref[0, 5:6, :] = peaks[0]
    st_ref[0, 6:7, :] = peaks[1]
    st_ref[0, 7:8, :] = denoms[0]
    st_ref[0, 8:9, :] = denoms[1]
    nt_ref[0] = numer


def far_kernel(
    off_ref, edge_ref, far_ref, flag_ref, qc_ref, g_ref, st_ref, nt_ref, mx_ref,
    opposite_ref, next_ref, prev_ref, f1_ref, f2_ref, f3_ref,
    att_ref, st2_ref, dq_ref, dring_ref, d1_ref, d2_ref, d3_ref, e3, e4, e5,
):
    step = pl.program_id(0)

    @pl.when(step == 0)
    def _():
        e3[...] = spreader(3)
        e4[...] = spreader(4)
        e5[...] = spreader(5)

    def one(s):
        windows = [lane_view(r, s) for r in (f1_ref, f2_ref, f3_ref, opposite_ref, next_ref, prev_ref)]
        grads = [lane_view(r, s) for r in (dring_ref, d1_ref, d2_ref, d3_ref)]
        return far_pair(
            step * SUB + s, off_ref, edge_ref, far_ref, flag_ref, lane_view(qc_ref, s), lane_view(g_ref, s),
            *[r.at[s : s + 1] for r in (st_ref, nt_ref, mx_ref)], *windows,
            lane_view(att_ref, s), *[r.at[s : s + 1] for r in (st2_ref, dq_ref)],
            *grads, (e3, e4, e5),
        )

    interleaved(one(s) for s in range(SUB))


def far_pair(
    pair, off_ref, edge_ref, far_ref, flag_ref, qc_ref, g_ref, st_ref, nt_ref, mx_ref,
    f1_ref, f2_ref, f3_ref, opposite_ref, next_ref, prev_ref,
    att_ref, st2_ref, dq_ref, dring_ref, d1_ref, d2_ref, d3_ref, spreads,
):
    first = flag_ref[0] > 0
    lower, upper = range(RING // 2), range(RING // 2, RING)
    coarse_q = {3: qc_ref[384:448], 4: qc_ref[448:480], 5: qc_ref[480:496]}
    gt = g_ref[0].T.astype(F32)
    windows = {3: [], 4: [], 5: []}
    for i in range(2):
        after, before = next_ref[i], prev_ref[i]
        windows[3].append(jnp.concatenate([f1_ref[i], f2_ref[i], f3_ref[i]], axis=0))
        near = jnp.where(first, before[0:128], after[0:128])
        windows[4].append(jnp.concatenate([opposite_ref[i], near], axis=0))
        windows[5].append(jnp.concatenate([
            jnp.where(first, before[128:192], before[0:64]),
            jnp.where(first, after[64:128], after[128:192]),
            jnp.where(first, after[0:64], before[64:128]),
        ], axis=0))
    levels = []
    for level, spread in zip((3, 4, 5), spreads):
        span = 512 >> level
        queries = two_heads(coarse_q[level])
        keys, values = windows[level]
        scores = dot_nt(keys, queries)
        parts = keys.shape[0] // HALF
        biases = [
            (i * HALF, (i + 1) * HALF, edge_ref[2 + i] if level == 3 else far_ref[level - 4, i]) for i in range(parts)
        ]
        top, weights, total = softmax_of(with_bias(scores, biases))
        mixed = own_head(dot_nn(values.T, weights.astype(BF16)), span).astype(BF16)
        low = off_ref[level - 1, 2 * pair] + level * LN2
        high = off_ref[level - 1, 2 * pair + 1] + level * LN2
        top = top + offset_row(low, high, span, top.shape)
        wide = spread_stats([top, total], span, spread[...])
        levels.append((level, span, queries, weights, wide, dot_nn(mixed, spread[...]), spread))
        yield

    logs, inners, numers = [], [], []
    for h in range(2):
        peak0, denom0 = st_ref[0, 5 + h : 6 + h, :], st_ref[0, 7 + h : 8 + h, :]
        peak = peak0
        for item in levels:
            peak = jnp.maximum(peak, item[4][h])
        keep = jnp.exp(peak0 - peak)
        denom = keep * denom0
        numer = keep * nt_ref[0, h * HALF : (h + 1) * HALF, :]
        for item in levels:
            f = jnp.exp(item[4][h] - peak)
            denom = denom + f * item[4][2 + h]
            numer = numer + f * item[5][h * HALF : (h + 1) * HALF]
        out = (numer / denom).astype(BF16)
        numers.append(out)
        logs.append(peak + jnp.log(denom))
        inners.append(
            jnp.sum(gt[h * HALF : (h + 1) * HALF] * out.astype(F32), axis=0, keepdims=True)
        )
    att_ref[0] = jnp.concatenate(numers, axis=0).T
    st2_ref[0] = stacked([logs[0], logs[1], inners[0], inners[1]], 8)
    cells = jnp.zeros((16, PAIR), F32)
    slot = (iota(cells.shape, 0) == flag_ref[1])
    lane = iota(cells.shape, 1)
    for level in range(1, LEVELS):
        for h in range(2):
            part = slice(h * HALF, (h + 1) * HALF)
            if level < 3:
                top = st_ref[0, 7 + 2 * level + h : 8 + 2 * level + h, :]
                at = TOTAL_ROWS[level][h]
                total, mixed = st_ref[0, at : at + 1, :], mx_ref[0, level - 1, part, :].astype(F32)
            else:
                item = levels[level - 3]
                top, total, mixed = item[4][h], item[4][2 + h], item[5][part]
            terms = jnp.sum(gt[part] * mixed, axis=0, keepdims=True) - inners[h] * total
            terms = jnp.sum(jnp.exp(top - logs[h]) * terms, axis=1, keepdims=True)
            for n, piece in enumerate(split3(terms)):
                cells = jnp.where(slot & (lane == 16 * n + 2 * (level - 1) + h), piece, cells)
    cells = cells.astype(BF16)
    for z in range(RING):
        at = SHARE * z + 80
        dring_ref[0, at : at + 16, :] = cells
        dring_ref[1, at : at + 16, :] = jnp.zeros_like(cells)
    yield

    dqt = jnp.zeros((PAIR, 512), F32)
    grads = {}
    for level, span, queries, weights, wide, _, spread in levels:
        dq, dk, dv = level_back(
            weights, *windows[level], queries, gt, wide[:2], logs, inners, span, spread
        )
        grads[level] = (dk.astype(BF16), dv.astype(BF16))
        last = (dk[128:192], dv[128:192])
        dqt = dqt + dq * (0.125 / 2**level)
        yield
    for i in range(2):
        for n, ref in enumerate((d1_ref, d2_ref, d3_ref)):
            ref[i] = grads[3][i][n * HALF : (n + 1) * HALF]
        four, five = grads[4][i], grads[5][i]
        blank = jnp.zeros((128, PAIR), BF16)
        far = uncoarsen(last[i]).astype(BF16)
        for part, on_low in ((lower, True), (upper, False)):
            here = jnp.logical_not(first) if on_low else first
            own = jnp.where(here, four[0:128], blank)
            foreign = jnp.where(here, four[128:256], far)
            for n, z in enumerate(part):
                at = SHARE * z
                dring_ref[i, at : at + 32, :] = own[32 * n : 32 * n + 32]
                dring_ref[i, at + 32 : at + 64, :] = foreign[32 * n : 32 * n + 32]
                dring_ref[i, at + 64 : at + 80, :] = five[16 * z : 16 * z + 16]
    dq_ref[0] = dqt


def grad_rows(gt, tops, logs, inners, span, spread):
    f = [jnp.exp(tops[h] - logs[h]) for h in range(2)]
    g = dot_nt(spread[...], by_head(f[0], f[1], gt).astype(BF16))
    mine = (iota(g.shape, 1) < HALF) == (iota(g.shape, 0) // span % 2 == 0)
    g = jnp.where(mine, g, 0.0).astype(BF16)
    flat = [part for h in range(2) for part in split3(f[h] * inners[h])]
    wide = dot_nt(stacked(flat, 16).astype(BF16), spread[...])
    low = wide[0:1] + wide[1:2] + wide[2:3]
    high = wide[3:4] + wide[4:5] + wide[5:6]
    corr = jnp.where(iota(low.shape, 1) // span % 2 == 0, low, high)
    return g, corr


def window_back(weights, values, queries, g, corr):
    dots = dot_nt(values, g)
    grad = weights * (dots - corr)
    short = grad.astype(BF16)
    return short, dot_nn(short, queries), dot_nn(weights.astype(BF16), g)


def level_back(weights, keys, values, queries, gt, tops, logs, inners, span, spread):
    g, corr = grad_rows(gt, tops, logs, inners, span, spread)
    short, dk, dv = window_back(weights, values, queries, g, corr)
    dq = own_head(dot_nn(keys.T, short), span).astype(BF16)
    return dot_nn(dq, spread[...]), dk, dv


def near_backward_kernel(
    edge_ref, q_ref, qc_ref, k_ref, v_ref, kvc_ref, g_ref, nl_ref, nr_ref, halo_ref,
    st_ref, st2_ref, dqf_ref,
    dq_ref, own_ref, gl_ref, gr_ref,
    e1, e2, *scratch,
):
    step = pl.program_id(0)

    @pl.when(step == 0)
    def _():
        e1[...] = spreader(1)
        e2[...] = spreader(2)

    def one(s):
        wide = [lane_view(r, s) for r in (q_ref, qc_ref, k_ref, v_ref, kvc_ref, g_ref, nl_ref, nr_ref, halo_ref)]
        per = [r.at[s : s + 1] for r in (st_ref, st2_ref, dqf_ref, dq_ref)]
        out = [lane_view(r, s) for r in (own_ref, gl_ref, gr_ref)]
        return near_backward_pair(
            edge_ref, *wide, *per, *out, e1, e2, *[r.at[s] for r in scratch]
        )

    interleaved(one(s) for s in range(SUB))


def near_backward_pair(
    edge_ref, q_ref, qc_ref, k_ref, v_ref, kvc_ref, g_ref, nl_ref, nr_ref, halo_ref, st_ref, st2_ref, dqf_ref,
    dq_ref, own_ref, gl_ref, gr_ref,
    e1, e2, k0s, k1s, k2s, v0s, v1s, v2s, kt0, kt1, kt2,
    dk0, dk1, dk2, dv0, dv1, dv2,
):
    left_bias, right_bias = edge_ref[0], edge_ref[1]
    q0 = q_ref[0] * jnp.asarray(0.125, BF16)
    q1, q2 = qc_ref[0:256], qc_ref[256:384]
    keys = near_keys(k_ref[0], kvc_ref[0], nl_ref[0], nr_ref[0], halo_ref[0])
    for dst, tdst, x in zip((k0s, k1s, k2s), (kt0, kt1, kt2), keys):
        dst[...] = x
        tdst[...] = x.T
    for dst, x in zip((v0s, v1s, v2s), near_keys(v_ref[0], kvc_ref[1], nl_ref[1], nr_ref[1], halo_ref[1])):
        dst[...] = x
    for ref in (dk0, dk1, dk2, dv0, dv1, dv2):
        ref[...] = jnp.zeros(ref.shape, F32)

    yield
    gt = g_ref[0].T.astype(F32)
    logs = [st2_ref[0, 0:1, :], st2_ref[0, 1:2, :]]
    inners = [st2_ref[0, 2:3, :], st2_ref[0, 3:4, :]]
    dqt = dqf_ref[0]

    for level, ks, vs, kt, dk, dv, queries, spread in (
        (1, k1s, v1s, kt1, dk1, dv1, q1, e1),
        (2, k2s, v2s, kt2, dk2, dv2, q2, e2),
    ):
        halves = 8 >> level
        tops = [st_ref[0, 7 + 2 * level + h : 8 + 2 * level + h, :] for h in range(2)]
        g, corr = grad_rows(gt, tops, logs, inners, HALF, spread)
        dqs = []
        for j in range(halves):
            spans = window_spans(j)
            at = slice(j * 128, (j + 1) * 128)
            queries_j = two_heads(queries[j * HALF : (j + 1) * HALF])
            scores = dot_nt(rows_of(ks, spans), queries_j)
            scores = with_bias(scores, window_biases(j, halves, left_bias, right_bias))
            weights = jnp.exp(scores - st_ref[0, 1 + level : 2 + level, at])
            short, dk_j, dv_j = window_back(weights, rows_of(vs, spans), queries_j, g[at], corr[:, at])
            base = 0
            for lo, hi in spans:
                dk[lo:hi, :] += dk_j[base : base + hi - lo]
                dv[lo:hi, :] += dv_j[base : base + hi - lo]
                base += hi - lo
            kt_j = jnp.concatenate([kt[:, lo:hi] for lo, hi in spans], axis=1)
            dqs.append(own_head(dot_nn(kt_j, short), HALF).astype(BF16))
            yield
        dqt = dqt + dot_nn(jnp.concatenate(dqs, axis=1), spread[...]) * (0.125 / 2**level)

    g0, corr0 = zero_rows(gt, st_ref, logs, inners)
    dq0 = {}
    for b in (0, 3):
        span = slice(b * 128, b * 128 + 384)
        dq0[b], dk_b, dv_b = block_back(
            b, k0s[span, :], v0s[span, :], kt0[:, span], q0, g0, corr0, st_ref, left_bias, right_bias
        )
        dk0[span, :] += dk_b
        dv0[span, :] += dv_b
        yield
    blank = jnp.zeros((PAIR, 256), F32)
    dq_ref[0] = dqt + jnp.concatenate([dq0[0], blank, dq0[3]], axis=1)

    for i, (zero, one, two) in enumerate(((dk0, dk1, dk2), (dv0, dv1, dv2))):
        left1 = one[0:128, :] + uncoarsen(two[64:128, :])
        left0 = zero[0:128, :] + uncoarsen(left1[64:128])
        gl_ref[i, 0:128, :] = left0.astype(BF16)
        gl_ref[i, 128:192, :] = left1[0:64].astype(BF16)
        gl_ref[i, 192:256, :] = two[0:64, :].astype(BF16)
        right1 = one[384:512, :] + uncoarsen(two[256:320, :])
        right0 = zero[640:768, :] + uncoarsen(right1[0:64])
        gr_ref[i, 0:128, :] = right0.astype(BF16)
        gr_ref[i, 128:192, :] = right1[64:128].astype(BF16)
        gr_ref[i, 192:256, :] = two[320:384, :].astype(BF16)
        mine1 = one[128:384, :] + uncoarsen(two[128:256, :])
        own_ref[i] = zero[128:640, :] + uncoarsen(mine1)


def zero_rows(gt, st_ref, logs, inners):
    f0 = [jnp.exp(st_ref[0, h : h + 1, :] - logs[h]) for h in range(2)]
    g0 = by_head(f0[0], f0[1], gt).astype(BF16).T
    return g0, [f0[h] * inners[h] for h in range(2)]


def block_back(b, keys, values, keys_t, q0, g0, corr0, st_ref, left_bias, right_bias):
    at = slice(b * 128, (b + 1) * 128)
    queries = two_heads(q0[at])
    scores = with_bias(dot_nt(keys, queries), block_biases(b, left_bias, right_bias))
    top = jnp.concatenate([st_ref[0, 0:1, at], st_ref[0, 1:2, at]], axis=1)
    corr = jnp.concatenate([corr0[0][:, at], corr0[1][:, at]], axis=1)
    weights = jnp.exp(scores - top)
    short, dk, dv = window_back(weights, values, queries, two_heads(g0[at]), corr)
    dq = dot_nn(keys_t, short)
    return jnp.concatenate([dq[:HALF, :128], dq[HALF:, 128:]], axis=0) * 0.125, dk, dv


def own_backward_kernel(
    q_ref, k_ref, v_ref, g_ref, st_ref, st2_ref, dqt_ref, own_in_ref, f1_ref, f2_ref, f3_ref,
    dq_ref, own_ref
):
    def one(s):
        wide = [lane_view(r, s) for r in (q_ref, k_ref, v_ref, g_ref)]
        per = [r.at[s : s + 1] for r in (st_ref, st2_ref, dqt_ref)]
        pieces = [lane_view(r, s) for r in (f1_ref, f2_ref, f3_ref)]
        return own_backward_pair(*wide, *per, pieces, *[lane_view(r, s) for r in (own_in_ref, dq_ref, own_ref)])

    interleaved(one(s) for s in range(SUB))


def own_backward_pair(
    q_ref, k_ref, v_ref, g_ref, st_ref, st2_ref, dqt_ref, pieces, own_in_ref, dq_ref, own_ref
):
    q0 = q_ref[0] * jnp.asarray(0.125, BF16)
    keys, values = k_ref[0], v_ref[0]
    keys_t = keys.T
    gt = g_ref[0].T.astype(F32)
    logs = [st2_ref[0, 0:1, :], st2_ref[0, 1:2, :]]
    inners = [st2_ref[0, 2:3, :], st2_ref[0, 3:4, :]]
    g0, corr0 = zero_rows(gt, st_ref, logs, inners)
    yield
    out = {}
    for b in (1, 2):
        span = slice((b - 1) * 128, (b + 2) * 128)
        out[b] = block_back(b, keys[span], values[span], keys_t[:, span], q0, g0, corr0, st_ref, None, None)
        yield
    dqt = dqt_ref[0]
    dqt = jnp.concatenate([dqt[:, :128], dqt[:, 128:256] + out[1][0], dqt[:, 256:384] + out[2][0], dqt[:, 384:]], axis=1)
    dq_ref[0] = dqt.astype(BF16).T
    for i in range(2):
        one, two = out[1][1 + i], out[2][1 + i]
        three = sum(ref[i].astype(F32) for ref in pieces) * 0.125
        far = dot_nn(doubling(HALF, 8), three.astype(BF16))
        own_ref[i, 0:128, :] = own_in_ref[i, 0:128, :] + far[0:128] + one[0:128]
        own_ref[i, 128:384, :] = own_in_ref[i, 128:384, :] + far[128:384] + one[128:384] + two[0:256]
        own_ref[i, 384:512, :] = own_in_ref[i, 384:512, :] + far[384:512] + two[256:384]


def finish_kernel(own_ref, left_ref, right_ref, sum_ref, next_ref, prev_ref, dk_ref, dv_ref):
    up2, up4, up16 = doubling(HALF, 2), doubling(HALF, 4), doubling(HALF // 2, 16)
    for i, out in enumerate((dk_ref, dv_ref)):
        four = sum_ref[i, 0:32, :].astype(F32) + next_ref[i].astype(F32) + prev_ref[i].astype(F32)
        far = dot_nn(up16, (four * 0.0625).astype(BF16))
        left1 = dot_nn(up2, left_ref[i, 128:192, :]) * 0.5
        left2 = dot_nn(up4, left_ref[i, 192:256, :]) * 0.25
        right1 = dot_nn(up2, right_ref[i, 128:192, :]) * 0.5
        right2 = dot_nn(up4, right_ref[i, 192:256, :]) * 0.25
        parts = [
            left_ref[i, 0:128, :].astype(F32) + right2[0:128],
            left1 + right2[128:256],
            left2[0:128] + right1,
            left2[128:256] + right_ref[i, 0:128, :].astype(F32),
        ]
        out[0] = (own_ref[i] + far + jnp.concatenate(parts, axis=0)).astype(BF16)


def lanes(rows, *lead, pairs=SUB):
    shape = tuple(lead) + (rows, PAIR * pairs)
    zeros = (0,) * (len(shape) - 1)
    return pl.BlockSpec(shape, lambda p: zeros + (p,))


def per_pair(*shape):
    zeros = (0,) * len(shape)
    return pl.BlockSpec((SUB,) + shape, lambda p: (p,) + zeros)


def interleaved(parts):
    live = list(parts)
    while live:
        for part in list(live):
            try:
                next(part)
            except StopIteration:
                live.remove(part)


def lane_view(ref, s):
    return ref.at[..., s * PAIR : (s + 1) * PAIR]


def scalars():
    return pl.BlockSpec(memory_space=pltpu.SMEM)


def shape_of(*shape, dtype=BF16):
    return jax.ShapeDtypeStruct(shape, dtype)


def call(kernel, steps, in_specs, out_specs, out_shape, scratch, cost, name, mib=48):
    return pl.pallas_call(
        kernel,
        grid=(steps,),
        in_specs=in_specs,
        out_specs=out_specs,
        out_shape=out_shape,
        scratch_shapes=scratch,
        compiler_params=pltpu.CompilerParams(
            vmem_limit_bytes=mib * MIB, dimension_semantics=("arbitrary",)
        ),
        cost_estimate=pl.CostEstimate(flops=cost, bytes_accessed=cost // 300, transcendentals=0),
        name=name,
    )


def permute(block, route):
    return lax.ppermute(block, "ctx", route)


def shifted(block, distance):
    n = lax.axis_size("ctx")
    return permute(block, [(i, i + distance) for i in range(n) if 0 <= i + distance < n])


def crossed(block, span):
    n = lax.axis_size("ctx")
    route = []
    for i in range(n):
        to = i + 3 * span if i // span % 2 == 0 else i - 3 * span
        if 0 <= to < n:
            route.append((i, to))
    return permute(block, route)


def ring_groups():
    n = lax.axis_size("ctx")
    return [list(range(i, i + RING)) for i in range(0, n, RING)]


def total_over(x, bits):
    count = lax.axis_size("dp") * lax.axis_size("ctx")

    def from_device(x, mask):
        return lax.ppermute(x, ("dp", "ctx"), [(i, i ^ mask) for i in range(count)])

    for at in range(0, len(bits), 2):
        a = 1 << bits[at]
        first = x + from_device(x, a)
        if at + 1 < len(bits):
            b = 1 << bits[at + 1]
            first = first + (from_device(x, b) + from_device(x, a | b))
        x = first
    return x


def body(queries, key_rows, values, grad_out, level_bias):
    width = queries.shape[2]
    pairs = width // PAIR
    n = lax.axis_size("ctx")
    me = lax.axis_index("ctx")

    def bias_of(flags):
        return jnp.where(jnp.stack(flags), 0.0, NEGATIVE).astype(F32)

    half = me % RING // 2
    is_first = half < 2
    has_prev, has_next = me >= RING, me < n - RING
    near_ring, far_ring = jnp.where(is_first, has_prev, has_next), jnp.where(is_first, has_next, has_prev)
    edge_bias = bias_of([
        me > 0, me < n - 1, me >= 2, me + 2 < n, jnp.where(me % 2 == 0, me + 3 < n, me >= 3)
    ])
    far_bias = jnp.stack([
        bias_of([half != 1, half != 2, near_ring & (half != 3), near_ring & (half != 0)]),
        bias_of([has_prev, has_next, far_ring, far_ring]),
    ])
    flag = jnp.stack([is_first.astype(jnp.int32), (me % RING).astype(jnp.int32)])

    send_right, send_left, l3, l4, kv_coarse = call(
        prep_kernel, pairs // 4,
        [lanes(512, 1, pairs=4)] * 2,
        [lanes(r, 2, pairs=4) for r in (256, 256, 64, 32, 384)],
        [shape_of(2, r, width) for r in (256, 256, 64, 32, 384)],
        [], 400_000_000, "prep", 60,
    )(key_rows, values)

    ring = lax.all_gather(l4, "ctx", axis=1, tiled=True, axis_index_groups=ring_groups())
    near_left = shifted(send_right, 1)
    near_right = shifted(send_left, -1)
    inner_stats, inner_mixed, third_out = call(
        inner_forward_kernel, pairs // SUB,
        [lanes(512, 1)] * 3 + [lanes(64, 2)],
        [per_pair(8, 512), per_pair(PAIR, 256), lanes(64, 2)],
        [shape_of(pairs, 8, 512, dtype=F32), shape_of(pairs, PAIR, 256, dtype=F32), shape_of(2, 64, width)],
        [], 10_000_000_000, "inner_forward",
    )(queries, key_rows, values, l3)
    third = [shifted(third_out, 2), shifted(third_out, -2), crossed(third_out, 1)]

    to_next, to_prev, opposite = call(
        pack_kernel, pairs // 4,
        [scalars(), lanes(256, 2, pairs=4)]
        + [pl.BlockSpec(memory_space=pl.ANY)] * 3,
        [lanes(r, 2, pairs=4) for r in (192, 192, 128)],
        [shape_of(2, r, width) for r in (192, 192, 128)],
        [], 400_000_000, "pack",
    )(flag, ring, inner_stats, near_left, near_right)
    from_prev = shifted(to_next, RING)
    from_next = shifted(to_prev, -RING)

    q_coarse = call(
        query_kernel, pairs // 4,
        [lanes(512, 1, pairs=4)], [lanes(496, pairs=4)], [shape_of(496, width)],
        [], 400_000_000, "queries",
    )(queries)[0]

    spreads = [pltpu.VMEM((r, 512), BF16) for r in (512, 256)]
    key_sets = [pltpu.VMEM((SUB, r, PAIR), BF16) for r in (768, 512, 384)]
    turned = [pltpu.VMEM((SUB, PAIR, r), BF16) for r in (768, 512, 384)]
    sums = [pltpu.VMEM((SUB, r, PAIR), F32) for r in (768, 512, 384)]

    stats, numer, mixed_near, halo = call(
        near_forward_kernel, pairs // SUB,
        [scalars(), scalars(), lanes(512, 1), lanes(496), lanes(512, 1), lanes(512, 1), lanes(384, 2)]
        + [lanes(256, 2)] * 2 + [per_pair(8, 512), per_pair(PAIR, 256)],
        [per_pair(16, 512), per_pair(PAIR, 512), per_pair(2, PAIR, 512), lanes(256, 2)],
        [
            shape_of(pairs, 16, 512, dtype=F32), shape_of(pairs, PAIR, 512, dtype=F32),
            shape_of(pairs, 2, PAIR, 512), shape_of(2, 256, width),
        ],
        spreads + key_sets + turned, 30_000_000_000, "near_forward",
    )(level_bias, edge_bias, queries, q_coarse, key_rows, values, kv_coarse, near_left, near_right, inner_stats, inner_mixed)

    attended, stats2, dq_far, d_ring, d1, d2, d3 = call(
        far_kernel, pairs // SUB,
        [scalars()] * 4 + [lanes(496), lanes(512, 1), per_pair(16, 512), per_pair(PAIR, 512), per_pair(2, PAIR, 512)]
        + [lanes(r, 2) for r in (128, 192, 192, 64, 64, 64)],
        [lanes(512, 1), per_pair(8, 512), per_pair(PAIR, 512), lanes(RING * SHARE, 2)]
        + [lanes(64, 2)] * 3,
        [
            shape_of(1, 512, width),
            shape_of(pairs, 8, 512, dtype=F32),
            shape_of(pairs, PAIR, 512, dtype=F32),
            shape_of(2, RING * SHARE, width),
        ] + [shape_of(2, 64, width)] * 3,
        [pltpu.VMEM((r, 512), BF16) for r in (128, 64, 32)], 20_000_000_000, "far",
    )(
        level_bias, edge_bias, far_bias, flag, q_coarse, grad_out, stats, numer, mixed_near,
        opposite, from_next, from_prev, *third,
    )
    back = [shifted(d1, -2), shifted(d2, 2), crossed(d3, 1)]

    d_share = lax.psum_scatter(d_ring, "ctx", scatter_dimension=1, tiled=True, axis_index_groups=ring_groups())

    grad_qt, own_part, to_left, to_right = call(
        near_backward_kernel, pairs // SUB,
        [scalars(), lanes(512, 1), lanes(496), lanes(512, 1), lanes(512, 1), lanes(384, 2), lanes(512, 1)]
        + [lanes(256, 2)] * 3
        + [per_pair(16, 512), per_pair(8, 512), per_pair(PAIR, 512)],
        [per_pair(PAIR, 512), lanes(512, 2)] + [lanes(256, 2)] * 2,
        [shape_of(pairs, PAIR, 512, dtype=F32), shape_of(2, 512, width, dtype=F32)]
        + [shape_of(2, 256, width)] * 2,
        spreads + key_sets + key_sets + turned + sums + sums, 30_000_000_000, "near_backward",
    )(
        edge_bias, queries, q_coarse, key_rows, values, kv_coarse, grad_out,
        near_left, near_right, halo, stats, stats2, dq_far,
    )

    back_right, back_left = shifted(to_right, 1), shifted(to_left, -1)

    grad_q, own = call(
        own_backward_kernel, pairs // SUB,
        [lanes(512, 1)] * 4 + [per_pair(16, 512), per_pair(8, 512), per_pair(PAIR, 512), lanes(512, 2)]
        + [lanes(64, 2)] * 3,
        [lanes(512, 1), lanes(512, 2)],
        [shape_of(1, 512, width), shape_of(2, 512, width, dtype=F32)],
        [], 15_000_000_000, "own_backward",
    )(queries, key_rows, values, grad_out, stats, stats2, grad_qt, own_part, *back)

    share_next, share_prev, cells = call(
        unshare_kernel, pairs // 4,
        [scalars(), lanes(SHARE, 2, pairs=4), pl.BlockSpec(memory_space=pl.ANY)],
        [lanes(32, 2, pairs=4)] * 2 + [lanes(16, pairs=4)],
        [shape_of(2, 32, width)] * 2 + [shape_of(16, width, dtype=F32)],
        [], 400_000_000, "unshare",
    )(flag, d_share, own)
    cells = cells[:RING].reshape(RING, pairs, PAIR)[:, :, :48]
    bias = jnp.sum(cells.reshape(RING, pairs, 3, 16), axis=(0, 2))[:, : 2 * (LEVELS - 1)]
    bias = jnp.transpose(bias.reshape(pairs, LEVELS - 1, 2), (1, 0, 2)).reshape(LEVELS - 1, 2 * pairs)
    count = n * lax.axis_size("dp")
    back_next, back_prev = shifted(share_prev, -RING), shifted(share_next, RING)
    bias = total_over(bias, range(3, 5))
    bias, back_next, back_prev = lax.optimization_barrier((bias, back_next, back_prev))
    bias = total_over(bias, range(5, count.bit_length() - 1))
    grad_bias = bias * (1.0 / math.sqrt(512 * count))

    grad_k, grad_v = call(
        finish_kernel, pairs // 4,
        [lanes(r, 2, pairs=4) for r in (512, 256, 256, SHARE, 32, 32)],
        [lanes(512, 1, pairs=4)] * 2,
        [shape_of(1, 512, width)] * 2,
        [], 400_000_000, "finish",
    )(own, back_right, back_left, d_share, back_next, back_prev)
    return attended, grad_q, grad_k, grad_v, grad_bias


def solution(mesh):
    rows = P("dp", "ctx", None)
    return jax.shard_map(
        body,
        mesh=mesh,
        in_specs=(rows, rows, rows, rows, P()),
        out_specs=(rows, rows, rows, rows, P()),
        check_vma=False,
    )
```
